256 devices in a mesh: row: 16 (over x, y), col: 16 (over z, core).
Axes of the slice: x: 4, y: 4, z: 8, core: 2. Of those that a mesh axis runs over, the one named last changes fastest.
Arguments:
- features: bfloat16 [131072, 256], P(('col', 'row')), may hold values from -6 to 6
- weight: bfloat16 [256, 256], replicated, may hold values from -0.375 to 0.375
- out_bias: float32 [256], replicated, may hold values from -3 to 3
- upstream: bfloat16 [131072, 256], P(('row', 'col')), may hold values from -6 to 6
- adj_tiles: bfloat16 [16, 16, 96, 128, 128], P('row', 'col'), may hold values from -0.5 to 0.5
- tile_rows: int32 [16, 16, 96], P('row', 'col'), may hold values from 0 to 63, as said below
- tile_cols: int32 [16, 16, 96], P('row', 'col'), may hold values from 0 to 63, as said below
- tile_count: int32 [16, 16], P('row', 'col'), may hold values from 12 to 96, as said below
Outputs:
- out_features: bfloat16 [131072, 256], P(('row', 'col'))
- grad_features: bfloat16 [131072, 256], P(('col', 'row'))
- grad_weight: float32 [256, 256], replicated
- grad_bias: float32 [256], replicated
The draws below stay inside these ranges and needn't reach their ends.
Inputs may be any that keep to these rules, and one draw needn't show every extreme that they name: Within one device the pairs (tile_rows, tile_cols) of all 96 slots are distinct and ordered by row block, then column block. `tile_cols`: see tile_rows. `tile_count`: some device uses all 96 slots.
All inputs are finite; a program needn't handle non-finite values.
Results may differ from the reference program's by a relative error of at most 0.022.
Values may be sent and summed in bfloat16 or wider, within the bound.
No kernel may reach another device: no remote copies, remote signals or barrier semaphores. Data moves between devices by JAX's collectives and lax.ppermute only.
A program may use at most 128 MiB of HBM per device.

```python
import jax
import jax.numpy as jnp
from jax import lax

F = 256
TILE = 128
NB_DEV = 4
SLOTS = 96
ROW_BLOCKS = 64
COL_BLOCKS = 64
NODES = 131072
N_ROW = 16
N_COL = 16


def slot_positions(key):
    device_keys = jax.random.split(key, N_ROW * N_COL)

    def one_device(device_key):
        order = jax.random.permutation(device_key, ROW_BLOCKS * COL_BLOCKS)[:SLOTS]
        return jnp.sort(order).astype(jnp.int32)
    return jax.vmap(one_device)(device_keys).reshape(N_ROW, N_COL, SLOTS)


def draw_tile_rows(key, part):
    positions = slot_positions(key)
    return (positions // COL_BLOCKS).astype(jnp.int32)


def draw_tile_cols(key, part):
    positions = slot_positions(key)
    return (positions % COL_BLOCKS).astype(jnp.int32)


def draw_tile_count(key, part):
    key = jax.random.fold_in(key, 3)
    first_key, second_key = jax.random.split(key)
    level = jax.random.randint(first_key, (N_ROW * N_COL,), 0, 65)
    floor_count = max(SLOTS // 8, 1)
    counts = floor_count + (SLOTS - floor_count) * level * level * level // 262144
    chosen = jax.random.randint(second_key, (), 0, N_ROW * N_COL)
    counts = jnp.where(jnp.arange(N_ROW * N_COL) == chosen, SLOTS, counts)
    return counts.reshape(N_ROW, N_COL).astype(jnp.int32)


def block_scale(own_key, shape, shards, smallest, largest):
    level, own = 1.0, jax.random.fold_in(own_key, 6)
    for dim, parts in shards:
        draws = jnp.exp(jax.random.uniform(jax.random.fold_in(own, dim), (parts,), jnp.float32, smallest / len(shards), largest / len(shards)))
        level = level * jnp.repeat(draws, shape[dim] // parts).reshape([-1 if axis == dim else 1 for axis in range(len(shape))])
    return level


def noise(rng, shape, width, reach, pieces=(), kind=jnp.bfloat16):
    array = width * jax.random.normal(rng, shape, jnp.float32)
    if pieces:
        array = array * block_scale(rng, shape, pieces, -0.22, 0.18)
    return jnp.clip(array, -reach, reach).astype(kind)


def setup_inputs(seed: int = 0) -> dict:
    seeds = jax.random.split(jax.random.key(seed), 9)
    return {
        "features": noise(seeds[0], (NODES, F), 1.0, 6.0, ((0, 256),)),
        "weight": noise(seeds[1], (F, F), F ** -0.5, 0.375),
        "out_bias": noise(seeds[2], (F,), 0.5, 3.0, (), jnp.float32),
        "upstream": noise(seeds[3], (NODES, F), 1.0, 6.0, ((0, 256),)),
        "adj_tiles": noise(seeds[4], (N_ROW, N_COL, SLOTS, TILE, TILE), ((NB_DEV * 10) ** 0.5 * (3 * SLOTS * TILE) ** -0.5), 0.5, ((0, 16), (1, 16))),
        "tile_rows": draw_tile_rows(jax.random.fold_in(seeds[8], 71), 0),
        "tile_cols": draw_tile_cols(jax.random.fold_in(seeds[8], 71), 0),
        "tile_count": draw_tile_count(jax.random.fold_in(seeds[8], 71), 0),
    }


def silu_slope(preact):
    squashed = jax.nn.sigmoid(preact)
    return squashed * (1.0 + preact * (1.0 - squashed))


def tile_sums(adj_block, source_index, target_index, filled, blocks, targets, pattern):
    picked = jnp.take(blocks, source_index, axis=0)
    products = jnp.einsum(pattern, adj_block.astype(jnp.float32), picked.astype(jnp.float32))
    active = jnp.arange(adj_block.shape[0], dtype=jnp.int32) < filled
    target = jnp.where(active, target_index, targets).astype(jnp.int32)
    summed = jax.ops.segment_sum(products, target, num_segments=targets + 1)
    return summed[:targets].reshape(targets * adj_block.shape[1], products.shape[2])


def reference(features, weight, out_bias, upstream, adj_tiles, tile_rows, tile_cols, tile_count):
    hidden = jnp.dot(features, weight, preferred_element_type=jnp.float32).astype(jnp.bfloat16)
    col_feats = hidden.reshape(N_COL, COL_BLOCKS, TILE, F)

    def forward_row(rindex):
        def add_one(running, cindex):
            piece_sum = tile_sums(adj_tiles[rindex, cindex], tile_cols[rindex, cindex], tile_rows[rindex, cindex],
                                  tile_count[rindex, cindex], col_feats[cindex], ROW_BLOCKS, "sik,skf->sif")
            piece_sum = lax.optimization_barrier(piece_sum.astype(jnp.bfloat16)).astype(jnp.float32)
            return running + piece_sum, None
        running, unused = lax.scan(add_one, jnp.zeros((ROW_BLOCKS * TILE, F), jnp.float32), jnp.arange(N_COL, dtype=jnp.int32))
        return running

    aggregated = lax.map(forward_row, jnp.arange(N_ROW, dtype=jnp.int32)).reshape(NODES, F)
    preact = aggregated + out_bias.astype(jnp.float32)[None, :]
    out_features = jax.nn.silu(preact).astype(jnp.bfloat16)
    grad_pre = (upstream.astype(jnp.float32) * silu_slope(preact)).astype(jnp.bfloat16)
    row_grads = grad_pre.reshape(N_ROW, ROW_BLOCKS, TILE, F)

    def backward_col(cindex):
        def add_one(running, rindex):
            piece_sum = tile_sums(adj_tiles[rindex, cindex], tile_rows[rindex, cindex], tile_cols[rindex, cindex],
                                  tile_count[rindex, cindex], row_grads[rindex], COL_BLOCKS, "ski,skf->sif")
            piece_sum = lax.optimization_barrier(piece_sum.astype(jnp.bfloat16)).astype(jnp.float32)
            return running + piece_sum, None
        running, unused = lax.scan(add_one, jnp.zeros((COL_BLOCKS * TILE, F), jnp.float32), jnp.arange(N_ROW, dtype=jnp.int32))
        return running

    grad_hidden = lax.map(backward_col, jnp.arange(N_COL, dtype=jnp.int32)).reshape(NODES, F).astype(jnp.bfloat16)
    grad_features = lax.dot_general(grad_hidden, weight, (((1,), (1,)), ((), ())),
                                    preferred_element_type=jnp.float32).astype(jnp.bfloat16)
    grad_weight = lax.dot_general(features, grad_hidden, (((0,), (0,)), ((), ())),
                                  preferred_element_type=jnp.float32)
    grad_bias = jnp.sum(grad_pre.astype(jnp.float32), axis=0)
    return (out_features, grad_features, grad_weight, grad_bias)
```

```python
import functools

import jax
import jax.numpy as jnp
from jax import lax
from jax.experimental import pallas as pl
from jax.experimental.pallas import tpu as pltpu
from jax.sharding import PartitionSpec as P

TILE = 128
UNROLL = 8
PIECE = 24


def silu_slope(preact):
    squashed = jax.nn.sigmoid(preact)
    return squashed * (1.0 + preact * (1.0 - squashed))


def tile_sums_kernel(dims, source_ref, target_ref, count_ref, tiles_ref, feats_ref, out_ref, acc_ref):
    blocks = out_ref.shape[0] // TILE
    count = count_ref[0]

    def clear(block, carry):
        acc_ref[block] = jnp.zeros(acc_ref.shape[1:], jnp.float32)
        return carry

    def add_group(group, carry):
        products, targets = [], []
        for member in range(UNROLL):
            slot = group * UNROLL + member
            start = pl.multiple_of(source_ref[slot] * TILE, TILE)
            products.append(
                lax.dot_general(
                    tiles_ref[slot], feats_ref[pl.ds(start, TILE), :], (dims, ((), ())),
                    preferred_element_type=jnp.float32,
                )
            )
            targets.append(jnp.where(slot < count, target_ref[slot], blocks))
        for product, target in zip(products, targets):
            acc_ref[target] += product
        return carry

    def finish(block, carry):
        out_ref[pl.ds(pl.multiple_of(block * TILE, TILE), TILE), :] = acc_ref[block].astype(out_ref.dtype)
        return carry

    lax.fori_loop(0, blocks, clear, 0)
    lax.fori_loop(0, (count + UNROLL - 1) // UNROLL, add_group, 0)
    lax.fori_loop(0, blocks, finish, 0)


def tile_sums(tiles, source, target, count, feats, dims):
    rows, channels = feats.shape
    slots = tiles.shape[0]
    return pl.pallas_call(
        functools.partial(tile_sums_kernel, dims),
        out_shape=jax.ShapeDtypeStruct((rows, channels), jnp.bfloat16),
        in_specs=[pl.BlockSpec(memory_space=pltpu.SMEM)] * 3 + [pl.BlockSpec(memory_space=pltpu.VMEM)] * 2,
        out_specs=pl.BlockSpec(memory_space=pltpu.VMEM),
        scratch_shapes=[pltpu.VMEM((rows // TILE + 1, TILE, channels), jnp.float32)],
        compiler_params=pltpu.CompilerParams(vmem_limit_bytes=40 * 2**20),
        cost_estimate=pl.CostEstimate(
            flops=2 * slots * TILE * TILE * channels, bytes_accessed=12 * 2**20, transcendentals=0
        ),
    )(source, target, count, tiles, feats)


def shift_x(value, step):
    return lax.ppermute(value, "row", [(i, (i + 4 * step) % 16) for i in range(16)])


def shift_y(value, step):
    return lax.ppermute(value, "row", [(i, i // 4 * 4 + (i + step) % 4) for i in range(16)])


def scatter_sum(value, shift, me):
    total = lax.dynamic_index_in_dim(value, me, 0, keepdims=False)
    parts = [shift(lax.dynamic_index_in_dim(value, (me + s) % 4, 0, keepdims=False), s) for s in (1, 2, 3)]
    for part in parts:
        total = total + part
    return total


def ring_gather(value, shift, me):
    parts = jnp.stack([value] + [shift(value, s) for s in (1, 2, 3)])
    return jnp.take(parts, (me - jnp.arange(4)) % 4, axis=0)


def sum_everywhere(weight_part, bias_part):
    row, channels = lax.axis_index("row"), weight_part.shape[1]
    bias_rows = jnp.zeros((16, 8, channels), jnp.float32).at[0, 0].set(bias_part)
    packed = jnp.concatenate([weight_part.reshape(16, 16, channels), bias_rows], axis=1)
    packed = packed.reshape(4, 4 * PIECE, channels)
    value = scatter_sum(packed, shift_x, row // 4)
    value = scatter_sum(value.reshape(4, PIECE, channels), shift_y, row % 4)
    for mask in (1, 2, 4, 8):
        value = value + lax.ppermute(value, "col", [(i, i ^ mask) for i in range(16)])
    value = ring_gather(value, shift_y, row % 4).reshape(4 * PIECE, channels)
    value = ring_gather(value, shift_x, row // 4).reshape(16, PIECE, channels)
    return value[:, :16].reshape(weight_part.shape), value[0, 16]


def body(features, weight, out_bias, upstream, adj_tiles, tile_rows, tile_cols, tile_count):
    tiles = adj_tiles[0, 0]
    row_index = tile_rows[0, 0]
    col_index = tile_cols[0, 0]
    count = tile_count[0]
    column_feats = lax.all_gather(features, "row", axis=0, tiled=True)
    part = tile_sums(tiles, col_index, row_index, count, column_feats, ((1,), (0,)))
    gathered = lax.psum_scatter(part, "col", scatter_dimension=0, tiled=True)
    preact = jnp.dot(gathered, weight, preferred_element_type=jnp.float32) + out_bias[None, :]
    grad_pre = (upstream.astype(jnp.float32) * silu_slope(preact)).astype(jnp.bfloat16)
    out_features = jax.nn.silu(preact).astype(jnp.bfloat16)
    row_grads = lax.all_gather(grad_pre, "col", axis=0, tiled=True)
    weight_part = lax.dot_general(
        gathered, grad_pre, (((0,), (0,)), ((), ())), preferred_element_type=jnp.float32
    )
    bias_part = jnp.sum(grad_pre.astype(jnp.float32), axis=0)
    grad_weight, grad_bias = sum_everywhere(weight_part, bias_part)
    back_part = tile_sums(tiles, row_index, col_index, count, row_grads, ((0,), (0,)))
    grad_hidden = lax.psum_scatter(back_part, "row", scatter_dimension=0, tiled=True)
    grad_features = lax.dot_general(
        grad_hidden, weight, (((1,), (1,)), ((), ())), preferred_element_type=jnp.float32
    ).astype(jnp.bfloat16)
    return (out_features, grad_features, grad_weight, grad_bias)


def solution(mesh):
    return jax.shard_map(
        body,
        mesh=mesh,
        in_specs=(
            P(("col", "row"), None),
            P(),
            P(),
            P(("row", "col"), None),
            P("row", "col", None, None, None),
            P("row", "col", None),
            P("row", "col", None),
            P("row", "col"),
        ),
        out_specs=(P(("row", "col"), None), P(("col", "row"), None), P(), P()),
        check_vma=False,
    )
```

```python
import functools

import jax
import jax.numpy as jnp
from jax import lax
from jax.experimental import pallas as pl
from jax.experimental.pallas import tpu as pltpu
from jax.sharding import PartitionSpec as P

TILE = 128
UNROLL = 8
SHARD = 512
LOCAL = SHARD // TILE
PIECE = 24


def silu_slope(preact):
    squashed = jax.nn.sigmoid(preact)
    return squashed * (1.0 + preact * (1.0 - squashed))


def shift_x(value, step):
    return lax.ppermute(value, "row", [(i, (i + 4 * step) % 16) for i in range(16)])


def shift_y(value, step):
    return lax.ppermute(value, "row", [(i, i // 4 * 4 + (i + step) % 4) for i in range(16)])


def shift_z(value, step):
    return lax.ppermute(value, "col", [(i, (i + 2 * step) % 16) for i in range(16)])


def swap_core(value):
    return lax.ppermute(value, "col", [(i, i ^ 1) for i in range(16)])


def total(*values):
    result = values[0].astype(jnp.float32)
    for value in values[1:]:
        result = result + value.astype(jnp.float32)
    return result


def row_place(block, row, sign):
    owner, within = block >> 2, block & 3
    x = (sign * ((owner >> 2) - (row >> 2))) & 3
    y = (sign * (owner - row)) & 3
    return (x * 4 + y) * LOCAL + within


def col_place(block, col, sign):
    owner, within = block >> 2, block & 3
    core = (owner ^ col) & 1
    z = (sign * ((owner >> 1) - (col >> 1))) & 7
    return (core * 8 + z) * LOCAL + within


def sum_tiles(dims, meta_ref, source_ref, target_ref, tiles_ref, feats_ref, acc_ref, source_place, target_place):
    blocks = acc_ref.shape[0] - 1
    count = meta_ref[0]

    def clear(block, carry):
        acc_ref[block] = jnp.zeros(acc_ref.shape[1:], jnp.float32)
        return carry

    def add_group(group, carry):
        products, targets = [], []
        for member in range(UNROLL):
            slot = group * UNROLL + member
            start = pl.multiple_of(source_place(source_ref[slot]) * TILE, TILE)
            products.append(
                lax.dot_general(
                    tiles_ref[slot], feats_ref[pl.ds(start, TILE), :], (dims, ((), ())),
                    preferred_element_type=jnp.float32,
                )
            )
            targets.append(jnp.where(slot < count, target_place(target_ref[slot]), blocks))
        for product, target in zip(products, targets):
            acc_ref[target] += product
        return carry

    lax.fori_loop(0, blocks, clear, 0)
    lax.fori_loop(0, (count + UNROLL - 1) // UNROLL, add_group, 0)


def copy_rows(out_ref, out_start, acc_ref, first_block, blocks, lanes):
    def one(block, carry):
        start = pl.multiple_of(out_start + block * TILE, TILE)
        out_ref[pl.ds(start, TILE), :] = acc_ref[first_block + block, :, lanes].astype(out_ref.dtype)
        return carry

    lax.fori_loop(0, blocks, one, 0)


def place_rows(feats_ref, lanes, place, ref, start, rows):
    def one(step, carry):
        at = step * TILE
        feats_ref[pl.ds(pl.multiple_of(place + at, TILE), TILE), lanes] = ref[pl.ds(pl.multiple_of(start + at, TILE), TILE), :]
        return carry

    lax.fori_loop(0, rows // TILE, one, 0)


def forward_kernel(meta_ref, rows_ref, cols_ref, tiles_ref, *refs):
    pieces, (other_ref, mine_ref, feats_ref, acc_ref) = refs[:10], refs[10:]
    half = feats_ref.shape[1] // 2
    for side, (own, plus, minus, far_a, far_b) in enumerate((pieces[:5], pieces[5:])):
        lanes = pl.ds(side * half, half)
        for second, ref, start, firsts in (
            (0, own, 0, (0, 1, 2, 3)), (1, plus, 0, (0, 1, 2, 3)), (3, minus, 0, (0, 1, 2, 3)),
            (2, far_a, 0, (0, 1)), (2, far_b, 2, (2, 3)),
        ):
            for first in firsts:
                place = first * 4 + second if side == 0 else second * 4 + first
                place_rows(feats_ref, lanes, place * SHARD, ref, (first - start) * SHARD, SHARD)
    row, col = meta_ref[1], meta_ref[2]
    sum_tiles(
        ((1,), (0,)), meta_ref, cols_ref, rows_ref, tiles_ref, feats_ref, acc_ref,
        lambda block: row_place(block, row, -1), lambda block: col_place(block, col, 1),
    )
    copy_rows(mine_ref, 0, acc_ref, 0, 8 * LOCAL, slice(None))
    copy_rows(other_ref, 0, acc_ref, 8 * LOCAL, 8 * LOCAL, slice(None))


def backward_kernel(meta_ref, rows_ref, cols_ref, tiles_ref, *refs):
    pieces, (left_ref, right_ref, feats_ref, acc_ref) = refs[:11], refs[11:]
    own, p1, m1, p2, m2, p3, m3, far_a, far_b, near, rest = pieces
    half_shard = SHARD // 2
    every = slice(None)
    for place, ref in ((0, own), (1, p1), (7, m1), (2, p2), (6, m2), (3, p3), (5, m3)):
        place_rows(feats_ref, every, place * SHARD, ref, 0, SHARD)
    place_rows(feats_ref, every, 4 * SHARD, far_a, 0, half_shard)
    place_rows(feats_ref, every, 4 * SHARD + half_shard, far_b, 0, half_shard)
    for index, place in enumerate((0, 1, 7, 2, 6)):
        place_rows(feats_ref, every, (8 + place) * SHARD, near, index * SHARD, SHARD)
    for index, place in enumerate((3, 5, 4)):
        place_rows(feats_ref, every, (8 + place) * SHARD, rest, index * SHARD, SHARD)
    row, col = meta_ref[1], meta_ref[2]
    sum_tiles(
        ((0,), (0,)), meta_ref, rows_ref, cols_ref, tiles_ref, feats_ref, acc_ref,
        lambda block: col_place(block, col, -1), lambda block: row_place(block, row, 1),
    )
    half = feats_ref.shape[1] // 2
    for x in range(4):
        for y in range(4):
            first_block = (x * 4 + y) * LOCAL
            copy_rows(left_ref, (y * 4 + x) * SHARD, acc_ref, first_block, LOCAL, pl.ds(0, half))
            copy_rows(right_ref, (x * 4 + y) * SHARD, acc_ref, first_block, LOCAL, pl.ds(half, half))


def tile_sums(kernel, outs, meta, rows, cols, tiles, pieces):
    channels = outs[0].shape[1] if kernel is forward_kernel else 2 * outs[0].shape[1]
    nodes = 16 * SHARD
    return pl.pallas_call(
        kernel,
        out_shape=outs,
        in_specs=[pl.BlockSpec(memory_space=pltpu.SMEM)] * 3
        + [pl.BlockSpec(memory_space=pltpu.VMEM)] * (1 + len(pieces)),
        out_specs=[pl.BlockSpec(memory_space=pltpu.VMEM)] * len(outs),
        scratch_shapes=[
            pltpu.VMEM((nodes, channels), jnp.bfloat16),
            pltpu.VMEM((nodes // TILE + 1, TILE, channels), jnp.float32),
        ],
        compiler_params=pltpu.CompilerParams(vmem_limit_bytes=32 * 2**20),
        cost_estimate=pl.CostEstimate(
            flops=2 * tiles.shape[0] * TILE * TILE * channels, bytes_accessed=12 * 2**20, transcendentals=0
        ),
    )(meta, rows, cols, tiles, *pieces)


def gather_two(value, first_shift, second_shift):
    own = jnp.concatenate([value] + [first_shift(value, step) for step in (1, 2, 3)])
    plus, minus = second_shift(own, 1), second_shift(own, -1)
    middle = own.shape[0] // 2
    far_a, far_b = second_shift(plus[:middle], 1), second_shift(minus[middle:], -1)
    return own, plus, minus, far_a, far_b


def scatter_two(value, first_shift, second_shift):
    value = value.reshape(4, 4 * SHARD, value.shape[1])
    middle = 2 * SHARD
    far_a, far_b = second_shift(value[2, :middle], 1), second_shift(value[2, middle:], -1)
    plus = jnp.concatenate([total(value[1, :middle], far_a).astype(jnp.bfloat16), value[1, middle:]])
    minus = jnp.concatenate([value[3, :middle], total(value[3, middle:], far_b).astype(jnp.bfloat16)])
    plus, minus = second_shift(plus, 1), second_shift(minus, -1)
    value = total(value[0], plus, minus).astype(jnp.bfloat16).reshape(4, SHARD, value.shape[2])
    return total(value[0], *[first_shift(value[step], step) for step in (1, 2, 3)])


def scatter_z(mine, other):
    other = swap_core(other)
    mine, other = mine.reshape(8, SHARD, -1), other.reshape(8, SHARD, -1)
    middle = SHARD // 2
    far = total(mine[4], other[4]).astype(jnp.bfloat16)
    plus, minus = shift_z(far[:middle], 1), shift_z(far[middle:], -1)
    for step in (3, 2, 1):
        if step == 3:
            up = jnp.concatenate([total(mine[3, :middle], other[3, :middle], plus), total(mine[3, middle:], other[3, middle:])])
            down = jnp.concatenate([total(mine[5, :middle], other[5, :middle]), total(mine[5, middle:], other[5, middle:], minus)])
        else:
            up, down = total(mine[step], other[step], plus), total(mine[8 - step], other[8 - step], minus)
        plus, minus = shift_z(up.astype(jnp.bfloat16), 1), shift_z(down.astype(jnp.bfloat16), -1)
    return total(mine[0], other[0], plus, minus)


def gather_z(value):
    middle = SHARD // 2
    p1, m1 = shift_z(value, 1), shift_z(value, -1)
    p2, m2 = shift_z(p1, 1), shift_z(m1, -1)
    p3, m3 = shift_z(p2, 1), shift_z(m2, -1)
    far_a, far_b = shift_z(p3[:middle], 1), shift_z(m3[middle:], -1)
    near = swap_core(jnp.concatenate([value, p1, m1, p2, m2]))
    rest = swap_core(jnp.concatenate([p3, m3, far_a, far_b]))
    return value, p1, m1, p2, m2, p3, m3, far_a, far_b, near, rest


def scatter_sum(value, shift, me):
    result = lax.dynamic_index_in_dim(value, me, 0, keepdims=False)
    parts = [shift(lax.dynamic_index_in_dim(value, (me + s) % 4, 0, keepdims=False), s) for s in (1, 2, 3)]
    for part in parts:
        result = result + part
    return result


def ring_gather(value, shift, me):
    parts = jnp.stack([value] + [shift(value, s) for s in (1, 2, 3)])
    return jnp.take(parts, (me - jnp.arange(4)) % 4, axis=0)


def sum_everywhere(weight_part, bias_part):
    row, channels = lax.axis_index("row"), weight_part.shape[1]
    bias_rows = jnp.zeros((16, 8, channels), jnp.float32).at[0, 0].set(bias_part)
    packed = jnp.concatenate([weight_part.reshape(16, 16, channels), bias_rows], axis=1)
    packed = packed.reshape(4, 4 * PIECE, channels)
    value = scatter_sum(packed, shift_x, row // 4)
    value = scatter_sum(value.reshape(4, PIECE, channels), shift_y, row % 4)
    for mask in (1, 2, 4, 8):
        value = value + lax.ppermute(value, "col", [(i, i ^ mask) for i in range(16)])
    value = ring_gather(value, shift_y, row % 4).reshape(4 * PIECE, channels)
    value = ring_gather(value, shift_x, row // 4).reshape(16, PIECE, channels)
    return value[:, :16].reshape(weight_part.shape), value[0, 16]


def body(features, weight, out_bias, upstream, adj_tiles, tile_rows, tile_cols, tile_count):
    tiles, rows, cols = adj_tiles[0, 0], tile_rows[0, 0], tile_cols[0, 0]
    meta = jnp.stack([tile_count[0, 0], lax.axis_index("row"), lax.axis_index("col")])
    channels = features.shape[1]
    half = channels // 2

    left = gather_two(features[:, :half], shift_x, shift_y)
    right = gather_two(features[:, half:], shift_y, shift_x)
    part = jax.ShapeDtypeStruct((8 * SHARD, channels), jnp.bfloat16)
    other, mine = tile_sums(forward_kernel, [part, part], meta, rows, cols, tiles, left + right)
    gathered = scatter_z(mine, other).astype(jnp.bfloat16)

    preact = jnp.dot(gathered, weight, preferred_element_type=jnp.float32) + out_bias[None, :]
    grad_pre = (upstream.astype(jnp.float32) * silu_slope(preact)).astype(jnp.bfloat16)
    out_features = jax.nn.silu(preact).astype(jnp.bfloat16)
    weight_part = lax.dot_general(
        gathered, grad_pre, (((0,), (0,)), ((), ())), preferred_element_type=jnp.float32
    )
    bias_part = jnp.sum(grad_pre.astype(jnp.float32), axis=0)
    grad_weight, grad_bias = sum_everywhere(weight_part, bias_part)

    pieces = gather_z(grad_pre)
    part = jax.ShapeDtypeStruct((16 * SHARD, half), jnp.bfloat16)
    left, right = tile_sums(backward_kernel, [part, part], meta, rows, cols, tiles, pieces)
    left = scatter_two(left, shift_x, shift_y)
    right = scatter_two(right, shift_y, shift_x)
    grad_hidden = jnp.concatenate([left, right], axis=1).astype(jnp.bfloat16)
    grad_features = lax.dot_general(
        grad_hidden, weight, (((1,), (1,)), ((), ())), preferred_element_type=jnp.float32
    ).astype(jnp.bfloat16)
    return (out_features, grad_features, grad_weight, grad_bias)


def solution(mesh):
    return jax.shard_map(
        body,
        mesh=mesh,
        in_specs=(
            P(("col", "row"), None),
            P(),
            P(),
            P(("row", "col"), None),
            P("row", "col", None, None, None),
            P("row", "col", None),
            P("row", "col", None),
            P("row", "col"),
        ),
        out_specs=(P(("row", "col"), None), P(("col", "row"), None), P(), P()),
        check_vma=False,
    )
```

```python
import jax
import jax.numpy as jnp
from jax import lax
from jax.experimental import pallas as pl
from jax.experimental.pallas import tpu as pltpu
from jax.sharding import PartitionSpec as P

TILE = 128
UNROLL = 8
SHARD = 512
LOCAL = SHARD // TILE
PIECE = 24


def shift_x(value, step):
    return lax.ppermute(value, "row", [(i, (i + 4 * step) % 16) for i in range(16)])


def shift_y(value, step):
    return lax.ppermute(value, "row", [(i, i // 4 * 4 + (i + step) % 4) for i in range(16)])


def shift_z(value, step):
    return lax.ppermute(value, "col", [(i, (i + 2 * step) % 16) for i in range(16)])


def swap_core(value):
    return lax.ppermute(value, "col", [(i, i ^ 1) for i in range(16)])


def total(*values):
    result = values[0].astype(jnp.float32)
    for value in values[1:]:
        result = result + value.astype(jnp.float32)
    return result


def row_place(block, row, sign):
    owner, within = block >> 2, block & 3
    return (sign * ((owner >> 2) - (row >> 2))) & 3, (sign * (owner - row)) & 3, within


def col_place(block, col):
    owner, within = block >> 2, block & 3
    core = (owner ^ col) & 1
    z = ((owner >> 1) - (col >> 1)) & 7
    return (core * 8 + z) * LOCAL + within


def sum_tiles(dims, meta_ref, source_ref, target_ref, tiles_ref, load, acc_ref, target_place):
    blocks = acc_ref.shape[0] - 1
    count = meta_ref[0]

    def add_group(group, carry):
        products, targets = [], []
        for member in range(UNROLL):
            slot = group * UNROLL + member
            products.append(
                lax.dot_general(
                    tiles_ref[slot], load(source_ref[slot]), (dims, ((), ())), preferred_element_type=jnp.float32
                )
            )
            targets.append(jnp.where(slot < count, target_place(target_ref[slot]), blocks))
        for product, target in zip(products, targets):
            acc_ref[target] += product
        return carry

    lax.fori_loop(0, (count + UNROLL - 1) // UNROLL, add_group, 0)


def clear(acc_ref):
    def one(block, carry):
        acc_ref[block] = jnp.zeros(acc_ref.shape[1:], jnp.float32)
        return carry

    lax.fori_loop(0, acc_ref.shape[0], one, 0)


def forward_kernel(meta_ref, rows_ref, cols_ref, tiles_ref, *refs):
    pieces, (mine_ref, other_ref, feats_ref, acc_ref, sems) = refs[:8], refs[8:]
    half = feats_ref.shape[4] // 2
    copies = []
    for step in range(4):
        for side in range(2):
            index = side * 4 + step
            if side == 0:
                there = feats_ref.at[:, step, :, :, pl.ds(0, half)]
            else:
                there = feats_ref.at[step, :, :, :, pl.ds(half, half)]
            copies.append(pltpu.make_async_copy(pieces[index], there, sems.at[index]))
    for copy in copies:
        copy.start()
    clear(acc_ref)
    for copy in copies:
        copy.wait()
    row, col = meta_ref[1], meta_ref[2]

    def load(block):
        x, y, within = row_place(block, row, -1)
        return feats_ref[x, y, within]

    sum_tiles(
        ((1,), (0,)), meta_ref, cols_ref, rows_ref, tiles_ref, load, acc_ref, lambda block: col_place(block, col)
    )

    def finish(step, carry):
        mine_ref[step >> 2, step & 3] = acc_ref[step].astype(jnp.bfloat16)
        other_ref[step >> 2, step & 3] = acc_ref[8 * LOCAL + step].astype(jnp.bfloat16)
        return carry

    lax.fori_loop(0, 8 * LOCAL, finish, 0)


def backward_kernel(meta_ref, rows_ref, cols_ref, tiles_ref, grads_ref, *refs):
    outs, (feats_ref, acc_ref, sem) = refs[:8], refs[8:]
    copy = pltpu.make_async_copy(grads_ref, feats_ref, sem)
    copy.start()
    clear(acc_ref)
    copy.wait()
    row = meta_ref[1]

    def place(block):
        x, y, within = row_place(block, row, 1)
        return (x * 4 + y) * LOCAL + within

    sum_tiles(
        ((0,), (0,)), meta_ref, rows_ref, cols_ref, tiles_ref, lambda block: feats_ref[block], acc_ref, place
    )
    half = feats_ref.shape[2] // 2
    for step in range(4):

        def finish(index, carry):
            first, within = index >> 2, index & 3
            left = acc_ref[(first * 4 + step) * LOCAL + within, :, pl.ds(0, half)]
            right = acc_ref[(step * 4 + first) * LOCAL + within, :, pl.ds(half, half)]
            outs[step][first, within] = left.astype(jnp.bfloat16)
            outs[4 + step][first, within] = right.astype(jnp.bfloat16)
            return carry

        lax.fori_loop(0, 4 * LOCAL, finish, 0)


SMEM = pl.BlockSpec(memory_space=pltpu.SMEM)
VMEM = pl.BlockSpec(memory_space=pltpu.VMEM)
ANY = pl.BlockSpec(memory_space=pl.ANY)


def tile_sums(kernel, outs, scratch, meta, rows, cols, tiles, pieces):
    channels = 256
    blocks = 16 * LOCAL
    return pl.pallas_call(
        kernel,
        out_shape=outs,
        in_specs=[SMEM] * 3 + [VMEM] + [ANY] * len(pieces),
        out_specs=[VMEM] * len(outs),
        scratch_shapes=[
            pltpu.VMEM(scratch, jnp.bfloat16),
            pltpu.VMEM((blocks + 1, TILE, channels), jnp.float32),
            pltpu.SemaphoreType.DMA((len(pieces),)) if len(pieces) > 1 else pltpu.SemaphoreType.DMA,
        ],
        compiler_params=pltpu.CompilerParams(vmem_limit_bytes=28 * 2**20),
        cost_estimate=pl.CostEstimate(
            flops=2 * tiles.shape[0] * TILE * TILE * channels, bytes_accessed=12 * 2**20, transcendentals=0
        ),
    )(meta, rows, cols, tiles, *pieces)


def middle_kernel(meta_ref, mine_ref, other_ref, plus_ref, minus_ref, weight_ref, bias_ref, upstream_ref,
                  out_ref, grad_ref, parts_ref):
    gathered = total(mine_ref[0], other_ref[0], plus_ref[...], minus_ref[...]).astype(jnp.bfloat16)
    preact = jnp.dot(gathered, weight_ref[...], preferred_element_type=jnp.float32) + bias_ref[...]
    squashed = jax.nn.sigmoid(preact)
    out_ref[...] = (preact * squashed).astype(jnp.bfloat16)
    slope = squashed * (1.0 + preact * (1.0 - squashed))
    grad = (upstream_ref[...].astype(jnp.float32) * slope).astype(jnp.bfloat16)
    grad_ref[...] = grad
    weight_part = lax.dot_general(gathered, grad, (((0,), (0,)), ((), ())), preferred_element_type=jnp.float32)
    bias_part = jnp.sum(grad.astype(jnp.float32), axis=0, keepdims=True)
    first = lax.broadcasted_iota(jnp.int32, (PIECE - 16, bias_part.shape[1]), 0) == 0
    row = meta_ref[1]
    for owner in range(16):
        x, y = ((owner >> 2) - (row >> 2)) & 3, (owner - row) & 3
        parts_ref[x, y, :16] = weight_part[owner * 16 : owner * 16 + 16]
        parts_ref[x, y, 16:] = jnp.where(first, bias_part, 0.0) if owner == 0 else jnp.zeros(first.shape, jnp.float32)


def middle(meta, mine, other, plus, minus, weight, bias, upstream):
    channels = weight.shape[0]
    shard = pl.BlockSpec((1, SHARD, channels), lambda step: (0, 0, 0))
    return pl.pallas_call(
        middle_kernel,
        grid=(1,),
        out_shape=[
            jax.ShapeDtypeStruct(upstream.shape, jnp.bfloat16),
            jax.ShapeDtypeStruct(upstream.shape, jnp.bfloat16),
            jax.ShapeDtypeStruct((4, 4, PIECE, channels), jnp.float32),
        ],
        in_specs=[SMEM, shard, shard] + [VMEM] * 5,
        out_specs=[VMEM] * 3,
        compiler_params=pltpu.CompilerParams(vmem_limit_bytes=16 * 2**20),
    )(meta, mine, other, plus, minus, weight, bias, upstream)


def unpack_kernel(meta_ref, value_ref, weight_ref, bias_ref):
    row = meta_ref[1]
    for x in range(4):
        for y in range(4):
            owner = (((row >> 2) - x) & 3) * 4 + ((row - y) & 3)
            weight_ref[owner] = value_ref[x, y, :16]
    bias_ref[...] = value_ref[row >> 2, row & 3, 16:17]


def unpack(meta, value):
    channels = value.shape[3]
    return pl.pallas_call(
        unpack_kernel,
        out_shape=[
            jax.ShapeDtypeStruct((16, 16, channels), jnp.float32),
            jax.ShapeDtypeStruct((1, channels), jnp.float32),
        ],
        in_specs=[SMEM, VMEM],
        out_specs=[VMEM] * 2,
    )(meta, value)


def split_kernel(own_ref, plus_ref, far_ref, minus_ref, *outs):
    for step, out_ref in enumerate(outs):
        out_ref[...] = total(own_ref[step], plus_ref[step], far_ref[step], minus_ref[step]).astype(jnp.bfloat16)


def split(own, plus, far, minus):
    shard = jax.ShapeDtypeStruct(own.shape[1:], jnp.bfloat16)
    return pl.pallas_call(
        split_kernel, out_shape=[shard] * 4, in_specs=[VMEM] * 4, out_specs=[VMEM] * 4,
        compiler_params=pltpu.CompilerParams(vmem_limit_bytes=16 * 2**20),
    )(own, plus, far, minus)


def last_kernel(*refs):
    weight_ref, out_ref = refs[8:]
    half = refs[0].shape[1]
    result = None
    for side in range(2):
        hidden = total(*[ref[...] for ref in refs[side * 4 : side * 4 + 4]]).astype(jnp.bfloat16)
        product = lax.dot_general(
            hidden, weight_ref[:, side * half : side * half + half], (((1,), (1,)), ((), ())),
            preferred_element_type=jnp.float32,
        )
        result = product if result is None else result + product
    out_ref[...] = result.astype(jnp.bfloat16)


def last(left, right, weight):
    return pl.pallas_call(
        last_kernel,
        out_shape=jax.ShapeDtypeStruct((SHARD, weight.shape[0]), jnp.bfloat16),
        in_specs=[VMEM] * 9,
        out_specs=VMEM,
        compiler_params=pltpu.CompilerParams(vmem_limit_bytes=16 * 2**20),
    )(*left, *right, weight)


def gather_two(value, first_shift, second_shift):
    own = jnp.stack([value] + [first_shift(value, step) for step in (1, 2, 3)])
    own = own.reshape(4, LOCAL, TILE, value.shape[1])
    return [own] + [second_shift(own, step) for step in (1, 2, 3)]


def scatter_two(pieces, first_shift, second_shift):
    pieces = [piece.reshape(4, SHARD, piece.shape[3]) for piece in pieces]
    moved = [second_shift(pieces[step], step) for step in (1, 2, 3)]
    pieces = split(pieces[0], *moved)
    return [pieces[0]] + [first_shift(pieces[step], step) for step in (1, 2, 3)]


def scatter_z(mine, other):
    other = swap_core(other)
    mine, other = mine.reshape(8, SHARD, -1), other.reshape(8, SHARD, -1)
    middle = SHARD // 2
    far = total(mine[4], other[4]).astype(jnp.bfloat16)
    plus, minus = shift_z(far[:middle], 1), shift_z(far[middle:], -1)
    for step in (3, 2, 1):
        if step == 3:
            up = jnp.concatenate([total(mine[3, :middle], other[3, :middle], plus), total(mine[3, middle:], other[3, middle:])])
            down = jnp.concatenate([total(mine[5, :middle], other[5, :middle]), total(mine[5, middle:], other[5, middle:], minus)])
        else:
            up, down = total(mine[step], other[step], plus), total(mine[8 - step], other[8 - step], minus)
        plus, minus = shift_z(up.astype(jnp.bfloat16), 1), shift_z(down.astype(jnp.bfloat16), -1)
    return mine, other, plus, minus


def sum_everywhere(meta, parts):
    value = sum([shift_x(parts[step], step) for step in (1, 2, 3)], parts[0])
    value = sum([shift_y(value[step], step) for step in (1, 2, 3)], value[0])
    for mask in (1, 2, 4, 8):
        value = value + lax.ppermute(value, "col", [(i, i ^ mask) for i in range(16)])
    value = jnp.stack([value] + [shift_y(value, step) for step in (1, 2, 3)])
    value = jnp.stack([value] + [shift_x(value, step) for step in (1, 2, 3)])
    return unpack(meta, value)


def body(features, weight, out_bias, upstream, adj_tiles, tile_rows, tile_cols, tile_count):
    tiles, rows, cols = adj_tiles[0, 0], tile_rows[0, 0], tile_cols[0, 0]
    meta = jnp.stack([tile_count[0, 0], lax.axis_index("row"), lax.axis_index("col")])
    channels = features.shape[1]
    half = channels // 2

    left = gather_two(features[:, :half], shift_x, shift_y)
    right = gather_two(features[:, half:], shift_y, shift_x)
    part = jax.ShapeDtypeStruct((8, LOCAL, TILE, channels), jnp.bfloat16)
    mine, other = tile_sums(
        forward_kernel, [part] * 2, (4, 4, LOCAL, TILE, channels), meta, rows, cols, tiles, left + right
    )
    terms = scatter_z(mine.reshape(8, SHARD, channels), other.reshape(8, SHARD, channels))
    out_features, grad_pre, parts = middle(meta, *terms, weight, out_bias[None, :], upstream)

    row_grads = lax.all_gather(grad_pre, "col", axis=0, tiled=True)
    grad_weight, grad_bias = sum_everywhere(meta, parts)
    row_grads, grad_weight, grad_bias = lax.optimization_barrier((row_grads, grad_weight, grad_bias))

    part = jax.ShapeDtypeStruct((4, LOCAL, TILE, half), jnp.bfloat16)
    row_grads = row_grads.reshape(16 * LOCAL, TILE, channels)
    pieces = tile_sums(backward_kernel, [part] * 8, row_grads.shape, meta, rows, cols, tiles, [row_grads])
    left = scatter_two(pieces[:4], shift_x, shift_y)
    right = scatter_two(pieces[4:], shift_y, shift_x)
    grad_features = last(left, right, weight)
    return (out_features, grad_features, grad_weight.reshape(weight.shape), grad_bias[0])


def solution(mesh):
    return jax.shard_map(
        body,
        mesh=mesh,
        in_specs=(
            P(("col", "row"), None),
            P(),
            P(),
            P(("row", "col"), None),
            P("row", "col", None, None, None),
            P("row", "col", None),
            P("row", "col", None),
            P("row", "col"),
        ),
        out_specs=(P(("row", "col"), None), P(("col", "row"), None), P(), P()),
        check_vma=False,
    )
```

```python
import jax
import jax.numpy as jnp
from jax import lax
from jax.experimental import pallas as pl
from jax.experimental.pallas import tpu as pltpu
from jax.sharding import PartitionSpec as P

TILE = 128
UNROLL = 8
SHARD = 512
LOCAL = SHARD // TILE
PIECE = 32


def shift_x(value, step):
    return lax.ppermute(value, "row", [(i, (i + 4 * step) % 16) for i in range(16)])


def shift_y(value, step):
    return lax.ppermute(value, "row", [(i, i // 4 * 4 + (i + step) % 4) for i in range(16)])


def shift_z(value, step):
    return lax.ppermute(value, "col", [(i, (i + 2 * step) % 16) for i in range(16)])


def swap_core(value):
    return lax.ppermute(value, "col", [(i, i ^ 1) for i in range(16)])


def total(*values):
    result = values[0].astype(jnp.float32)
    for value in values[1:]:
        result = result + value.astype(jnp.float32)
    return result


def row_place(block, row, sign):
    owner, within = block >> 2, block & 3
    return (sign * ((owner >> 2) - (row >> 2))) & 3, (sign * (owner - row)) & 3, within


def col_place(block, col, sign):
    owner, within = block >> 2, block & 3
    return (owner ^ col) & 1, (sign * ((owner >> 1) - (col >> 1))) & 7, within


def sum_tiles(dims, meta_ref, source_ref, target_ref, tiles_ref, load, acc_ref, target_place):
    blocks = acc_ref.shape[0] - 1
    count = meta_ref[0]

    def add_group(group, carry):
        products, targets = [], []
        for member in range(UNROLL):
            slot = group * UNROLL + member
            products.append(
                lax.dot_general(
                    tiles_ref[slot], load(source_ref[slot]), (dims, ((), ())), preferred_element_type=jnp.float32
                )
            )
            targets.append(jnp.where(slot < count, target_place(target_ref[slot]), blocks))
        for product, target in zip(products, targets):
            acc_ref[target] += product
        return carry

    lax.fori_loop(0, (count + UNROLL - 1) // UNROLL, add_group, 0)


def clear(acc_ref):
    def one(block, carry):
        acc_ref[block] = jnp.zeros(acc_ref.shape[1:], jnp.float32)
        return carry

    lax.fori_loop(0, acc_ref.shape[0], one, 0)


def forward_kernel(meta_ref, rows_ref, cols_ref, tiles_any, *refs):
    pieces, (mine_ref, other_ref, tiles_ref, feats_ref, acc_ref, sems) = refs[:8], refs[8:]
    half = feats_ref.shape[4] // 2
    copies = [pltpu.make_async_copy(tiles_any, tiles_ref, sems.at[8])]
    for step in range(4):
        for side in range(2):
            index = side * 4 + step
            if side == 0:
                there = feats_ref.at[:, step, :, :, pl.ds(0, half)]
            else:
                there = feats_ref.at[step, :, :, :, pl.ds(half, half)]
            copies.append(pltpu.make_async_copy(pieces[index], there, sems.at[index]))
    for copy in copies:
        copy.start()
    clear(acc_ref)
    for copy in copies:
        copy.wait()
    row, col = meta_ref[1], meta_ref[2]

    def load(block):
        x, y, within = row_place(block, row, -1)
        return feats_ref[x, y, within]

    def target(block):
        core, z, within = col_place(block, col, 1)
        return (core * 8 + z) * LOCAL + within

    sum_tiles(
        ((1,), (0,)), meta_ref, cols_ref, rows_ref, tiles_ref, load, acc_ref, target
    )

    def finish(step, carry):
        mine_ref[step >> 2, step & 3] = acc_ref[step].astype(jnp.bfloat16)
        other_ref[step >> 2, step & 3] = acc_ref[8 * LOCAL + step].astype(jnp.bfloat16)
        return carry

    lax.fori_loop(0, 8 * LOCAL, finish, 0)


def backward_kernel(meta_ref, rows_ref, cols_ref, tiles_any, *refs):
    pieces, value_ref, outs, (tiles_ref, feats_ref, acc_ref, sems) = refs[:11], refs[11], refs[12:20], refs[20:]
    own, p1, m1, p2, m2, p3, m3, far_a, far_b, near, rest = pieces
    middle = SHARD // 2
    sources = [(own, 0), (p1, 1), (m1, 7), (p2, 2), (m2, 6), (p3, 3), (m3, 5)]
    sources = [(ref, feats_ref.at[place]) for ref, place in sources]
    sources.append((far_a, feats_ref.at[4, pl.ds(0, middle)]))
    sources.append((far_b, feats_ref.at[4, pl.ds(middle, middle)]))
    sources += [(near.at[index], feats_ref.at[8 + place]) for index, place in enumerate((0, 1, 7, 2, 6))]
    sources += [(rest.at[index], feats_ref.at[8 + place]) for index, place in enumerate((3, 5, 4))]
    sources.append((tiles_any, tiles_ref))
    copies = [pltpu.make_async_copy(ref, there, sems.at[index]) for index, (ref, there) in enumerate(sources)]
    for copy in copies:
        copy.start()
    clear(acc_ref)
    for copy in copies:
        copy.wait()
    col = meta_ref[2]

    def load(block):
        core, z, within = col_place(block, col, -1)
        return feats_ref[core * 8 + z, pl.ds(pl.multiple_of(within * TILE, TILE), TILE), :]

    row = meta_ref[1]

    def place(block):
        x, y, within = row_place(block, row, 1)
        return (x * 4 + y) * LOCAL + within

    sum_tiles(
        ((0,), (0,)), meta_ref, rows_ref, cols_ref, tiles_ref, load, acc_ref, place
    )
    half = feats_ref.shape[2] // 2
    value = value_ref[...].astype(jnp.bfloat16)
    for step in range(4):

        def finish(index, carry):
            first, within = index >> 2, index & 3
            left = acc_ref[(first * 4 + step) * LOCAL + within, :, pl.ds(0, half)]
            right = acc_ref[(step * 4 + first) * LOCAL + within, :, pl.ds(half, half)]
            start = pl.multiple_of(index * TILE, TILE)
            outs[step][pl.ds(start, TILE), :] = left.astype(jnp.bfloat16)
            outs[4 + step][pl.ds(start, TILE), :] = right.astype(jnp.bfloat16)
            return carry

        lax.fori_loop(0, 4 * LOCAL, finish, 0)
        outs[step][pl.ds(4 * SHARD, PIECE), :] = value[:, :half]
        outs[4 + step][pl.ds(4 * SHARD, PIECE), :] = value[:, half:]


SMEM = pl.BlockSpec(memory_space=pltpu.SMEM)
VMEM = pl.BlockSpec(memory_space=pltpu.VMEM)
ANY = pl.BlockSpec(memory_space=pl.ANY)


def tile_sums(kernel, outs, scratch, copies, meta, rows, cols, tiles, pieces, more=()):
    channels = scratch[-1]
    blocks = 16 * LOCAL
    return pl.pallas_call(
        kernel,
        out_shape=outs,
        in_specs=[SMEM] * 3 + [ANY] * (1 + len(pieces)) + [VMEM] * len(more),
        out_specs=[VMEM] * len(outs),
        scratch_shapes=[
            pltpu.VMEM(tiles.shape, jnp.bfloat16),
            pltpu.VMEM(scratch, jnp.bfloat16),
            pltpu.VMEM((blocks + 1, TILE, channels), jnp.float32),
            pltpu.SemaphoreType.DMA((copies,)),
        ],
        compiler_params=pltpu.CompilerParams(vmem_limit_bytes=28 * 2**20),
        cost_estimate=pl.CostEstimate(
            flops=2 * tiles.shape[0] * TILE * TILE * channels, bytes_accessed=12 * 2**20, transcendentals=0
        ),
    )(meta, rows, cols, tiles, *pieces, *more)


def middle_kernel(meta_ref, mine_ref, other_ref, plus_ref, minus_ref, weight_ref, bias_ref, upstream_ref,
                  out_ref, grad_ref, parts_ref):
    gathered = total(mine_ref[0], other_ref[0], plus_ref[...], minus_ref[...]).astype(jnp.bfloat16)
    preact = jnp.dot(gathered, weight_ref[...], preferred_element_type=jnp.float32) + bias_ref[...]
    squashed = jax.nn.sigmoid(preact)
    out_ref[...] = (preact * squashed).astype(jnp.bfloat16)
    slope = squashed * (1.0 + preact * (1.0 - squashed))
    grad = (upstream_ref[...].astype(jnp.float32) * slope).astype(jnp.bfloat16)
    grad_ref[...] = grad
    weight_part = lax.dot_general(gathered, grad, (((0,), (0,)), ((), ())), preferred_element_type=jnp.float32)
    bias_part = jnp.sum(grad.astype(jnp.float32), axis=0, keepdims=True)
    first = lax.broadcasted_iota(jnp.int32, (PIECE - 16, bias_part.shape[1]), 0) == 0
    row = meta_ref[1]
    for owner in range(16):
        x, y = ((owner >> 2) - (row >> 2)) & 3, (owner - row) & 3
        parts_ref[x, y, :16] = weight_part[owner * 16 : owner * 16 + 16]
        parts_ref[x, y, 16:] = jnp.where(first, bias_part, 0.0) if owner == 0 else jnp.zeros(first.shape, jnp.float32)


def middle(meta, mine, other, plus, minus, weight, bias, upstream):
    channels = weight.shape[0]
    shard = pl.BlockSpec((1, SHARD, channels), lambda step: (0, 0, 0))
    return pl.pallas_call(
        middle_kernel,
        grid=(1,),
        out_shape=[
            jax.ShapeDtypeStruct(upstream.shape, jnp.bfloat16),
            jax.ShapeDtypeStruct(upstream.shape, jnp.bfloat16),
            jax.ShapeDtypeStruct((4, 4, PIECE, channels), jnp.float32),
        ],
        in_specs=[SMEM, shard, shard] + [VMEM] * 5,
        out_specs=[VMEM] * 3,
        compiler_params=pltpu.CompilerParams(vmem_limit_bytes=16 * 2**20),
    )(meta, mine, other, plus, minus, weight, bias, upstream)


def split_kernel(own_ref, plus_ref, far_ref, minus_ref, *outs):
    arrived = (own_ref, plus_ref, far_ref, minus_ref)
    for step, out_ref in enumerate(outs):
        at = pl.ds(step * SHARD, SHARD)
        out_ref[pl.ds(0, SHARD), :] = total(*[ref[at, :] for ref in arrived]).astype(jnp.bfloat16)
        for index, ref in enumerate(arrived):
            out_ref[pl.ds(SHARD + index * PIECE, PIECE), :] = ref[pl.ds(4 * SHARD, PIECE), :]


def split(own, plus, far, minus):
    shard = jax.ShapeDtypeStruct((SHARD + 4 * PIECE, own.shape[1]), jnp.bfloat16)
    return pl.pallas_call(
        split_kernel, out_shape=[shard] * 4, in_specs=[VMEM] * 4, out_specs=[VMEM] * 4,
        compiler_params=pltpu.CompilerParams(vmem_limit_bytes=16 * 2**20),
    )(own, plus, far, minus)


def last_kernel(meta_ref, *refs):
    weight_ref, out_ref, grad_weight_ref, grad_bias_ref = refs[8:]
    row = meta_ref[1]
    half = refs[0].shape[1]
    result = None
    for side in range(2):
        arrived = refs[side * 4 : side * 4 + 4]
        lanes = slice(side * half, side * half + half)
        hidden = total(*[ref[pl.ds(0, SHARD), :] for ref in arrived]).astype(jnp.bfloat16)
        product = lax.dot_general(
            hidden, weight_ref[:, lanes], (((1,), (1,)), ((), ())), preferred_element_type=jnp.float32
        )
        result = product if result is None else result + product
        for first in range(4):
            for second in range(4):
                x, y = (first, second) if side == 0 else (second, first)
                x, y = ((row >> 2) - x) & 3, (row - y) & 3
                at = SHARD + second * PIECE
                piece = arrived[first][pl.ds(at, PIECE), :].astype(jnp.float32)
                grad_weight_ref[x * 4 + y, :, lanes] = piece[:16]

                @pl.when(x * 4 + y == 0)
                def _():
                    grad_bias_ref[:, lanes] = piece[16:17]

    out_ref[...] = result.astype(jnp.bfloat16)


def last(meta, left, right, weight):
    channels = weight.shape[0]
    return pl.pallas_call(
        last_kernel,
        out_shape=[
            jax.ShapeDtypeStruct((SHARD, channels), jnp.bfloat16),
            jax.ShapeDtypeStruct((16, 16, channels), jnp.float32),
            jax.ShapeDtypeStruct((1, channels), jnp.float32),
        ],
        in_specs=[SMEM] + [VMEM] * 9,
        out_specs=[VMEM] * 3,
        compiler_params=pltpu.CompilerParams(vmem_limit_bytes=16 * 2**20),
    )(meta, *left, *right, weight)


def gather_two(features):
    half = features.shape[1] // 2
    left, right = features[:, :half], features[:, half:]
    left = jnp.stack([left] + [shift_x(left, step) for step in (1, 2, 3)]).reshape(4, LOCAL, TILE, half)
    right = jnp.stack([right] + [shift_y(right, step) for step in (1, 2, 3)]).reshape(4, LOCAL, TILE, half)
    left, right = lax.optimization_barrier((left, right))
    return [left] + [shift_y(left, step) for step in (1, 2, 3)] + [right] + [shift_x(right, step) for step in (1, 2, 3)]


def scatter_two(pieces, first_shift, second_shift):
    moved = [second_shift(pieces[step], step) for step in (1, 2, 3)]
    pieces = split(pieces[0], *moved)
    return [pieces[0]] + [first_shift(pieces[step], step) for step in (1, 2, 3)]


def scatter_z(mine, other):
    other = swap_core(other)
    mine, other = mine.reshape(8, SHARD, -1), other.reshape(8, SHARD, -1)
    middle = SHARD // 2
    far = total(mine[4], other[4]).astype(jnp.bfloat16)
    plus, minus = shift_z(far[:middle], 1), shift_z(far[middle:], -1)
    for step in (3, 2, 1):
        if step == 3:
            up = jnp.concatenate([total(mine[3, :middle], other[3, :middle], plus), total(mine[3, middle:], other[3, middle:])])
            down = jnp.concatenate([total(mine[5, :middle], other[5, :middle]), total(mine[5, middle:], other[5, middle:], minus)])
        else:
            up, down = total(mine[step], other[step], plus), total(mine[8 - step], other[8 - step], minus)
        plus, minus = shift_z(up.astype(jnp.bfloat16), 1), shift_z(down.astype(jnp.bfloat16), -1)
    return mine, other, plus, minus


def gather_z(value):
    middle = SHARD // 2
    p1, m1 = shift_z(value, 1), shift_z(value, -1)
    p2, m2 = shift_z(p1, 1), shift_z(m1, -1)
    p3, m3 = shift_z(p2, 1), shift_z(m2, -1)
    far_a, far_b = shift_z(p3[:middle], 1), shift_z(m3[middle:], -1)
    near = swap_core(jnp.stack([value, p1, m1, p2, m2]))
    rest = swap_core(jnp.stack([p3, m3, jnp.concatenate([far_a, far_b])]))
    return value, p1, m1, p2, m2, p3, m3, far_a, far_b, near, rest


def sum_pieces(parts):
    value = sum([shift_x(parts[step], step) for step in (1, 2, 3)], parts[0])
    value = sum([shift_y(value[step], step) for step in (1, 2, 3)], value[0])
    for mask in (1, 2, 4, 8):
        value = value + lax.ppermute(value, "col", [(i, i ^ mask) for i in range(16)])
    return value


def body(features, weight, out_bias, upstream, adj_tiles, tile_rows, tile_cols, tile_count):
    tiles, rows, cols = adj_tiles[0, 0], tile_rows[0, 0], tile_cols[0, 0]
    meta = jnp.stack([tile_count[0, 0], lax.axis_index("row"), lax.axis_index("col")])
    channels = features.shape[1]
    half = channels // 2

    pieces = gather_two(features)
    part = jax.ShapeDtypeStruct((8, LOCAL, TILE, channels), jnp.bfloat16)
    mine, other = tile_sums(
        forward_kernel, [part] * 2, (4, 4, LOCAL, TILE, channels), 9, meta, rows, cols, tiles, pieces
    )
    terms = scatter_z(mine.reshape(8, SHARD, channels), other.reshape(8, SHARD, channels))
    out_features, grad_pre, parts = middle(meta, *terms, weight, out_bias[None, :], upstream)

    pieces = gather_z(grad_pre)
    value = sum_pieces(parts)
    part = jax.ShapeDtypeStruct((4 * SHARD + PIECE, half), jnp.bfloat16)
    pieces = tile_sums(
        backward_kernel, [part] * 8, (16, SHARD, channels), 18, meta, rows, cols, tiles, pieces, (value,)
    )
    left = scatter_two(pieces[:4], shift_x, shift_y)
    right = scatter_two(pieces[4:], shift_y, shift_x)
    grad_features, grad_weight, grad_bias = last(meta, left, right, weight)
    return (out_features, grad_features, grad_weight.reshape(weight.shape), grad_bias[0])


def solution(mesh):
    return jax.shard_map(
        body,
        mesh=mesh,
        in_specs=(
            P(("col", "row"), None),
            P(),
            P(),
            P(("row", "col"), None),
            P("row", "col", None, None, None),
            P("row", "col", None),
            P("row", "col", None),
            P("row", "col"),
        ),
        out_specs=(P(("row", "col"), None), P(("col", "row"), None), P(), P()),
        check_vma=False,
    )
```

```python
import jax
import jax.numpy as jnp
from jax import lax
from jax.experimental import pallas as pl
from jax.experimental.pallas import tpu as pltpu
from jax.sharding import PartitionSpec as P

TILE = 128
UNROLL = 8
SHARD = 512
LOCAL = SHARD // TILE
PIECE = 32


def shift_x(value, step):
    return lax.ppermute(value, "row", [(i, (i + 4 * step) % 16) for i in range(16)])


def shift_y(value, step):
    return lax.ppermute(value, "row", [(i, i // 4 * 4 + (i + step) % 4) for i in range(16)])


def shift_z(value, step):
    return lax.ppermute(value, "col", [(i, (i + 2 * step) % 16) for i in range(16)])


def swap_core(value):
    return lax.ppermute(value, "col", [(i, i ^ 1) for i in range(16)])


def total(*values):
    result = values[0].astype(jnp.float32)
    for value in values[1:]:
        result = result + value.astype(jnp.float32)
    return result


def row_place(block, row, sign):
    owner, within = block >> 2, block & 3
    return (sign * ((owner >> 2) - (row >> 2))) & 3, (sign * (owner - row)) & 3, within


def col_place(block, col, sign):
    owner, within = block >> 2, block & 3
    return (owner ^ col) & 1, (sign * ((owner >> 1) - (col >> 1))) & 7, within


def sum_tiles(dims, meta_ref, source_ref, target_ref, tiles_ref, load, acc_ref, target_place):
    blocks = acc_ref.shape[0] - 1
    count = meta_ref[0]

    def add_group(group, carry):
        products, targets = [], []
        for member in range(UNROLL):
            slot = group * UNROLL + member
            products.append(
                lax.dot_general(
                    tiles_ref[slot], load(source_ref[slot]), (dims, ((), ())), preferred_element_type=jnp.float32
                )
            )
            targets.append(jnp.where(slot < count, target_place(target_ref[slot]), blocks))
        for product, target in zip(products, targets):
            acc_ref[target] += product
        return carry

    lax.fori_loop(0, (count + UNROLL - 1) // UNROLL, add_group, 0)


def clear(acc_ref):
    def one(block, carry):
        acc_ref[block] = jnp.zeros(acc_ref.shape[1:], jnp.float32)
        return carry

    lax.fori_loop(0, acc_ref.shape[0], one, 0)


def forward_kernel(meta_ref, rows_ref, cols_ref, tiles_any, *refs):
    pieces, (mine_ref, other_ref, tiles_ref, feats_ref, acc_ref, sems) = refs[:16], refs[16:]
    half = feats_ref.shape[4] // 2
    copies = [pltpu.make_async_copy(tiles_any, tiles_ref, sems.at[16])]
    for index, piece in enumerate(pieces):
        first, second = pl.ds(index % 2 * 2, 2), index // 2 % 4
        if index < 8:
            there = feats_ref.at[first, second, :, :, pl.ds(0, half)]
        else:
            there = feats_ref.at[second, first, :, :, pl.ds(half, half)]
        copies.append(pltpu.make_async_copy(piece, there, sems.at[index]))
    for copy in copies:
        copy.start()
    clear(acc_ref)
    for copy in copies:
        copy.wait()
    row, col = meta_ref[1], meta_ref[2]

    def load(block):
        x, y, within = row_place(block, row, -1)
        return feats_ref[x, y, within]

    def target(block):
        core, z, within = col_place(block, col, 1)
        return (core * 8 + z) * LOCAL + within

    sum_tiles(
        ((1,), (0,)), meta_ref, cols_ref, rows_ref, tiles_ref, load, acc_ref, target
    )

    def finish(step, carry):
        mine_ref[step >> 2, step & 3] = acc_ref[step].astype(jnp.bfloat16)
        other_ref[step >> 2, step & 3] = acc_ref[8 * LOCAL + step].astype(jnp.bfloat16)
        return carry

    lax.fori_loop(0, 8 * LOCAL, finish, 0)


def backward_kernel(meta_ref, rows_ref, cols_ref, tiles_any, *refs):
    pieces, value_ref, outs, (tiles_ref, feats_ref, acc_ref, sems) = refs[:11], refs[11], refs[12:26], refs[26:]
    own, p1, m1, p2, m2, p3, m3, far_a, far_b, near, rest = pieces
    middle = SHARD // 2
    sources = [(own, 0), (p1, 1), (m1, 7), (p2, 2), (m2, 6), (p3, 3), (m3, 5)]
    sources = [(ref, feats_ref.at[place]) for ref, place in sources]
    sources.append((far_a, feats_ref.at[4, pl.ds(0, middle)]))
    sources.append((far_b, feats_ref.at[4, pl.ds(middle, middle)]))
    sources += [(near.at[index], feats_ref.at[8 + place]) for index, place in enumerate((0, 1, 7, 2, 6))]
    sources += [(rest.at[index], feats_ref.at[8 + place]) for index, place in enumerate((3, 5, 4))]
    sources.append((tiles_any, tiles_ref))
    copies = [pltpu.make_async_copy(ref, there, sems.at[index]) for index, (ref, there) in enumerate(sources)]
    for copy in copies:
        copy.start()
    clear(acc_ref)
    for copy in copies:
        copy.wait()
    col = meta_ref[2]

    def load(block):
        core, z, within = col_place(block, col, -1)
        return feats_ref[core * 8 + z, pl.ds(pl.multiple_of(within * TILE, TILE), TILE), :]

    row = meta_ref[1]

    def place(block):
        x, y, within = row_place(block, row, 1)
        return (x * 4 + y) * LOCAL + within

    sum_tiles(
        ((0,), (0,)), meta_ref, rows_ref, cols_ref, tiles_ref, load, acc_ref, place
    )
    half = feats_ref.shape[2] // 2
    value = value_ref[...].astype(jnp.bfloat16)
    for side in range(2):
        keep, plus_a, plus_b, minus_a, minus_b, far_a, far_b = outs[side * 7 : side * 7 + 7]
        lanes = pl.ds(side * half, half)
        for step, low, high in ((0, keep, keep), (1, plus_a, plus_b), (2, far_a, far_b), (3, minus_a, minus_b)):
            for part, out in enumerate((low, high)):

                def finish(index, carry):
                    first, within = part * 2 + (index >> 2), index & 3
                    x, y = (first, step) if side == 0 else (step, first)
                    start = pl.multiple_of((index + (part * 2 * LOCAL if step == 0 else 0)) * TILE, TILE)
                    out[pl.ds(start, TILE), :] = acc_ref[(x * 4 + y) * LOCAL + within, :, lanes].astype(jnp.bfloat16)
                    return carry

                lax.fori_loop(0, 2 * LOCAL, finish, 0)
        for out in (plus_a, minus_b, far_a):
            out[pl.ds(2 * SHARD, PIECE), :] = value[:, side * half : side * half + half]


SMEM = pl.BlockSpec(memory_space=pltpu.SMEM)
VMEM = pl.BlockSpec(memory_space=pltpu.VMEM)
ANY = pl.BlockSpec(memory_space=pl.ANY)


def tile_sums(kernel, outs, scratch, copies, meta, rows, cols, tiles, pieces, more=()):
    channels = scratch[-1]
    blocks = 16 * LOCAL
    return pl.pallas_call(
        kernel,
        out_shape=outs,
        in_specs=[SMEM] * 3 + [ANY] * (1 + len(pieces)) + [VMEM] * len(more),
        out_specs=[VMEM] * len(outs),
        scratch_shapes=[
            pltpu.VMEM(tiles.shape, jnp.bfloat16),
            pltpu.VMEM(scratch, jnp.bfloat16),
            pltpu.VMEM((blocks + 1, TILE, channels), jnp.float32),
            pltpu.SemaphoreType.DMA((copies,)),
        ],
        compiler_params=pltpu.CompilerParams(vmem_limit_bytes=28 * 2**20),
        cost_estimate=pl.CostEstimate(
            flops=2 * tiles.shape[0] * TILE * TILE * channels, bytes_accessed=12 * 2**20, transcendentals=0
        ),
    )(meta, rows, cols, tiles, *pieces, *more)


def middle_kernel(meta_ref, mine_ref, other_ref, plus_ref, minus_ref, weight_ref, bias_ref, upstream_ref,
                  out_ref, grad_ref, parts_ref):
    gathered = total(mine_ref[0], other_ref[0], plus_ref[...], minus_ref[...]).astype(jnp.bfloat16)
    preact = jnp.dot(gathered, weight_ref[...], preferred_element_type=jnp.float32) + bias_ref[...]
    squashed = jax.nn.sigmoid(preact)
    out_ref[...] = (preact * squashed).astype(jnp.bfloat16)
    slope = squashed * (1.0 + preact * (1.0 - squashed))
    grad = (upstream_ref[...].astype(jnp.float32) * slope).astype(jnp.bfloat16)
    grad_ref[...] = grad
    weight_part = lax.dot_general(gathered, grad, (((0,), (0,)), ((), ())), preferred_element_type=jnp.float32)
    bias_part = jnp.sum(grad.astype(jnp.float32), axis=0, keepdims=True)
    first = lax.broadcasted_iota(jnp.int32, (PIECE - 16, bias_part.shape[1]), 0) == 0
    row = meta_ref[1]
    for owner in range(16):
        x, y = ((owner >> 2) - (row >> 2)) & 3, (owner - row) & 3
        parts_ref[x, y, :16] = weight_part[owner * 16 : owner * 16 + 16]
        parts_ref[x, y, 16:] = jnp.where(first, bias_part, 0.0) if owner == 0 else jnp.zeros(first.shape, jnp.float32)


def middle(meta, mine, other, plus, minus, weight, bias, upstream):
    channels = weight.shape[0]
    shard = pl.BlockSpec((1, SHARD, channels), lambda step: (0, 0, 0))
    return pl.pallas_call(
        middle_kernel,
        grid=(1,),
        out_shape=[
            jax.ShapeDtypeStruct(upstream.shape, jnp.bfloat16),
            jax.ShapeDtypeStruct(upstream.shape, jnp.bfloat16),
            jax.ShapeDtypeStruct((4, 4, PIECE, channels), jnp.float32),
        ],
        in_specs=[SMEM, shard, shard] + [VMEM] * 5,
        out_specs=[VMEM] * 3,
        compiler_params=pltpu.CompilerParams(vmem_limit_bytes=16 * 2**20),
    )(meta, mine, other, plus, minus, weight, bias, upstream)


def relay_kernel(own_ref, far_ref, out_ref):
    rows = 2 * SHARD
    out_ref[pl.ds(0, rows), :] = total(own_ref[pl.ds(0, rows), :], far_ref[pl.ds(0, rows), :]).astype(jnp.bfloat16)
    more = own_ref.shape[0] - rows
    if more:
        out_ref[pl.ds(rows, more), :] = own_ref[pl.ds(rows, more), :]
    if far_ref.shape[0] > rows:
        out_ref[pl.ds(rows + more, PIECE), :] = far_ref[pl.ds(rows, PIECE), :]


def relay(own, far):
    rows = own.shape[0] + far.shape[0] - 2 * SHARD
    return pl.pallas_call(
        relay_kernel, out_shape=jax.ShapeDtypeStruct((rows, own.shape[1]), jnp.bfloat16), in_specs=[VMEM] * 2, out_specs=VMEM,
        compiler_params=pltpu.CompilerParams(vmem_limit_bytes=16 * 2**20),
    )(own, far)


def split_kernel(value_ref, keep_ref, plus_a, plus_b, minus_a, minus_b, *outs):
    half = keep_ref.shape[1]
    rows = 2 * SHARD
    tails = (
        None, plus_a[pl.ds(rows, PIECE), :], plus_a[pl.ds(rows + PIECE, PIECE), :], minus_b[pl.ds(rows, PIECE), :]
    )
    for first, out_ref in enumerate(outs):
        plus, minus = (plus_a, minus_a) if first < 2 else (plus_b, minus_b)
        at = pl.ds(first % 2 * SHARD, SHARD)
        arrived = total(keep_ref[pl.ds(first * SHARD, SHARD), :], plus[at, :], minus[at, :])
        out_ref[pl.ds(0, SHARD), :] = arrived.astype(jnp.bfloat16)
        out_ref[pl.ds(SHARD, PIECE), :] = value_ref[...].astype(jnp.bfloat16)
        for index in (1, 2, 3):
            out_ref[pl.ds(SHARD + index * PIECE, PIECE), :] = tails[index]


def split(value, *arrived):
    shard = jax.ShapeDtypeStruct((SHARD + 4 * PIECE, value.shape[1]), jnp.bfloat16)
    return pl.pallas_call(
        split_kernel, out_shape=[shard] * 4, in_specs=[VMEM] * 6, out_specs=[VMEM] * 4,
        compiler_params=pltpu.CompilerParams(vmem_limit_bytes=16 * 2**20),
    )(value, *arrived)


def last_kernel(meta_ref, *refs):
    weight_ref, out_ref, grad_weight_ref, grad_bias_ref = refs[8:]
    row = meta_ref[1]
    half = refs[0].shape[1]
    result = None
    for side in range(2):
        arrived = refs[side * 4 : side * 4 + 4]
        lanes = slice(side * half, side * half + half)
        hidden = total(*[ref[pl.ds(0, SHARD), :] for ref in arrived]).astype(jnp.bfloat16)
        product = lax.dot_general(
            hidden, weight_ref[:, lanes], (((1,), (1,)), ((), ())), preferred_element_type=jnp.float32
        )
        result = product if result is None else result + product
        for first in range(4):
            for second in range(4):
                x, y = (first, second) if side == 0 else (second, first)
                x, y = ((row >> 2) - x) & 3, (row - y) & 3
                at = SHARD + second * PIECE
                piece = arrived[first][pl.ds(at, PIECE), :].astype(jnp.float32)
                grad_weight_ref[x * 4 + y, :, lanes] = piece[:16]

                @pl.when(x * 4 + y == 0)
                def _():
                    grad_bias_ref[:, lanes] = piece[16:17]

    out_ref[...] = result.astype(jnp.bfloat16)


def last(meta, left, right, weight):
    channels = weight.shape[0]
    return pl.pallas_call(
        last_kernel,
        out_shape=[
            jax.ShapeDtypeStruct((SHARD, channels), jnp.bfloat16),
            jax.ShapeDtypeStruct((16, 16, channels), jnp.float32),
            jax.ShapeDtypeStruct((1, channels), jnp.float32),
        ],
        in_specs=[SMEM] + [VMEM] * 9,
        out_specs=[VMEM] * 3,
        compiler_params=pltpu.CompilerParams(vmem_limit_bytes=16 * 2**20),
    )(meta, *left, *right, weight)


def gather_two(features):
    half = features.shape[1] // 2
    sides = []
    for value, shift in ((features[:, :half], shift_x), (features[:, half:], shift_y)):
        value = value.reshape(LOCAL, TILE, half)
        sides.append((value, shift(value, 1), shift(value, 3), shift(value, 2)))
    (l0, l1, l3, l2), (r0, r1, r3, r2) = lax.optimization_barrier(tuple(sides))
    results = []
    firsts = []
    for values, shift in (((l0, l1, l2, l3), shift_y), ((r0, r1, r2, r3), shift_x)):
        a, b = jnp.stack(values[:2]), jnp.stack(values[2:])
        firsts.append((a, b, shift(a, 1), shift(b, 3)))
    for (a, b, a1, b3), shift in zip(firsts, (shift_y, shift_x)):
        b1, a3 = shift(b, 1), shift(a, 3)
        a2, b2 = shift(a1, 1), shift(b3, 3)
        results += [a, b, a1, b1, a2, b2, a3, b3]
    return results


def scatter_two(sides, value):
    half = value.shape[1] // 2
    shifts = ((shift_x, shift_y), (shift_y, shift_x))
    far = [(second(side[5], 1), second(side[6], 3)) for side, (_, second) in zip(sides, shifts)]
    near = [(second(side[2], 1), second(side[3], 3)) for side, (_, second) in zip(sides, shifts)]
    results = []
    for index, (side, (first, second)) in enumerate(zip(sides, shifts)):
        keep, plus_a, _, _, minus_b, _, _ = side
        plus_b, minus_a = near[index]
        plus_a, minus_b = second(relay(plus_a, far[index][0]), 1), second(relay(minus_b, far[index][1]), 3)
        pieces = split(value[:, index * half : index * half + half], keep, plus_a, plus_b, minus_a, minus_b)
        results.append([pieces[0]] + [first(pieces[step], step) for step in (1, 2, 3)])
    return results


def scatter_z(mine, other):
    other = swap_core(other)
    mine, other = mine.reshape(8, SHARD, -1), other.reshape(8, SHARD, -1)
    middle = SHARD // 2
    far = total(mine[4], other[4]).astype(jnp.bfloat16)
    plus, minus = shift_z(far[:middle], 1), shift_z(far[middle:], -1)
    for step in (3, 2, 1):
        if step == 3:
            up = jnp.concatenate([total(mine[3, :middle], other[3, :middle], plus), total(mine[3, middle:], other[3, middle:])])
            down = jnp.concatenate([total(mine[5, :middle], other[5, :middle]), total(mine[5, middle:], other[5, middle:], minus)])
        else:
            up, down = total(mine[step], other[step], plus), total(mine[8 - step], other[8 - step], minus)
        plus, minus = shift_z(up.astype(jnp.bfloat16), 1), shift_z(down.astype(jnp.bfloat16), -1)
    return mine, other, plus, minus


def swap_col(value, mask):
    return lax.ppermute(value, "col", [(i, i ^ mask) for i in range(16)])


def gather_z(value, parts):
    middle = SHARD // 2
    tie = lax.optimization_barrier
    p1, m1 = shift_z(value, 1), shift_z(value, -1)
    sums = sum([shift_x(parts[step], step) for step in (1, 2, 3)], parts[0])
    p1, m1, sums = tie((p1, m1, sums))
    p2, m2 = shift_z(p1, 1), shift_z(m1, -1)
    sums = sum([shift_y(sums[step], step) for step in (1, 2, 3)], sums[0])
    p2, m2, sums = tie((p2, m2, sums))
    p3, m3 = shift_z(p2, 1), shift_z(m2, -1)
    sums = (sums + swap_col(sums, 2)) + (swap_col(sums, 4) + swap_col(sums, 6))
    p3, m3, sums = tie((p3, m3, sums))
    far_a, far_b = shift_z(p3[:middle], 1), shift_z(m3[middle:], -1)
    sums = (sums + swap_col(sums, 1)) + (swap_col(sums, 8) + swap_col(sums, 9))
    near = swap_core(jnp.stack([value, p1, m1, p2, m2]))
    far_a, far_b, sums = tie((far_a, far_b, sums))
    rest = swap_core(jnp.stack([p3, m3, jnp.concatenate([far_a, far_b])]))
    return (value, p1, m1, p2, m2, p3, m3, far_a, far_b, near, rest), sums


def body(features, weight, out_bias, upstream, adj_tiles, tile_rows, tile_cols, tile_count):
    tiles, rows, cols = adj_tiles[0, 0], tile_rows[0, 0], tile_cols[0, 0]
    meta = jnp.stack([tile_count[0, 0], lax.axis_index("row"), lax.axis_index("col")])
    channels = features.shape[1]
    half = channels // 2

    pieces = gather_two(features)
    part = jax.ShapeDtypeStruct((8, LOCAL, TILE, channels), jnp.bfloat16)
    mine, other = tile_sums(
        forward_kernel, [part] * 2, (4, 4, LOCAL, TILE, channels), 17, meta, rows, cols, tiles, pieces
    )
    terms = scatter_z(mine.reshape(8, SHARD, channels), other.reshape(8, SHARD, channels))
    out_features, grad_pre, parts = middle(meta, *terms, weight, out_bias[None, :], upstream)

    pieces, value = gather_z(grad_pre, parts)
    rows_of = (4 * SHARD, 2 * SHARD + PIECE, 2 * SHARD, 2 * SHARD, 2 * SHARD + PIECE, 2 * SHARD + PIECE, 2 * SHARD)
    outs = [jax.ShapeDtypeStruct((count, half), jnp.bfloat16) for count in rows_of * 2]
    pieces = tile_sums(
        backward_kernel, outs, (16, SHARD, channels), 18, meta, rows, cols, tiles, pieces, (value,)
    )
    left, right = scatter_two((pieces[:7], pieces[7:]), value)
    grad_features, grad_weight, grad_bias = last(meta, left, right, weight)
    return (out_features, grad_features, grad_weight.reshape(weight.shape), grad_bias[0])


def solution(mesh):
    return jax.shard_map(
        body,
        mesh=mesh,
        in_specs=(
            P(("col", "row"), None),
            P(),
            P(),
            P(("row", "col"), None),
            P("row", "col", None, None, None),
            P("row", "col", None),
            P("row", "col", None),
            P("row", "col"),
        ),
        out_specs=(P(("row", "col"), None), P(("col", "row"), None), P(), P()),
        check_vma=False,
    )
```

```python
import jax
import jax.numpy as jnp
from jax import lax
from jax.experimental import pallas as pl
from jax.experimental.pallas import tpu as pltpu
from jax.sharding import PartitionSpec as P

TILE = 128
UNROLL = 8
SHARD = 512
LOCAL = SHARD // TILE
HALF = 128
TAIL = HALF + 16
BF16, F32 = jnp.bfloat16, jnp.float32

SMEM = pl.BlockSpec(memory_space=pltpu.SMEM)
VMEM = pl.BlockSpec(memory_space=pltpu.VMEM)
ANY = pl.BlockSpec(memory_space=pl.ANY)


def ring(value, second, step):
    pairs = []
    for row in range(16):
        for col in range(16):
            x, y = row // 4, row % 4
            if col % 2 == second:
                x = (x + step) % 4
            else:
                y = (y + step) % 4
            pairs.append((row * 16 + col, (x * 4 + y) * 16 + col))
    return lax.ppermute(value, ("row", "col"), pairs)


def along_z(value):
    return lax.ppermute(value, "col", [(i, (i + (-2 if i % 2 else 2)) % 16) for i in range(16)])


def swap(value, mask=1):
    return lax.ppermute(value, "col", [(i, i ^ mask) for i in range(16)])


def total(*values):
    result = values[0].astype(F32)
    for value in values[1:]:
        result = result + value.astype(F32)
    return result


def row_place(block, meta_ref, sign):
    row, core = meta_ref[1], meta_ref[2] & 1
    owner, within = block >> 2, block & 3
    x, y = (sign * ((owner >> 2) - (row >> 2))) & 3, (sign * (owner - row)) & 3
    return jnp.where(core == 0, y * 4 + x, x * 4 + y), within


def col_steps(block, meta_ref, sign):
    col = meta_ref[2]
    owner, within = block >> 2, block & 3
    way = sign * (1 - 2 * (col & 1))
    return (way * ((owner >> 1) - (col >> 1))) & 7, (owner ^ col) & 1, within


def sum_tiles(dims, meta_ref, source_ref, target_ref, tiles_ref, load, acc_ref, place):
    blocks = acc_ref.shape[0] - 1
    count = meta_ref[0]

    def add_group(group, carry):
        products, targets = [], []
        for member in range(UNROLL):
            slot = group * UNROLL + member
            products.append(
                lax.dot_general(tiles_ref[slot], load(source_ref[slot]), (dims, ((), ())), preferred_element_type=F32)
            )
            targets.append(jnp.where(slot < count, place(target_ref[slot]), blocks))
        for product, target in zip(products, targets):
            acc_ref[target] += product
        return carry

    lax.fori_loop(0, (count + UNROLL - 1) // UNROLL, add_group, 0)


def fill(pairs, sems, acc_ref):
    copies = [pltpu.make_async_copy(source, there, sems.at[index]) for index, (source, there) in enumerate(pairs)]
    for copy in copies:
        copy.start()

    def clear(block, carry):
        acc_ref[block] = jnp.zeros(acc_ref.shape[1:], F32)
        return carry

    lax.fori_loop(0, acc_ref.shape[0], clear, 0)
    for copy in copies:
        copy.wait()


def forward_kernel(meta_ref, rows_ref, cols_ref, tiles_any, *refs):
    pieces, (mine_ref, other_ref, tiles_ref, feats_ref, acc_ref, sems) = refs[:8], refs[8:]
    pairs = [(ref, feats_ref.at[pl.ds(index * 2, 2)]) for index, ref in enumerate(pieces)]
    fill(pairs + [(tiles_any, tiles_ref)], sems, acc_ref)

    def load(block):
        owner, within = row_place(block, meta_ref, -1)
        return feats_ref[owner, pl.ds(pl.multiple_of(within * TILE, TILE), TILE), :]

    def place(block):
        steps, other, within = col_steps(block, meta_ref, 1)
        flip = jnp.where((steps > 4) | (((steps & 3) == 0) & (other == 1)), 1, 0)
        steps, other = jnp.where(flip == 1, (8 - steps) & 7, steps), other ^ flip
        return (flip * 8 + jnp.maximum(2 * steps - 1, 0) + other) * LOCAL + within

    sum_tiles(((1,), (0,)), meta_ref, cols_ref, rows_ref, tiles_ref, load, acc_ref, place)

    def finish(step, carry):
        at = pl.ds(pl.multiple_of((step & 3) * TILE, TILE), TILE)
        mine_ref[step >> 2, at, :] = acc_ref[step].astype(BF16)
        other_ref[step >> 2, at, :] = acc_ref[8 * LOCAL + step].astype(BF16)
        return carry

    lax.fori_loop(0, 8 * LOCAL, finish, 0)


def backward_kernel(meta_ref, rows_ref, cols_ref, tiles_any, *refs):
    (m0, m1, m2, m3, m4, s1, s2, s3, s4), tail_ref = refs[:9], refs[9]
    (keep, plus_a, plus_b, minus_a, minus_b, far_a, far_b), refs = refs[10:17], refs[17:]
    tiles_ref, feats_ref, acc_ref, sems = refs
    pairs = [(ref, feats_ref.at[steps]) for steps, ref in enumerate((m0, m1, m2, m3))]
    pairs += [(m4, feats_ref.at[4, 0]), (s4, feats_ref.at[4, 1])]
    for steps, ref in ((7, s1), (6, s2), (5, s3)):
        pairs += [(ref.at[0], feats_ref.at[steps, 1]), (ref.at[1], feats_ref.at[steps, 0])]
    fill(pairs + [(tiles_any, tiles_ref)], sems, acc_ref)

    def load(block):
        steps, other, within = col_steps(block, meta_ref, -1)
        return feats_ref[steps, other, pl.ds(pl.multiple_of(within * TILE, TILE), TILE), :]

    def place(block):
        owner, within = row_place(block, meta_ref, 1)
        return owner * LOCAL + within

    sum_tiles(((0,), (0,)), meta_ref, rows_ref, cols_ref, tiles_ref, load, acc_ref, place)
    for out, first_block, blocks in (
        (far_a, 32, 8), (far_b, 40, 8), (plus_b, 24, 8), (minus_a, 48, 8), (plus_a, 16, 8), (minus_b, 56, 8), (keep, 0, 16),
    ):

        def finish(index, carry):
            out[pl.ds(pl.multiple_of(index * TILE, TILE), TILE), :] = acc_ref[first_block + index].astype(BF16)
            return carry

        lax.fori_loop(0, blocks, finish, 0)
    for out in (far_a, plus_a, minus_b):
        out[pl.ds(2 * SHARD, TAIL), :] = tail_ref[...]


def tile_sums(kernel, outs, scratch, copies, meta, rows, cols, tiles, pieces, more=()):
    channels = scratch[-1]
    blocks = 16 * LOCAL
    return pl.pallas_call(
        kernel,
        out_shape=outs,
        in_specs=[SMEM] * 3 + [ANY] * (1 + len(pieces)) + [VMEM] * len(more),
        out_specs=[VMEM] * len(outs),
        scratch_shapes=[
            pltpu.VMEM(tiles.shape, BF16),
            pltpu.VMEM(scratch, BF16),
            pltpu.VMEM((blocks + 1, TILE, channels), F32),
            pltpu.SemaphoreType.DMA((copies,)),
        ],
        compiler_params=pltpu.CompilerParams(vmem_limit_bytes=28 * 2**20),
        cost_estimate=pl.CostEstimate(
            flops=2 * tiles.shape[0] * TILE * TILE * channels, bytes_accessed=12 * 2**20, transcendentals=0
        ),
    )(meta, rows, cols, tiles, *pieces, *more)


def small_call(kernel, outs, *args, **more):
    return pl.pallas_call(
        kernel, out_shape=outs, in_specs=[VMEM] * len(args), out_specs=[VMEM] * len(outs),
        compiler_params=pltpu.CompilerParams(vmem_limit_bytes=16 * 2**20), **more,
    )(*args)


def middle_kernel(meta_ref, mine_ref, other_ref, same_ref, swapped_ref, weight_ref, bias_ref, upstream_ref,
                  out_ref, message_ref, tail_ref):
    gathered = total(mine_ref[0], other_ref[0], same_ref[0], swapped_ref[0]).astype(BF16)
    preact = jnp.dot(gathered, weight_ref[...], preferred_element_type=F32) + bias_ref[...]
    squashed = jax.nn.sigmoid(preact)
    out_ref[...] = (preact * squashed).astype(BF16)
    slope = squashed * (1.0 + preact * (1.0 - squashed))
    grad = (upstream_ref[...].astype(F32) * slope).astype(BF16)
    message_ref[pl.ds(0, SHARD), :] = grad
    weight_part = lax.dot_general(gathered, grad, (((0,), (0,)), ((), ())), preferred_element_type=F32)
    bias_part = jnp.sum(grad.astype(F32), axis=0, keepdims=True)
    first = lax.broadcasted_iota(jnp.int32, (TAIL - HALF, bias_part.shape[1]), 0) == 0
    bias_part = jnp.where(first, bias_part, 0.0)
    lower = (meta_ref[2] & 1) == 0
    tail_ref[pl.ds(0, HALF), :] = jnp.where(lower, weight_part[:HALF], weight_part[HALF:])
    tail_ref[pl.ds(HALF, TAIL - HALF), :] = bias_part
    message_ref[pl.ds(SHARD, HALF), :] = jnp.where(lower, weight_part[HALF:], weight_part[:HALF]).astype(BF16)
    message_ref[pl.ds(SHARD + HALF, TAIL - HALF), :] = bias_part.astype(BF16)


def middle(meta, mine, other, arrived, swapped, weight, bias, upstream):
    channels = weight.shape[0]

    def one(index):
        return pl.BlockSpec((1, SHARD, channels), lambda step: (index, 0, 0))

    return pl.pallas_call(
        middle_kernel,
        grid=(1,),
        out_shape=[
            jax.ShapeDtypeStruct(upstream.shape, BF16),
            jax.ShapeDtypeStruct((SHARD + TAIL, channels), BF16),
            jax.ShapeDtypeStruct((TAIL, channels), F32),
        ],
        in_specs=[SMEM, one(0), one(0), one(0), one(1)] + [VMEM] * 3,
        out_specs=[VMEM] * 3,
        compiler_params=pltpu.CompilerParams(vmem_limit_bytes=16 * 2**20),
    )(meta, mine, other, arrived, swapped, weight, bias, upstream)


def relay_kernel(own_ref, far_ref, out_ref):
    rows = 2 * SHARD
    out_ref[pl.ds(0, rows), :] = total(own_ref[pl.ds(0, rows), :], far_ref[pl.ds(0, rows), :]).astype(BF16)
    at = rows
    for ref in (own_ref, far_ref):
        if ref.shape[0] > rows:
            out_ref[pl.ds(at, TAIL), :] = ref[pl.ds(rows, TAIL), :]
            at += TAIL


def relay(own, far):
    rows = own.shape[0] + far.shape[0] - 2 * SHARD
    return small_call(relay_kernel, [jax.ShapeDtypeStruct((rows, own.shape[1]), BF16)], own, far)[0]


def four(own, plus, far, minus):
    return total(own, far) + total(plus, minus)


def split_kernel(tail_ref, keep_ref, plus_a, plus_b, minus_a, minus_b, *outs):
    rows = 2 * SHARD
    tail = four(
        tail_ref[...], plus_a[pl.ds(rows, TAIL), :], plus_a[pl.ds(rows + TAIL, TAIL), :], minus_b[pl.ds(rows, TAIL), :]
    ).astype(BF16)
    for first, out_ref in enumerate(outs):
        plus, minus = (plus_a, minus_a) if first < 2 else (plus_b, minus_b)
        at = pl.ds(first % 2 * SHARD, SHARD)
        arrived = total(keep_ref[pl.ds(first * SHARD, SHARD), :], plus[at, :], minus[at, :])
        out_ref[pl.ds(0, SHARD), :] = arrived.astype(BF16)
        out_ref[pl.ds(SHARD, TAIL), :] = tail


def last_tail_kernel(own_ref, plus_ref, far_ref, minus_ref, out_ref):
    out_ref[...] = four(*[ref[pl.ds(SHARD, TAIL), :] for ref in (own_ref, plus_ref, far_ref, minus_ref)])


def last_kernel(own_ref, plus_ref, far_ref, minus_ref, weight_ref, out_ref):
    hidden = total(*[ref[pl.ds(0, SHARD), :] for ref in (own_ref, plus_ref, far_ref, minus_ref)]).astype(BF16)
    out_ref[...] = lax.dot_general(
        hidden, weight_ref[...], (((1,), (1,)), ((), ())), preferred_element_type=F32
    ).astype(BF16)


def gather_rows(value):
    one, three, two = ring(value, 0, 1), ring(value, 0, 3), ring(value, 0, 2)
    a, b = jnp.stack([value, one]), jnp.stack([two, three])
    a1, b3 = ring(a, 1, 1), ring(b, 1, 3)
    b1, a3 = ring(b, 1, 1), ring(a, 1, 3)
    a2, b2 = ring(a1, 1, 1), ring(b3, 1, 3)
    return a, b, a1, b1, a2, b2, a3, b3


def scatter_rows(pieces, tail):
    keep, plus_a, plus_b, minus_a, minus_b, far_a, far_b = pieces
    far_a, far_b = ring(far_a, 1, 1), ring(far_b, 1, 3)
    plus_b, minus_a = ring(plus_b, 1, 1), ring(minus_a, 1, 3)
    plus_a, minus_b = ring(relay(plus_a, far_a), 1, 1), ring(relay(minus_b, far_b), 1, 3)
    shard = jax.ShapeDtypeStruct((SHARD + TAIL, tail.shape[1]), BF16)
    pieces = small_call(split_kernel, [shard] * 4, tail, keep, plus_a, plus_b, minus_a, minus_b)
    return [pieces[0]] + [ring(pieces[step], 0, step) for step in (1, 2, 3)]


def scatter_cols(mine, other):
    other = swap(other)
    arrived = along_z(total(mine[7], other[7]).astype(BF16))
    arrived = along_z(jnp.stack([total(mine[5], other[5], arrived), total(mine[6], other[6])]).astype(BF16))
    arrived = along_z(total(mine[3:5], other[3:5], arrived).astype(BF16))
    arrived = along_z(total(mine[1:3], other[1:3], arrived).astype(BF16))
    return mine, other, arrived, swap(arrived)


def gather_cols(message, tail):
    tie = lax.optimization_barrier
    swapped = swap(message)
    m0 = jnp.stack([message[:SHARD], swapped[:SHARD]])
    tail = total(tail, swapped[SHARD:]).astype(BF16)
    m1 = along_z(m0)
    tail = total(tail, swap(tail, 2)).astype(BF16)
    m1, tail = tie((m1, tail))
    m2, s1 = along_z(m1), swap(m1)
    tail = total(tail, swap(tail, 4)).astype(BF16)
    m2, tail = tie((m2, tail))
    m3, s2 = along_z(m2), swap(m2)
    tail = total(tail, swap(tail, 8)).astype(BF16)
    m3, tail = tie((m3, tail))
    m4, s3 = along_z(m3[0]), swap(m3)
    s4 = swap(m4)
    return (m0, m1, m2, m3, m4, s1, s2, s3, s4), tail


def body(features, weight, out_bias, upstream, adj_tiles, tile_rows, tile_cols, tile_count):
    tiles, rows, cols = adj_tiles[0, 0], tile_rows[0, 0], tile_cols[0, 0]
    meta = jnp.stack([tile_count[0, 0], lax.axis_index("row"), lax.axis_index("col")])
    channels = features.shape[1]

    part = jax.ShapeDtypeStruct((8, SHARD, channels), BF16)
    mine, other = tile_sums(
        forward_kernel, [part] * 2, (16, SHARD, channels), 9, meta, rows, cols, tiles, gather_rows(features)
    )
    terms = scatter_cols(mine, other)
    out_features, message, tail = middle(meta, *terms, weight, out_bias[None, :], upstream)

    pieces, tail = gather_cols(message, tail)
    two = 2 * SHARD
    outs = [
        jax.ShapeDtypeStruct((count, channels), BF16)
        for count in (2 * two, two + TAIL, two, two, two + TAIL, two + TAIL, two)
    ]
    pieces = tile_sums(
        backward_kernel, outs, (8, 2, SHARD, channels), 13, meta, rows, cols, tiles, pieces, (tail,)
    )
    terms = scatter_rows(pieces, tail)
    [tail] = small_call(last_tail_kernel, [jax.ShapeDtypeStruct((TAIL, channels), F32)], *terms)
    swapped = swap(tail)
    [grad_features] = small_call(last_kernel, [jax.ShapeDtypeStruct(features.shape, BF16)], *terms, weight)
    lower = (lax.axis_index("col") & 1) == 0
    first, second = jnp.where(lower, tail, swapped), jnp.where(lower, swapped[:HALF], tail[:HALF])
    return (out_features, grad_features, jnp.concatenate([first[:HALF], second]), first[HALF])


def solution(mesh):
    return jax.shard_map(
        body,
        mesh=mesh,
        in_specs=(
            P(("col", "row"), None),
            P(),
            P(),
            P(("row", "col"), None),
            P("row", "col", None, None, None),
            P("row", "col", None),
            P("row", "col", None),
            P("row", "col"),
        ),
        out_specs=(P(("row", "col"), None), P(("col", "row"), None), P(), P()),
        check_vma=False,
    )
```

```python
import jax
import jax.numpy as jnp
from jax import lax
from jax.experimental import pallas as pl
from jax.experimental.pallas import tpu as pltpu
from jax.sharding import PartitionSpec as P

TILE = 128
UNROLL = 8
SHARD = 512
LOCAL = SHARD // TILE
HALF = 128
TAIL = HALF + 16
BF16, F32 = jnp.bfloat16, jnp.float32

SMEM = pl.BlockSpec(memory_space=pltpu.SMEM)
VMEM = pl.BlockSpec(memory_space=pltpu.VMEM)
ANY = pl.BlockSpec(memory_space=pl.ANY)


def ring(value, second, step):
    pairs = []
    for row in range(16):
        for col in range(16):
            x, y = row // 4, row % 4
            if col % 2 == second:
                x = (x + step) % 4
            else:
                y = (y + step) % 4
            pairs.append((row * 16 + col, (x * 4 + y) * 16 + col))
    return lax.ppermute(value, ("row", "col"), pairs)


def along_z(value):
    return lax.ppermute(value, "col", [(i, (i + (-2 if i % 2 else 2)) % 16) for i in range(16)])


def along_z_across(value, own):
    pairs = []
    for i in range(16):
        core = i % 2 if own else 1 - i % 2
        pairs.append((i, ((i + (-2 if core else 2)) % 16) ^ 1))
    return lax.ppermute(value, "col", pairs)


def swap(value, mask=1):
    return lax.ppermute(value, "col", [(i, i ^ mask) for i in range(16)])


def total(*values):
    result = values[0].astype(F32)
    for value in values[1:]:
        result = result + value.astype(F32)
    return result


def row_place(block, meta_ref, sign):
    row, core = meta_ref[1], meta_ref[2] & 1
    owner, within = block >> 2, block & 3
    x, y = (sign * ((owner >> 2) - (row >> 2))) & 3, (sign * (owner - row)) & 3
    return jnp.where(core == 0, y * 4 + x, x * 4 + y), within


def col_steps(block, meta_ref, sign):
    col = meta_ref[2]
    owner, within = block >> 2, block & 3
    way = sign * (1 - 2 * (col & 1))
    return (way * ((owner >> 1) - (col >> 1))) & 7, (owner ^ col) & 1, within


def sum_tiles(dims, meta_ref, source_ref, target_ref, tiles_ref, load, acc_ref, place):
    blocks = acc_ref.shape[0] - 1
    count = meta_ref[0]

    def add_group(group, carry):
        products, targets = [], []
        for member in range(UNROLL):
            slot = group * UNROLL + member
            products.append(
                lax.dot_general(tiles_ref[slot], load(source_ref[slot]), (dims, ((), ())), preferred_element_type=F32)
            )
            targets.append(jnp.where(slot < count, place(target_ref[slot]), blocks))
        for product, target in zip(products, targets):
            acc_ref[target] += product
        return carry

    lax.fori_loop(0, (count + UNROLL - 1) // UNROLL, add_group, 0)


def fill(pairs, sems, acc_ref):
    copies = [pltpu.make_async_copy(source, there, sems.at[index]) for index, (source, there) in enumerate(pairs)]
    for copy in copies:
        copy.start()

    def clear(block, carry):
        acc_ref[block] = jnp.zeros(acc_ref.shape[1:], F32)
        return carry

    lax.fori_loop(0, acc_ref.shape[0], clear, 0)
    for copy in copies:
        copy.wait()


def forward_kernel(meta_ref, rows_ref, cols_ref, tiles_ref, *refs):
    pieces, (mine_ref, other_ref, far_ref, far_other_ref, feats_ref, acc_ref, sems) = refs[:8], refs[8:]
    fill([(ref, feats_ref.at[pl.ds(index * 2, 2)]) for index, ref in enumerate(pieces)], sems, acc_ref)

    def load(block):
        owner, within = row_place(block, meta_ref, -1)
        return feats_ref[owner, pl.ds(pl.multiple_of(within * TILE, TILE), TILE), :]

    def place(block):
        steps, other, within = col_steps(block, meta_ref, 1)
        flip = jnp.where((steps > 4) | ((steps == 0) & (other == 1)), 1, 0)
        near, side = jnp.where(flip == 1, (8 - steps) & 7, steps), other ^ flip
        near = flip * 7 + jnp.maximum(2 * near - 1, 0) + side
        return jnp.where(steps == 4, 14 + other, near) * LOCAL + within

    sum_tiles(((1,), (0,)), meta_ref, cols_ref, rows_ref, tiles_ref, load, acc_ref, place)

    def finish(step, carry):
        at = pl.ds(pl.multiple_of((step & 3) * TILE, TILE), TILE)
        mine_ref[step >> 2, at, :] = acc_ref[step].astype(BF16)
        other_ref[step >> 2, at, :] = acc_ref[7 * LOCAL + step].astype(BF16)
        return carry

    lax.fori_loop(0, 7 * LOCAL, finish, 0)
    for within in range(LOCAL):
        at = pl.ds(within * TILE, TILE)
        far_ref[at, :] = acc_ref[14 * LOCAL + within].astype(BF16)
        far_other_ref[at, :] = acc_ref[15 * LOCAL + within].astype(BF16)


def backward_kernel(meta_ref, rows_ref, cols_ref, tiles_ref, *refs):
    pieces, near, tail_ref = refs[:10], refs[10], refs[11]
    (keep, plus_a, plus_b, minus_a, minus_b, far_a, far_b), (feats_ref, acc_ref, sems) = refs[12:19], refs[19:]
    pairs = [(ref, feats_ref.at[index // 2, index % 2]) for index, ref in enumerate(pieces)]
    pairs += [(near.at[index], feats_ref.at[7 - index // 2, 1 - index % 2]) for index in range(6)]
    fill(pairs, sems, acc_ref)

    def load(block):
        steps, other, within = col_steps(block, meta_ref, -1)
        return feats_ref[steps, other, pl.ds(pl.multiple_of(within * TILE, TILE), TILE), :]

    def place(block):
        owner, within = row_place(block, meta_ref, 1)
        return owner * LOCAL + within

    sum_tiles(((0,), (0,)), meta_ref, rows_ref, cols_ref, tiles_ref, load, acc_ref, place)
    for out, first_block, blocks in (
        (far_a, 32, 8), (far_b, 40, 8), (plus_b, 24, 8), (minus_a, 48, 8), (plus_a, 16, 8), (minus_b, 56, 8), (keep, 0, 16),
    ):

        def finish(index, carry):
            out[pl.ds(pl.multiple_of(index * TILE, TILE), TILE), :] = acc_ref[first_block + index].astype(BF16)
            return carry

        lax.fori_loop(0, blocks, finish, 0)
    for out in (far_a, plus_a, minus_b):
        out[pl.ds(2 * SHARD, TAIL), :] = tail_ref[...]


def tile_sums(kernel, outs, scratch, copies, meta, rows, cols, tiles, pieces, more=()):
    channels = scratch[-1]
    blocks = 16 * LOCAL
    return pl.pallas_call(
        kernel,
        out_shape=outs,
        in_specs=[SMEM] * 3 + [VMEM] + [ANY] * len(pieces) + [VMEM] * len(more),
        out_specs=[VMEM] * len(outs),
        scratch_shapes=[
            pltpu.VMEM(scratch, BF16),
            pltpu.VMEM((blocks + 1, TILE, channels), F32),
            pltpu.SemaphoreType.DMA((copies,)),
        ],
        compiler_params=pltpu.CompilerParams(vmem_limit_bytes=28 * 2**20),
        cost_estimate=pl.CostEstimate(
            flops=2 * tiles.shape[0] * TILE * TILE * channels, bytes_accessed=12 * 2**20, transcendentals=0
        ),
    )(meta, rows, cols, tiles, *pieces, *more)


def small_call(kernel, outs, *args, **more):
    return pl.pallas_call(
        kernel, out_shape=outs, in_specs=[VMEM] * len(args), out_specs=[VMEM] * len(outs),
        compiler_params=pltpu.CompilerParams(vmem_limit_bytes=16 * 2**20), **more,
    )(*args)


def middle_kernel(meta_ref, same_ref, cross_ref, weight_ref, bias_ref, upstream_ref,
                  out_ref, grad_ref, tail_ref, message_ref):
    gathered = total(same_ref[...], cross_ref[...]).astype(BF16)
    preact = jnp.dot(gathered, weight_ref[...], preferred_element_type=F32) + bias_ref[...]
    squashed = jax.nn.sigmoid(preact)
    out_ref[...] = (preact * squashed).astype(BF16)
    slope = squashed * (1.0 + preact * (1.0 - squashed))
    grad = (upstream_ref[...].astype(F32) * slope).astype(BF16)
    grad_ref[...] = grad
    weight_part = lax.dot_general(gathered, grad, (((0,), (0,)), ((), ())), preferred_element_type=F32)
    bias_part = jnp.sum(grad.astype(F32), axis=0, keepdims=True)
    first = lax.broadcasted_iota(jnp.int32, (TAIL - HALF, bias_part.shape[1]), 0) == 0
    bias_part = jnp.where(first, bias_part, 0.0)
    lower = (meta_ref[2] & 1) == 0
    tail_ref[pl.ds(0, HALF), :] = jnp.where(lower, weight_part[:HALF], weight_part[HALF:])
    tail_ref[pl.ds(HALF, TAIL - HALF), :] = bias_part
    message_ref[pl.ds(0, HALF), :] = jnp.where(lower, weight_part[HALF:], weight_part[:HALF]).astype(BF16)
    message_ref[pl.ds(HALF, TAIL - HALF), :] = bias_part.astype(BF16)


def middle(meta, same, cross, weight, bias, upstream):
    channels = weight.shape[0]

    return pl.pallas_call(
        middle_kernel,
        out_shape=[
            jax.ShapeDtypeStruct(upstream.shape, BF16),
            jax.ShapeDtypeStruct(upstream.shape, BF16),
            jax.ShapeDtypeStruct((TAIL, channels), F32),
            jax.ShapeDtypeStruct((TAIL, channels), BF16),
        ],
        in_specs=[SMEM] + [VMEM] * 5,
        out_specs=[VMEM] * 4,
        compiler_params=pltpu.CompilerParams(vmem_limit_bytes=16 * 2**20),
    )(meta, same, cross, weight, bias, upstream)


def relay_kernel(own_ref, far_ref, out_ref):
    rows = 2 * SHARD
    out_ref[pl.ds(0, rows), :] = total(own_ref[pl.ds(0, rows), :], far_ref[pl.ds(0, rows), :]).astype(BF16)
    at = rows
    for ref in (own_ref, far_ref):
        if ref.shape[0] > rows:
            out_ref[pl.ds(at, TAIL), :] = ref[pl.ds(rows, TAIL), :]
            at += TAIL


def relay(own, far):
    rows = own.shape[0] + far.shape[0] - 2 * SHARD
    return small_call(relay_kernel, [jax.ShapeDtypeStruct((rows, own.shape[1]), BF16)], own, far)[0]


def four(own, plus, far, minus):
    return total(own, far) + total(plus, minus)


def near_kernel(keep_ref, plus_b, minus_a, out_ref):
    rows = 2 * SHARD
    out_ref[pl.ds(0, rows), :] = total(keep_ref[pl.ds(0, rows), :], minus_a[...])
    out_ref[pl.ds(rows, rows), :] = total(keep_ref[pl.ds(rows, rows), :], plus_b[...])


def split_kernel(tail_ref, near_ref, plus_a, minus_b, *outs):
    rows = 2 * SHARD
    tail = four(
        tail_ref[...], plus_a[pl.ds(rows, TAIL), :], plus_a[pl.ds(rows + TAIL, TAIL), :], minus_b[pl.ds(rows, TAIL), :]
    ).astype(BF16)
    for first, out_ref in enumerate(outs):
        ref = plus_a if first < 2 else minus_b
        arrived = total(near_ref[pl.ds(first * SHARD, SHARD), :], ref[pl.ds(first % 2 * SHARD, SHARD), :])
        out_ref[pl.ds(0, SHARD), :] = arrived.astype(BF16)
        out_ref[pl.ds(SHARD, TAIL), :] = tail


def last_tail_kernel(own_ref, plus_ref, far_ref, minus_ref, out_ref):
    out_ref[...] = four(*[ref[pl.ds(SHARD, TAIL), :] for ref in (own_ref, plus_ref, far_ref, minus_ref)])


def last_kernel(own_ref, plus_ref, far_ref, minus_ref, weight_ref, out_ref):
    hidden = total(*[ref[pl.ds(0, SHARD), :] for ref in (own_ref, plus_ref, far_ref, minus_ref)]).astype(BF16)
    out_ref[...] = lax.dot_general(
        hidden, weight_ref[...], (((1,), (1,)), ((), ())), preferred_element_type=F32
    ).astype(BF16)


def gather_rows(value):
    one, three, two = ring(value, 0, 1), ring(value, 0, 3), ring(value, 0, 2)
    a, b = jnp.stack([value, one]), jnp.stack([two, three])
    a1, b3 = ring(a, 1, 1), ring(b, 1, 3)
    b1, a3 = ring(b, 1, 1), ring(a, 1, 3)
    a2, b2 = ring(a1, 1, 1), ring(b3, 1, 3)
    return a, b, a1, b1, a2, b2, a3, b3


def scatter_rows(pieces, tail):
    keep, plus_a, plus_b, minus_a, minus_b, far_a, far_b = pieces
    far_a, far_b = ring(far_a, 1, 1), ring(far_b, 1, 3)
    plus_b, minus_a = ring(plus_b, 1, 1), ring(minus_a, 1, 3)
    plus_a, minus_b = ring(relay(plus_a, far_a), 1, 1), ring(relay(minus_b, far_b), 1, 3)
    shard = jax.ShapeDtypeStruct((SHARD + TAIL, tail.shape[1]), BF16)
    [near] = small_call(near_kernel, [jax.ShapeDtypeStruct(keep.shape, F32)], keep, plus_b, minus_a)
    pieces = small_call(split_kernel, [shard] * 4, tail, near, plus_a, minus_b)
    return [pieces[0]] + [ring(pieces[step], 0, step) for step in (1, 2, 3)]


def add_kernel(mine_ref, other_ref, arrived_ref, out_ref):
    out_ref[...] = total(mine_ref[0], other_ref[0], arrived_ref[...]).astype(BF16)


def add(index, mine, other, arrived):
    shard = pl.BlockSpec((1, *arrived.shape), lambda step: (index, 0, 0))
    return pl.pallas_call(
        add_kernel, grid=(1,), out_shape=jax.ShapeDtypeStruct(arrived.shape, BF16), in_specs=[shard, shard, VMEM],
        out_specs=VMEM, compiler_params=pltpu.CompilerParams(vmem_limit_bytes=16 * 2**20),
    )(mine, other, arrived)


def scatter_cols(mine, other, far, far_other):
    same, cross = along_z(far), along_z(far_other)
    other = swap(other)
    for steps in (3, 2, 1):
        same = along_z(add(2 * steps - 1, mine, other, same))
        cross = add(2 * steps, mine, other, cross)
        cross = along_z(cross) if steps > 1 else along_z_across(cross, True)
    return add(0, mine, other, same), cross


def gather_cols(value, tail, message):
    tie = lax.optimization_barrier
    pieces = [value, swap(value)]
    same, cross = value, value
    for mask in (1, 8, 4, 2):
        same, cross = along_z(same), along_z_across(cross, False) if mask == 1 else along_z(cross)
        tail = total(tail, swap(message if mask == 1 else tail, mask)).astype(BF16)
        if mask != 2:
            cross, tail = tie((cross, tail))
        pieces += [same, cross]
    return pieces + [swap(jnp.stack(pieces[2:8]))], tail


def body(features, weight, out_bias, upstream, adj_tiles, tile_rows, tile_cols, tile_count):
    tiles, rows, cols = adj_tiles[0, 0], tile_rows[0, 0], tile_cols[0, 0]
    meta = jnp.stack([tile_count[0, 0], lax.axis_index("row"), lax.axis_index("col")])
    channels = features.shape[1]

    part, shard = [jax.ShapeDtypeStruct(shape, BF16) for shape in ((7, SHARD, channels), (SHARD, channels))]
    terms = tile_sums(
        forward_kernel, [part, part, shard, shard], (16, SHARD, channels), 8, meta, rows, cols, tiles,
        gather_rows(features),
    )
    terms = scatter_cols(*terms)
    out_features, grad_pre, tail, message = middle(meta, *terms, weight, out_bias[None, :], upstream)

    pieces, tail = gather_cols(grad_pre, tail, message)
    two = 2 * SHARD
    outs = [
        jax.ShapeDtypeStruct((count, channels), BF16)
        for count in (2 * two, two + TAIL, two, two, two + TAIL, two + TAIL, two)
    ]
    pieces = tile_sums(
        backward_kernel, outs, (8, 2, SHARD, channels), 16, meta, rows, cols, tiles, pieces, (tail,)
    )
    terms = scatter_rows(pieces, tail)
    [tail] = small_call(last_tail_kernel, [jax.ShapeDtypeStruct((TAIL, channels), F32)], *terms)
    swapped = swap(tail)
    [grad_features] = small_call(last_kernel, [jax.ShapeDtypeStruct(features.shape, BF16)], *terms, weight)
    lower = (lax.axis_index("col") & 1) == 0
    first, second = jnp.where(lower, tail, swapped), jnp.where(lower, swapped[:HALF], tail[:HALF])
    return (out_features, grad_features, jnp.concatenate([first[:HALF], second]), first[HALF])


def solution(mesh):
    return jax.shard_map(
        body,
        mesh=mesh,
        in_specs=(
            P(("col", "row"), None),
            P(),
            P(),
            P(("row", "col"), None),
            P("row", "col", None, None, None),
            P("row", "col", None),
            P("row", "col", None),
            P("row", "col"),
        ),
        out_specs=(P(("row", "col"), None), P(("col", "row"), None), P(), P()),
        check_vma=False,
    )
```

```python
import jax
import jax.numpy as jnp
from jax import lax
from jax.experimental import pallas as pl
from jax.experimental.pallas import tpu as pltpu
from jax.sharding import PartitionSpec as P

TILE = 128
UNROLL = 8
SHARD = 512
LOCAL = SHARD // TILE
HALF = 128
TAIL = HALF + 16
BF16, F32 = jnp.bfloat16, jnp.float32

SMEM = pl.BlockSpec(memory_space=pltpu.SMEM)
VMEM = pl.BlockSpec(memory_space=pltpu.VMEM)
ANY = pl.BlockSpec(memory_space=pl.ANY)


def ring(value, second, step):
    pairs = []
    for row in range(16):
        for col in range(16):
            x, y = row // 4, row % 4
            if col % 2 == second:
                x = (x + step) % 4
            else:
                y = (y + step) % 4
            pairs.append((row * 16 + col, (x * 4 + y) * 16 + col))
    return lax.ppermute(value, ("row", "col"), pairs)


def along_z(value):
    return lax.ppermute(value, "col", [(i, (i + (-2 if i % 2 else 2)) % 16) for i in range(16)])


def along_z_across(value, own):
    pairs = []
    for i in range(16):
        core = i % 2 if own else 1 - i % 2
        pairs.append((i, ((i + (-2 if core else 2)) % 16) ^ 1))
    return lax.ppermute(value, "col", pairs)


def swap(value, mask=1):
    return lax.ppermute(value, "col", [(i, i ^ mask) for i in range(16)])


def total(*values):
    result = values[0].astype(F32)
    for value in values[1:]:
        result = result + value.astype(F32)
    return result


def row_place(block, meta_ref, sign):
    row, core = meta_ref[1], meta_ref[2] & 1
    owner, within = block >> 2, block & 3
    x, y = (sign * ((owner >> 2) - (row >> 2))) & 3, (sign * (owner - row)) & 3
    return jnp.where(core == 0, y * 4 + x, x * 4 + y), within


def col_steps(block, meta_ref, sign):
    col = meta_ref[2]
    owner, within = block >> 2, block & 3
    way = sign * (1 - 2 * (col & 1))
    return (way * ((owner >> 1) - (col >> 1))) & 7, (owner ^ col) & 1, within


def sum_tiles(dims, meta_ref, source_ref, target_ref, tiles_ref, load, acc_ref, place):
    blocks = acc_ref.shape[0] - 1
    count = meta_ref[0]

    def add_group(group, carry):
        products, targets = [], []
        for member in range(UNROLL):
            slot = group * UNROLL + member
            products.append(
                lax.dot_general(tiles_ref[slot], load(source_ref[slot]), (dims, ((), ())), preferred_element_type=F32)
            )
            targets.append(jnp.where(slot < count, place(target_ref[slot]), blocks))
        for product, target in zip(products, targets):
            acc_ref[target] += product
        return carry

    lax.fori_loop(0, (count + UNROLL - 1) // UNROLL, add_group, 0)


def fill(pairs, sems, acc_ref):
    copies = [pltpu.make_async_copy(source, there, sems.at[index]) for index, (source, there) in enumerate(pairs)]
    for copy in copies:
        copy.start()

    def clear(block, carry):
        acc_ref[block] = jnp.zeros(acc_ref.shape[1:], F32)
        return carry

    lax.fori_loop(0, acc_ref.shape[0], clear, 0)
    for copy in copies:
        copy.wait()


def forward_kernel(meta_ref, rows_ref, cols_ref, tiles_any, *refs):
    pieces, (mine_ref, other_ref, far_ref, far_other_ref, tiles_ref, feats_ref, acc_ref, sems) = refs[:8], refs[8:]
    pairs = [(ref, feats_ref.at[pl.ds(index * 2, 2)]) for index, ref in enumerate(pieces)]
    fill(pairs + [(tiles_any, tiles_ref)], sems, acc_ref)

    def load(block):
        owner, within = row_place(block, meta_ref, -1)
        return feats_ref[owner, pl.ds(pl.multiple_of(within * TILE, TILE), TILE), :]

    def place(block):
        steps, other, within = col_steps(block, meta_ref, 1)
        flip = jnp.where((steps > 4) | ((steps == 0) & (other == 1)), 1, 0)
        near, side = jnp.where(flip == 1, (8 - steps) & 7, steps), other ^ flip
        near = flip * 7 + jnp.maximum(2 * near - 1, 0) + side
        return jnp.where(steps == 4, 14 + other, near) * LOCAL + within

    sum_tiles(((1,), (0,)), meta_ref, cols_ref, rows_ref, tiles_ref, load, acc_ref, place)

    def finish(step, carry):
        at = pl.ds(pl.multiple_of((step & 3) * TILE, TILE), TILE)
        mine_ref[step >> 2, at, :] = acc_ref[step].astype(BF16)
        other_ref[step >> 2, at, :] = acc_ref[7 * LOCAL + step].astype(BF16)
        return carry

    lax.fori_loop(0, 7 * LOCAL, finish, 0)
    for within in range(LOCAL):
        at = pl.ds(within * TILE, TILE)
        far_ref[at, :] = acc_ref[14 * LOCAL + within].astype(BF16)
        far_other_ref[at, :] = acc_ref[15 * LOCAL + within].astype(BF16)


def backward_kernel(meta_ref, rows_ref, cols_ref, tiles_any, *refs):
    pieces, near, tail_ref = refs[:10], refs[10], refs[11]
    (keep, plus_a, plus_b, minus_a, minus_b, far_a, far_b), (tiles_ref, feats_ref, acc_ref, sems) = refs[12:19], refs[19:]
    pairs = [(ref, feats_ref.at[index // 2, index % 2]) for index, ref in enumerate(pieces)]
    pairs += [(near.at[index], feats_ref.at[7 - index // 2, 1 - index % 2]) for index in range(6)]
    fill(pairs + [(tiles_any, tiles_ref)], sems, acc_ref)

    def load(block):
        steps, other, within = col_steps(block, meta_ref, -1)
        return feats_ref[steps, other, pl.ds(pl.multiple_of(within * TILE, TILE), TILE), :]

    def place(block):
        owner, within = row_place(block, meta_ref, 1)
        return owner * LOCAL + within

    sum_tiles(((0,), (0,)), meta_ref, rows_ref, cols_ref, tiles_ref, load, acc_ref, place)
    for out, first_block, blocks in (
        (far_a, 32, 8), (far_b, 40, 8), (plus_b, 24, 8), (minus_a, 48, 8), (plus_a, 16, 8), (minus_b, 56, 8), (keep, 0, 16),
    ):

        def finish(index, carry):
            out[pl.ds(pl.multiple_of(index * TILE, TILE), TILE), :] = acc_ref[first_block + index].astype(BF16)
            return carry

        lax.fori_loop(0, blocks, finish, 0)
    for out in (far_a, plus_a, minus_b):
        out[pl.ds(2 * SHARD, TAIL), :] = tail_ref[...]


def tile_sums(kernel, outs, scratch, copies, meta, rows, cols, tiles, pieces, more=()):
    channels = scratch[-1]
    blocks = 16 * LOCAL
    return pl.pallas_call(
        kernel,
        out_shape=outs,
        in_specs=[SMEM] * 3 + [ANY] * (1 + len(pieces)) + [VMEM] * len(more),
        out_specs=[VMEM] * len(outs),
        scratch_shapes=[
            pltpu.VMEM(tiles.shape, BF16),
            pltpu.VMEM(scratch, BF16),
            pltpu.VMEM((blocks + 1, TILE, channels), F32),
            pltpu.SemaphoreType.DMA((copies,)),
        ],
        compiler_params=pltpu.CompilerParams(vmem_limit_bytes=28 * 2**20),
        cost_estimate=pl.CostEstimate(
            flops=2 * tiles.shape[0] * TILE * TILE * channels, bytes_accessed=12 * 2**20, transcendentals=0
        ),
    )(meta, rows, cols, tiles, *pieces, *more)


def small_call(kernel, outs, *args, **more):
    return pl.pallas_call(
        kernel, out_shape=outs, in_specs=[VMEM] * len(args), out_specs=[VMEM] * len(outs),
        compiler_params=pltpu.CompilerParams(vmem_limit_bytes=16 * 2**20), **more,
    )(*args)


def middle_kernel(meta_ref, same_ref, cross_ref, weight_ref, bias_ref, upstream_ref,
                  out_ref, grad_ref, tail_ref, message_ref):
    gathered = total(same_ref[...], cross_ref[...]).astype(BF16)
    preact = jnp.dot(gathered, weight_ref[...], preferred_element_type=F32) + bias_ref[...]
    squashed = jax.nn.sigmoid(preact)
    out_ref[...] = (preact * squashed).astype(BF16)
    slope = squashed * (1.0 + preact * (1.0 - squashed))
    grad = (upstream_ref[...].astype(F32) * slope).astype(BF16)
    grad_ref[...] = grad
    weight_part = lax.dot_general(gathered, grad, (((0,), (0,)), ((), ())), preferred_element_type=F32)
    bias_part = jnp.sum(grad.astype(F32), axis=0, keepdims=True)
    first = lax.broadcasted_iota(jnp.int32, (TAIL - HALF, bias_part.shape[1]), 0) == 0
    bias_part = jnp.where(first, bias_part, 0.0)
    lower = (meta_ref[2] & 1) == 0
    tail_ref[pl.ds(0, HALF), :] = jnp.where(lower, weight_part[:HALF], weight_part[HALF:])
    tail_ref[pl.ds(HALF, TAIL - HALF), :] = bias_part
    message_ref[pl.ds(0, HALF), :] = jnp.where(lower, weight_part[HALF:], weight_part[:HALF]).astype(BF16)
    message_ref[pl.ds(HALF, TAIL - HALF), :] = bias_part.astype(BF16)


def middle(meta, same, cross, weight, bias, upstream):
    channels = weight.shape[0]

    return pl.pallas_call(
        middle_kernel,
        out_shape=[
            jax.ShapeDtypeStruct(upstream.shape, BF16),
            jax.ShapeDtypeStruct(upstream.shape, BF16),
            jax.ShapeDtypeStruct((TAIL, channels), F32),
            jax.ShapeDtypeStruct((TAIL, channels), BF16),
        ],
        in_specs=[SMEM] + [VMEM] * 5,
        out_specs=[VMEM] * 4,
        compiler_params=pltpu.CompilerParams(vmem_limit_bytes=16 * 2**20),
    )(meta, same, cross, weight, bias, upstream)


def relay_kernel(own_ref, far_ref, out_ref):
    rows = 2 * SHARD
    out_ref[pl.ds(0, rows), :] = total(own_ref[pl.ds(0, rows), :], far_ref[pl.ds(0, rows), :]).astype(BF16)
    at = rows
    for ref in (own_ref, far_ref):
        if ref.shape[0] > rows:
            out_ref[pl.ds(at, TAIL), :] = ref[pl.ds(rows, TAIL), :]
            at += TAIL


def relay(own, far):
    rows = own.shape[0] + far.shape[0] - 2 * SHARD
    return small_call(relay_kernel, [jax.ShapeDtypeStruct((rows, own.shape[1]), BF16)], own, far)[0]


def four(own, plus, far, minus):
    return total(own, far) + total(plus, minus)


def near_kernel(keep_ref, plus_b, minus_a, out_ref):
    rows = 2 * SHARD
    out_ref[pl.ds(0, rows), :] = total(keep_ref[pl.ds(0, rows), :], minus_a[...])
    out_ref[pl.ds(rows, rows), :] = total(keep_ref[pl.ds(rows, rows), :], plus_b[...])


def split_kernel(tail_ref, near_ref, plus_a, minus_b, *outs):
    rows = 2 * SHARD
    tail = four(
        tail_ref[...], plus_a[pl.ds(rows, TAIL), :], plus_a[pl.ds(rows + TAIL, TAIL), :], minus_b[pl.ds(rows, TAIL), :]
    ).astype(BF16)
    for first, out_ref in enumerate(outs):
        ref = plus_a if first < 2 else minus_b
        arrived = total(near_ref[pl.ds(first * SHARD, SHARD), :], ref[pl.ds(first % 2 * SHARD, SHARD), :])
        out_ref[pl.ds(0, SHARD), :] = arrived.astype(BF16)
        out_ref[pl.ds(SHARD, TAIL), :] = tail


def last_tail_kernel(own_ref, plus_ref, far_ref, minus_ref, out_ref):
    out_ref[...] = four(*[ref[pl.ds(SHARD, TAIL), :] for ref in (own_ref, plus_ref, far_ref, minus_ref)])


def unpack_kernel(meta_ref, own_ref, swapped_ref, weight_ref, bias_ref):
    lower = (meta_ref[2] & 1) == 0
    weight_ref[pl.ds(0, HALF), :] = jnp.where(lower, own_ref[:HALF], swapped_ref[:HALF])
    weight_ref[pl.ds(HALF, HALF), :] = jnp.where(lower, swapped_ref[:HALF], own_ref[:HALF])
    bias_ref[...] = jnp.where(lower, own_ref[HALF : HALF + 1], swapped_ref[HALF : HALF + 1])


def unpack(meta, own, swapped):
    channels = own.shape[1]
    return pl.pallas_call(
        unpack_kernel,
        out_shape=[jax.ShapeDtypeStruct((2 * HALF, channels), F32), jax.ShapeDtypeStruct((1, channels), F32)],
        in_specs=[SMEM, VMEM, VMEM], out_specs=[VMEM] * 2,
    )(meta, own, swapped)


def last_kernel(own_ref, plus_ref, far_ref, minus_ref, weight_ref, out_ref):
    hidden = total(*[ref[pl.ds(0, SHARD), :] for ref in (own_ref, plus_ref, far_ref, minus_ref)]).astype(BF16)
    out_ref[...] = lax.dot_general(
        hidden, weight_ref[...], (((1,), (1,)), ((), ())), preferred_element_type=F32
    ).astype(BF16)


def gather_rows(value):
    one, three, two = ring(value, 0, 1), ring(value, 0, 3), ring(value, 0, 2)
    a = jnp.stack([value, one])
    two, three = lax.optimization_barrier((two, three, a))[:2]
    b = jnp.stack([two, three])
    b3, a1 = ring(b, 1, 3), ring(a, 1, 1)
    b1, a3 = ring(b, 1, 1), ring(a, 1, 3)
    b2, a2 = ring(b3, 1, 3), ring(a1, 1, 1)
    return a, b, a1, b1, a2, b2, a3, b3


def scatter_rows(pieces, tail):
    keep, plus_a, plus_b, minus_a, minus_b, far_a, far_b = pieces
    far_a, far_b = ring(far_a, 1, 1), ring(far_b, 1, 3)
    plus_b, minus_a = ring(plus_b, 1, 1), ring(minus_a, 1, 3)
    plus_a, minus_b = ring(relay(plus_a, far_a), 1, 1), ring(relay(minus_b, far_b), 1, 3)
    shard = jax.ShapeDtypeStruct((SHARD + TAIL, tail.shape[1]), BF16)
    [near] = small_call(near_kernel, [jax.ShapeDtypeStruct(keep.shape, F32)], keep, plus_b, minus_a)
    pieces = small_call(split_kernel, [shard] * 4, tail, near, plus_a, minus_b)
    return [pieces[0]] + [ring(pieces[step], 0, step) for step in (1, 2, 3)]


def add_kernel(mine_ref, other_ref, arrived_ref, out_ref):
    out_ref[...] = total(mine_ref[0], other_ref[0], arrived_ref[...]).astype(BF16)


def add(index, mine, other, arrived):
    shard = pl.BlockSpec((1, *arrived.shape), lambda step: (index, 0, 0))
    return pl.pallas_call(
        add_kernel, grid=(1,), out_shape=jax.ShapeDtypeStruct(arrived.shape, BF16), in_specs=[shard, shard, VMEM],
        out_specs=VMEM, compiler_params=pltpu.CompilerParams(vmem_limit_bytes=16 * 2**20),
    )(mine, other, arrived)


def scatter_cols(mine, other, far, far_other):
    same, cross = along_z(far), along_z(far_other)
    other = swap(other)
    for steps in (3, 2, 1):
        same = along_z(add(2 * steps - 1, mine, other, same))
        cross = add(2 * steps, mine, other, cross)
        cross = along_z(cross) if steps > 1 else along_z_across(cross, True)
    return add(0, mine, other, same), cross


def gather_cols(value, tail, message):
    tie = lax.optimization_barrier
    pieces = [value, swap(value)]
    same, cross = value, value
    for mask in (1, 2, 4, 8):
        same, cross = along_z(same), along_z_across(cross, False) if mask == 1 else along_z(cross)
        tail = total(tail, swap(message if mask == 1 else tail, mask)).astype(BF16)
        if mask != 8:
            cross, tail = tie((cross, tail))
        pieces += [same, cross]
    return pieces + [swap(jnp.stack(pieces[2:8]))], tail


def body(features, weight, out_bias, upstream, adj_tiles, tile_rows, tile_cols, tile_count):
    tiles, rows, cols = adj_tiles[0, 0], tile_rows[0, 0], tile_cols[0, 0]
    meta = jnp.stack([tile_count[0, 0], lax.axis_index("row"), lax.axis_index("col")])
    channels = features.shape[1]

    part, shard = [jax.ShapeDtypeStruct(shape, BF16) for shape in ((7, SHARD, channels), (SHARD, channels))]
    terms = tile_sums(
        forward_kernel, [part, part, shard, shard], (16, SHARD, channels), 9, meta, rows, cols, tiles,
        gather_rows(features),
    )
    terms = scatter_cols(*terms)
    out_features, grad_pre, tail, message = middle(meta, *terms, weight, out_bias[None, :], upstream)

    pieces, tail = gather_cols(grad_pre, tail, message)
    two = 2 * SHARD
    outs = [
        jax.ShapeDtypeStruct((count, channels), BF16)
        for count in (2 * two, two + TAIL, two, two, two + TAIL, two + TAIL, two)
    ]
    pieces = tile_sums(
        backward_kernel, outs, (8, 2, SHARD, channels), 17, meta, rows, cols, tiles, pieces, (tail,)
    )
    terms = scatter_rows(pieces, tail)
    [tail] = small_call(last_tail_kernel, [jax.ShapeDtypeStruct((TAIL, channels), F32)], *terms)
    swapped = swap(tail)
    [grad_features] = small_call(last_kernel, [jax.ShapeDtypeStruct(features.shape, BF16)], *terms, weight)
    grad_weight, grad_bias = unpack(meta, tail, swapped)
    return (out_features, grad_features, grad_weight, grad_bias[0])


def solution(mesh):
    return jax.shard_map(
        body,
        mesh=mesh,
        in_specs=(
            P(("col", "row"), None),
            P(),
            P(),
            P(("row", "col"), None),
            P("row", "col", None, None, None),
            P("row", "col", None),
            P("row", "col", None),
            P("row", "col"),
        ),
        out_specs=(P(("row", "col"), None), P(("col", "row"), None), P(), P()),
        check_vma=False,
    )
```

```python
import jax
import jax.numpy as jnp
from jax import lax
from jax.experimental import pallas as pl
from jax.experimental.pallas import tpu as pltpu
from jax.sharding import PartitionSpec as P

TILE = 128
UNROLL = 8
SHARD = 512
LOCAL = SHARD // TILE
HALF = 128
TAIL = HALF + 16
BF16, F32 = jnp.bfloat16, jnp.float32

SMEM = pl.BlockSpec(memory_space=pltpu.SMEM)
VMEM = pl.BlockSpec(memory_space=pltpu.VMEM)
ANY = pl.BlockSpec(memory_space=pl.ANY)


def ring(value, second, step):
    pairs = []
    for row in range(16):
        for col in range(16):
            x, y = row // 4, row % 4
            if col % 2 == second:
                x = (x + step) % 4
            else:
                y = (y + step) % 4
            pairs.append((row * 16 + col, (x * 4 + y) * 16 + col))
    return lax.ppermute(value, ("row", "col"), pairs)


def along_z(value):
    return lax.ppermute(value, "col", [(i, (i + (-2 if i % 2 else 2)) % 16) for i in range(16)])


def along_z_across(value, own):
    pairs = []
    for i in range(16):
        core = i % 2 if own else 1 - i % 2
        pairs.append((i, ((i + (-2 if core else 2)) % 16) ^ 1))
    return lax.ppermute(value, "col", pairs)


def swap(value, mask=1):
    return lax.ppermute(value, "col", [(i, i ^ mask) for i in range(16)])


def total(*values):
    result = values[0].astype(F32)
    for value in values[1:]:
        result = result + value.astype(F32)
    return result


def row_place(block, meta_ref, sign):
    row, core = meta_ref[1], meta_ref[2] & 1
    owner, within = block >> 2, block & 3
    x, y = (sign * ((owner >> 2) - (row >> 2))) & 3, (sign * (owner - row)) & 3
    return jnp.where(core == 0, y * 4 + x, x * 4 + y), within


def col_steps(block, meta_ref, sign):
    col = meta_ref[2]
    owner, within = block >> 2, block & 3
    way = sign * (1 - 2 * (col & 1))
    return (way * ((owner >> 1) - (col >> 1))) & 7, (owner ^ col) & 1, within


def sum_tiles(dims, meta_ref, source_ref, target_ref, tiles_ref, load, acc_ref, place):
    blocks = acc_ref.shape[0] - 1
    count = meta_ref[0]

    def add_group(group, carry):
        products, targets = [], []
        for member in range(UNROLL):
            slot = group * UNROLL + member
            products.append(
                lax.dot_general(tiles_ref[slot], load(source_ref[slot]), (dims, ((), ())), preferred_element_type=F32)
            )
            targets.append(jnp.where(slot < count, place(target_ref[slot]), blocks))
        for product, target in zip(products, targets):
            acc_ref[target] += product
        return carry

    lax.fori_loop(0, (count + UNROLL - 1) // UNROLL, add_group, 0)


def fill(pairs, sems, acc_ref):
    copies = [pltpu.make_async_copy(source, there, sems.at[index]) for index, (source, there) in enumerate(pairs)]
    for copy in copies:
        copy.start()

    def clear(block, carry):
        acc_ref[block] = jnp.zeros(acc_ref.shape[1:], F32)
        return carry

    lax.fori_loop(0, acc_ref.shape[0], clear, 0)
    for copy in copies:
        copy.wait()


def forward_kernel(meta_ref, rows_ref, cols_ref, tiles_any, *refs):
    pieces, (mine_ref, other_ref, far_ref, far_other_ref, tiles_ref, feats_ref, acc_ref, sems) = refs[:4], refs[4:]
    pairs = [(ref, feats_ref.at[pl.ds(index * 4, 4)]) for index, ref in enumerate(pieces)]
    fill(pairs + [(tiles_any, tiles_ref)], sems, acc_ref)

    def load(block):
        owner, within = row_place(block, meta_ref, -1)
        return feats_ref[owner, pl.ds(pl.multiple_of(within * TILE, TILE), TILE), :]

    def place(block):
        steps, other, within = col_steps(block, meta_ref, 1)
        flip = jnp.where((steps > 4) | ((steps == 0) & (other == 1)), 1, 0)
        near, side = jnp.where(flip == 1, (8 - steps) & 7, steps), other ^ flip
        near = flip * 7 + jnp.maximum(2 * near - 1, 0) + side
        return jnp.where(steps == 4, 14 + other, near) * LOCAL + within

    sum_tiles(((1,), (0,)), meta_ref, cols_ref, rows_ref, tiles_ref, load, acc_ref, place)

    def finish(step, carry):
        at = pl.ds(pl.multiple_of((step & 3) * TILE, TILE), TILE)
        mine_ref[step >> 2, at, :] = acc_ref[step].astype(BF16)
        other_ref[step >> 2, at, :] = acc_ref[7 * LOCAL + step].astype(BF16)
        return carry

    lax.fori_loop(0, 7 * LOCAL, finish, 0)
    for within in range(LOCAL):
        at = pl.ds(within * TILE, TILE)
        far_ref[at, :] = acc_ref[14 * LOCAL + within].astype(BF16)
        far_other_ref[at, :] = acc_ref[15 * LOCAL + within].astype(BF16)


def backward_kernel(meta_ref, rows_ref, cols_ref, tiles_any, *refs):
    pieces, near, outs, (tiles_ref, feats_ref, acc_ref, sems) = refs[:10], refs[10], refs[11:15], refs[15:]
    pairs = [(ref, feats_ref.at[index // 2, index % 2]) for index, ref in enumerate(pieces)]
    pairs += [(near.at[index], feats_ref.at[7 - index // 2, 1 - index % 2]) for index in range(6)]
    fill(pairs + [(tiles_any, tiles_ref)], sems, acc_ref)

    def load(block):
        steps, other, within = col_steps(block, meta_ref, -1)
        return feats_ref[steps, other, pl.ds(pl.multiple_of(within * TILE, TILE), TILE), :]

    def place(block):
        owner, within = row_place(block, meta_ref, 1)
        return owner * LOCAL + within

    sum_tiles(((0,), (0,)), meta_ref, rows_ref, cols_ref, tiles_ref, load, acc_ref, place)
    for second in (2, 1, 3, 0):
        out, first_block = outs[second], second * 4 * LOCAL

        def finish(index, carry):
            out[pl.ds(pl.multiple_of(index * TILE, TILE), TILE), :] = acc_ref[first_block + index].astype(BF16)
            return carry

        lax.fori_loop(0, 4 * LOCAL, finish, 0)


def tile_sums(kernel, outs, scratch, copies, meta, rows, cols, tiles, pieces):
    channels = scratch[-1]
    blocks = 16 * LOCAL
    return pl.pallas_call(
        kernel,
        out_shape=outs,
        in_specs=[SMEM] * 3 + [ANY] * (1 + len(pieces)),
        out_specs=[VMEM] * len(outs),
        scratch_shapes=[
            pltpu.VMEM(tiles.shape, BF16),
            pltpu.VMEM(scratch, BF16),
            pltpu.VMEM((blocks + 1, TILE, channels), F32),
            pltpu.SemaphoreType.DMA((copies,)),
        ],
        compiler_params=pltpu.CompilerParams(vmem_limit_bytes=28 * 2**20),
        cost_estimate=pl.CostEstimate(
            flops=2 * tiles.shape[0] * TILE * TILE * channels, bytes_accessed=12 * 2**20, transcendentals=0
        ),
    )(meta, rows, cols, tiles, *pieces)


def small_call(kernel, outs, *args, **more):
    return pl.pallas_call(
        kernel, out_shape=outs, in_specs=[VMEM] * len(args), out_specs=[VMEM] * len(outs),
        compiler_params=pltpu.CompilerParams(vmem_limit_bytes=16 * 2**20), **more,
    )(*args)


def middle_kernel(meta_ref, same_ref, cross_ref, weight_ref, bias_ref, upstream_ref,
                  out_ref, grad_ref, tail_ref, message_ref):
    gathered = total(same_ref[...], cross_ref[...]).astype(BF16)
    preact = jnp.dot(gathered, weight_ref[...], preferred_element_type=F32) + bias_ref[...]
    squashed = jax.nn.sigmoid(preact)
    out_ref[...] = (preact * squashed).astype(BF16)
    slope = squashed * (1.0 + preact * (1.0 - squashed))
    grad = (upstream_ref[...].astype(F32) * slope).astype(BF16)
    grad_ref[...] = grad
    weight_part = lax.dot_general(gathered, grad, (((0,), (0,)), ((), ())), preferred_element_type=F32)
    bias_part = jnp.sum(grad.astype(F32), axis=0, keepdims=True)
    first = lax.broadcasted_iota(jnp.int32, (TAIL - HALF, bias_part.shape[1]), 0) == 0
    bias_part = jnp.where(first, bias_part, 0.0)
    lower = (meta_ref[2] & 1) == 0
    tail_ref[pl.ds(0, HALF), :] = jnp.where(lower, weight_part[:HALF], weight_part[HALF:])
    tail_ref[pl.ds(HALF, TAIL - HALF), :] = bias_part
    message_ref[pl.ds(0, HALF), :] = jnp.where(lower, weight_part[HALF:], weight_part[:HALF]).astype(BF16)
    message_ref[pl.ds(HALF, TAIL - HALF), :] = bias_part.astype(BF16)


def middle(meta, same, cross, weight, bias, upstream):
    channels = weight.shape[0]

    return pl.pallas_call(
        middle_kernel,
        out_shape=[
            jax.ShapeDtypeStruct(upstream.shape, BF16),
            jax.ShapeDtypeStruct(upstream.shape, BF16),
            jax.ShapeDtypeStruct((TAIL, channels), F32),
            jax.ShapeDtypeStruct((TAIL, channels), BF16),
        ],
        in_specs=[SMEM] + [VMEM] * 5,
        out_specs=[VMEM] * 4,
        compiler_params=pltpu.CompilerParams(vmem_limit_bytes=16 * 2**20),
    )(meta, same, cross, weight, bias, upstream)


def four(own, plus, far, minus):
    return total(own, far) + total(plus, minus)


def split_kernel(tail_ref, tail1_ref, tail2_ref, tail3_ref, own_ref, plus_ref, far_ref, minus_ref, *outs):
    tail = four(tail_ref[...], tail1_ref[...], tail2_ref[...], tail3_ref[...]).astype(BF16)
    for first, out_ref in enumerate(outs):
        at = pl.ds(first * SHARD, SHARD)
        out_ref[pl.ds(0, SHARD), :] = total(*[ref[at, :] for ref in (own_ref, plus_ref, far_ref, minus_ref)]).astype(BF16)
        out_ref[pl.ds(SHARD, TAIL), :] = tail


def last_tail_kernel(own_ref, plus_ref, far_ref, minus_ref, out_ref):
    out_ref[...] = four(*[ref[pl.ds(SHARD, TAIL), :] for ref in (own_ref, plus_ref, far_ref, minus_ref)])


def last_kernel(own_ref, plus_ref, far_ref, minus_ref, weight_ref, out_ref):
    hidden = total(*[ref[pl.ds(0, SHARD), :] for ref in (own_ref, plus_ref, far_ref, minus_ref)]).astype(BF16)
    out_ref[...] = lax.dot_general(
        hidden, weight_ref[...], (((1,), (1,)), ((), ())), preferred_element_type=F32
    ).astype(BF16)


def gather_rows(value):
    own = jnp.stack([value] + [ring(value, 0, step) for step in (1, 2, 3)])
    return [own] + [ring(own, 1, step) for step in (1, 2, 3)]


def scatter_rows(pieces, tail):
    moved = [ring(pieces[step], 1, step) for step in (1, 2, 3)]
    tails = [ring(tail, 1, step) for step in (1, 2, 3)]
    shard = jax.ShapeDtypeStruct((SHARD + TAIL, tail.shape[1]), BF16)
    pieces = small_call(split_kernel, [shard] * 4, tail, *tails, pieces[0], *moved)
    return [pieces[0]] + [ring(pieces[step], 0, step) for step in (1, 2, 3)]


def add_kernel(mine_ref, other_ref, arrived_ref, out_ref):
    out_ref[...] = total(mine_ref[0], other_ref[0], arrived_ref[...]).astype(BF16)


def add(index, mine, other, arrived):
    shard = pl.BlockSpec((1, *arrived.shape), lambda step: (index, 0, 0))
    return pl.pallas_call(
        add_kernel, grid=(1,), out_shape=jax.ShapeDtypeStruct(arrived.shape, BF16), in_specs=[shard, shard, VMEM],
        out_specs=VMEM, compiler_params=pltpu.CompilerParams(vmem_limit_bytes=16 * 2**20),
    )(mine, other, arrived)


def scatter_cols(mine, other, far, far_other):
    same, cross = along_z(far), along_z(far_other)
    other = swap(other)
    for steps in (3, 2, 1):
        same = along_z(add(2 * steps - 1, mine, other, same))
        cross = add(2 * steps, mine, other, cross)
        cross = along_z(cross) if steps > 1 else along_z_across(cross, True)
    return add(0, mine, other, same), cross


def gather_cols(value, tail, message):
    tie = lax.optimization_barrier
    pieces = [value, swap(value)]
    same, cross = value, value
    for mask in (1, 2, 4, 8):
        same, cross = along_z(same), along_z_across(cross, False) if mask == 1 else along_z(cross)
        tail = total(tail, swap(message if mask == 1 else tail, mask)).astype(BF16)
        if mask < 4:
            cross, tail = tie((cross, tail))
        pieces += [same, cross]
    return pieces + [swap(jnp.stack(pieces[2:8]))], tail


def body(features, weight, out_bias, upstream, adj_tiles, tile_rows, tile_cols, tile_count):
    tiles, rows, cols = adj_tiles[0, 0], tile_rows[0, 0], tile_cols[0, 0]
    meta = jnp.stack([tile_count[0, 0], lax.axis_index("row"), lax.axis_index("col")])
    channels = features.shape[1]

    part, shard = [jax.ShapeDtypeStruct(shape, BF16) for shape in ((7, SHARD, channels), (SHARD, channels))]
    terms = tile_sums(
        forward_kernel, [part, part, shard, shard], (16, SHARD, channels), 5, meta, rows, cols, tiles,
        gather_rows(features),
    )
    terms = scatter_cols(*terms)
    out_features, grad_pre, tail, message = middle(meta, *terms, weight, out_bias[None, :], upstream)

    pieces, tail = gather_cols(grad_pre, tail, message)
    part = jax.ShapeDtypeStruct((4 * SHARD, channels), BF16)
    pieces = tile_sums(
        backward_kernel, [part] * 4, (8, 2, SHARD, channels), 17, meta, rows, cols, tiles, pieces
    )
    terms = scatter_rows(pieces, tail)
    [tail] = small_call(last_tail_kernel, [jax.ShapeDtypeStruct((TAIL, channels), F32)], *terms)
    swapped = swap(tail)
    [grad_features] = small_call(last_kernel, [jax.ShapeDtypeStruct(features.shape, BF16)], *terms, weight)
    lower = (lax.axis_index("col") & 1) == 0
    first, second = jnp.where(lower, tail, swapped), jnp.where(lower, swapped[:HALF], tail[:HALF])
    return (out_features, grad_features, jnp.concatenate([first[:HALF], second]), first[HALF])


def solution(mesh):
    return jax.shard_map(
        body,
        mesh=mesh,
        in_specs=(
            P(("col", "row"), None),
            P(),
            P(),
            P(("row", "col"), None),
            P("row", "col", None, None, None),
            P("row", "col", None),
            P("row", "col", None),
            P("row", "col"),
        ),
        out_specs=(P(("row", "col"), None), P(("col", "row"), None), P(), P()),
        check_vma=False,
    )
```

```python
import jax
import jax.numpy as jnp
from jax import lax
from jax.experimental import pallas as pl
from jax.experimental.pallas import tpu as pltpu
from jax.sharding import PartitionSpec as P

TILE = 128
UNROLL = 8
SHARD = 512
LOCAL = SHARD // TILE
HALF = 128
TAIL = HALF + 16
BF16, F32 = jnp.bfloat16, jnp.float32

SMEM = pl.BlockSpec(memory_space=pltpu.SMEM)
VMEM = pl.BlockSpec(memory_space=pltpu.VMEM)
ANY = pl.BlockSpec(memory_space=pl.ANY)


def ring(value, second, step):
    pairs = []
    for row in range(16):
        for col in range(16):
            x, y = row // 4, row % 4
            if col % 2 == second:
                x = (x + step) % 4
            else:
                y = (y + step) % 4
            pairs.append((row * 16 + col, (x * 4 + y) * 16 + col))
    return lax.ppermute(value, ("row", "col"), pairs)


def along_z(value):
    return lax.ppermute(value, "col", [(i, (i + (-2 if i % 2 else 2)) % 16) for i in range(16)])


def along_z_across(value, own):
    pairs = []
    for i in range(16):
        core = i % 2 if own else 1 - i % 2
        pairs.append((i, ((i + (-2 if core else 2)) % 16) ^ 1))
    return lax.ppermute(value, "col", pairs)


def swap(value, mask=1):
    return lax.ppermute(value, "col", [(i, i ^ mask) for i in range(16)])


def total(*values):
    result = values[0].astype(F32)
    for value in values[1:]:
        result = result + value.astype(F32)
    return result


def row_place(block, meta_ref, sign):
    row, core = meta_ref[1], meta_ref[2] & 1
    owner, within = block >> 2, block & 3
    x, y = (sign * ((owner >> 2) - (row >> 2))) & 3, (sign * (owner - row)) & 3
    return jnp.where(core == 0, y * 4 + x, x * 4 + y), within


def col_steps(block, meta_ref, sign):
    col = meta_ref[2]
    owner, within = block >> 2, block & 3
    way = sign * (1 - 2 * (col & 1))
    return (way * ((owner >> 1) - (col >> 1))) & 7, (owner ^ col) & 1, within


def sum_tiles(dims, meta_ref, source_ref, target_ref, tiles_ref, load, acc_ref, place):
    blocks = acc_ref.shape[0] - 1
    count = meta_ref[0]

    def add_group(group, carry):
        products, targets = [], []
        for member in range(UNROLL):
            slot = group * UNROLL + member
            products.append(
                lax.dot_general(tiles_ref[slot], load(source_ref[slot]), (dims, ((), ())), preferred_element_type=F32)
            )
            targets.append(jnp.where(slot < count, place(target_ref[slot]), blocks))
        for product, target in zip(products, targets):
            acc_ref[target] += product
        return carry

    lax.fori_loop(0, (count + UNROLL - 1) // UNROLL, add_group, 0)


def fill(pairs, sems, acc_ref):
    copies = [pltpu.make_async_copy(source, there, sems.at[index]) for index, (source, there) in enumerate(pairs)]
    for copy in copies:
        copy.start()

    def clear(block, carry):
        acc_ref[block] = jnp.zeros(acc_ref.shape[1:], F32)
        return carry

    lax.fori_loop(0, acc_ref.shape[0], clear, 0)
    for copy in copies:
        copy.wait()


def forward_kernel(meta_ref, rows_ref, cols_ref, tiles_any, *refs):
    pieces, (mine_ref, other_ref, far_ref, far_other_ref, tiles_ref, feats_ref, acc_ref, sems) = refs[:8], refs[8:]
    pairs = [(ref, feats_ref.at[pl.ds(index * 2, 2)]) for index, ref in enumerate(pieces)]
    fill(pairs + [(tiles_any, tiles_ref)], sems, acc_ref)

    def load(block):
        owner, within = row_place(block, meta_ref, -1)
        return feats_ref[owner, pl.ds(pl.multiple_of(within * TILE, TILE), TILE), :]

    def place(block):
        steps, other, within = col_steps(block, meta_ref, 1)
        flip = jnp.where((steps > 4) | ((steps == 0) & (other == 1)), 1, 0)
        near, side = jnp.where(flip == 1, (8 - steps) & 7, steps), other ^ flip
        near = flip * 7 + jnp.maximum(2 * near - 1, 0) + side
        return jnp.where(steps == 4, 14 + other, near) * LOCAL + within

    sum_tiles(((1,), (0,)), meta_ref, cols_ref, rows_ref, tiles_ref, load, acc_ref, place)

    def finish(step, carry):
        at = pl.ds(pl.multiple_of((step & 3) * TILE, TILE), TILE)
        mine_ref[step >> 2, at, :] = acc_ref[step].astype(BF16)
        other_ref[step >> 2, at, :] = acc_ref[7 * LOCAL + step].astype(BF16)
        return carry

    lax.fori_loop(0, 7 * LOCAL, finish, 0)
    for within in range(LOCAL):
        at = pl.ds(within * TILE, TILE)
        far_ref[at, :] = acc_ref[14 * LOCAL + within].astype(BF16)
        far_other_ref[at, :] = acc_ref[15 * LOCAL + within].astype(BF16)


def backward_kernel(meta_ref, rows_ref, cols_ref, tiles_any, *refs):
    pieces, near, outs, (tiles_ref, feats_ref, acc_ref, sems) = refs[:10], refs[10:16], refs[16:20], refs[20:]
    pairs = [(ref, feats_ref.at[index // 2, index % 2]) for index, ref in enumerate(pieces)]
    pairs += [(ref, feats_ref.at[7 - index // 2, 1 - index % 2]) for index, ref in enumerate(near)]
    fill(pairs + [(tiles_any, tiles_ref)], sems, acc_ref)

    def load(block):
        steps, other, within = col_steps(block, meta_ref, -1)
        return feats_ref[steps, other, pl.ds(pl.multiple_of(within * TILE, TILE), TILE), :]

    def place(block):
        owner, within = row_place(block, meta_ref, 1)
        return owner * LOCAL + within

    sum_tiles(((0,), (0,)), meta_ref, rows_ref, cols_ref, tiles_ref, load, acc_ref, place)
    for second in (2, 1, 3, 0):
        out, first_block = outs[second], second * 4 * LOCAL

        def finish(index, carry):
            out[pl.ds(pl.multiple_of(index * TILE, TILE), TILE), :] = acc_ref[first_block + index].astype(BF16)
            return carry

        lax.fori_loop(0, 4 * LOCAL, finish, 0)


def tile_sums(kernel, outs, scratch, copies, meta, rows, cols, tiles, pieces):
    channels = scratch[-1]
    blocks = 16 * LOCAL
    return pl.pallas_call(
        kernel,
        out_shape=outs,
        in_specs=[SMEM] * 3 + [ANY] * (1 + len(pieces)),
        out_specs=[VMEM] * len(outs),
        scratch_shapes=[
            pltpu.VMEM(tiles.shape, BF16),
            pltpu.VMEM(scratch, BF16),
            pltpu.VMEM((blocks + 1, TILE, channels), F32),
            pltpu.SemaphoreType.DMA((copies,)),
        ],
        compiler_params=pltpu.CompilerParams(vmem_limit_bytes=28 * 2**20),
        cost_estimate=pl.CostEstimate(
            flops=2 * tiles.shape[0] * TILE * TILE * channels, bytes_accessed=12 * 2**20, transcendentals=0
        ),
    )(meta, rows, cols, tiles, *pieces)


def small_call(kernel, outs, *args, **more):
    return pl.pallas_call(
        kernel, out_shape=outs, in_specs=[VMEM] * len(args), out_specs=[VMEM] * len(outs),
        compiler_params=pltpu.CompilerParams(vmem_limit_bytes=16 * 2**20), **more,
    )(*args)


def middle_kernel(meta_ref, same_ref, cross_ref, weight_ref, bias_ref, upstream_ref,
                  out_ref, grad_ref, tail_ref, message_ref):
    gathered = total(same_ref[...], cross_ref[...]).astype(BF16)
    preact = jnp.dot(gathered, weight_ref[...], preferred_element_type=F32) + bias_ref[...]
    squashed = jax.nn.sigmoid(preact)
    out_ref[...] = (preact * squashed).astype(BF16)
    slope = squashed * (1.0 + preact * (1.0 - squashed))
    grad = (upstream_ref[...].astype(F32) * slope).astype(BF16)
    grad_ref[...] = grad
    weight_part = lax.dot_general(gathered, grad, (((0,), (0,)), ((), ())), preferred_element_type=F32)
    bias_part = jnp.sum(grad.astype(F32), axis=0, keepdims=True)
    first = lax.broadcasted_iota(jnp.int32, (TAIL - HALF, bias_part.shape[1]), 0) == 0
    bias_part = jnp.where(first, bias_part, 0.0)
    lower = (meta_ref[2] & 1) == 0
    tail_ref[pl.ds(0, HALF), :] = jnp.where(lower, weight_part[:HALF], weight_part[HALF:])
    tail_ref[pl.ds(HALF, TAIL - HALF), :] = bias_part
    message_ref[pl.ds(0, HALF), :] = jnp.where(lower, weight_part[HALF:], weight_part[:HALF]).astype(BF16)
    message_ref[pl.ds(HALF, TAIL - HALF), :] = bias_part.astype(BF16)


def middle(meta, same, cross, weight, bias, upstream):
    channels = weight.shape[0]

    return pl.pallas_call(
        middle_kernel,
        out_shape=[
            jax.ShapeDtypeStruct(upstream.shape, BF16),
            jax.ShapeDtypeStruct(upstream.shape, BF16),
            jax.ShapeDtypeStruct((TAIL, channels), F32),
            jax.ShapeDtypeStruct((TAIL, channels), BF16),
        ],
        in_specs=[SMEM] + [VMEM] * 5,
        out_specs=[VMEM] * 4,
        compiler_params=pltpu.CompilerParams(vmem_limit_bytes=16 * 2**20),
    )(meta, same, cross, weight, bias, upstream)


def four(own, plus, far, minus):
    return total(own, far) + total(plus, minus)


def split_kernel(tail_ref, tail1_ref, tail2_ref, tail3_ref, own_ref, plus_ref, far_ref, minus_ref, *outs):
    tail = four(tail_ref[...], tail1_ref[...], tail2_ref[...], tail3_ref[...]).astype(BF16)
    for first, out_ref in enumerate(outs):
        at = pl.ds(first * SHARD, SHARD)
        out_ref[pl.ds(0, SHARD), :] = total(*[ref[at, :] for ref in (own_ref, plus_ref, far_ref, minus_ref)]).astype(BF16)
        out_ref[pl.ds(SHARD, TAIL), :] = tail


def last_tail_kernel(own_ref, plus_ref, far_ref, minus_ref, out_ref):
    out_ref[...] = four(*[ref[pl.ds(SHARD, TAIL), :] for ref in (own_ref, plus_ref, far_ref, minus_ref)])


def last_kernel(own_ref, plus_ref, far_ref, minus_ref, weight_ref, out_ref):
    hidden = total(*[ref[pl.ds(0, SHARD), :] for ref in (own_ref, plus_ref, far_ref, minus_ref)]).astype(BF16)
    out_ref[...] = lax.dot_general(
        hidden, weight_ref[...], (((1,), (1,)), ((), ())), preferred_element_type=F32
    ).astype(BF16)


def gather_rows(value):
    one, three, two = ring(value, 0, 1), ring(value, 0, 3), ring(value, 0, 2)
    a = jnp.stack([value, one])
    two, three = lax.optimization_barrier((two, three, a))[:2]
    b = jnp.stack([two, three])
    b3, a1 = ring(b, 1, 3), ring(a, 1, 1)
    b1, a3 = ring(b, 1, 1), ring(a, 1, 3)
    b2, a2 = ring(b3, 1, 3), ring(a1, 1, 1)
    return a, b, a1, b1, a2, b2, a3, b3


def scatter_rows(pieces, tail):
    moved = [ring(pieces[step], 1, step) for step in (1, 2, 3)]
    tails = [ring(tail, 1, step) for step in (1, 2, 3)]
    shard = jax.ShapeDtypeStruct((SHARD + TAIL, tail.shape[1]), BF16)
    pieces = small_call(split_kernel, [shard] * 4, tail, *tails, pieces[0], *moved)
    return [pieces[0]] + [ring(pieces[step], 0, step) for step in (1, 2, 3)]


def add_kernel(mine_ref, other_ref, arrived_ref, out_ref):
    out_ref[...] = total(mine_ref[0], other_ref[0], arrived_ref[...]).astype(BF16)


def add(index, mine, other, arrived):
    shard = pl.BlockSpec((1, *arrived.shape), lambda step: (index, 0, 0))
    return pl.pallas_call(
        add_kernel, grid=(1,), out_shape=jax.ShapeDtypeStruct(arrived.shape, BF16), in_specs=[shard, shard, VMEM],
        out_specs=VMEM, compiler_params=pltpu.CompilerParams(vmem_limit_bytes=16 * 2**20),
    )(mine, other, arrived)


def scatter_cols(mine, other, far, far_other):
    same, cross = along_z(far), along_z(far_other)
    other = swap(other)
    for steps in (3, 2, 1):
        same = along_z(add(2 * steps - 1, mine, other, same))
        cross = add(2 * steps, mine, other, cross)
        cross = along_z(cross) if steps > 1 else along_z_across(cross, True)
    return add(0, mine, other, same), cross


def gather_cols(value, tail, message):
    tie = lax.optimization_barrier
    pieces = [value, swap(value)]
    same, cross = value, value
    for mask in (1, 2, 4, 8):
        same, cross = along_z(same), along_z_across(cross, False) if mask == 1 else along_z(cross)
        tail = total(tail, swap(message if mask == 1 else tail, mask)).astype(BF16)
        if mask != 8:
            cross, tail = tie((cross, tail))
        pieces += [same, cross]
    return pieces + [swap(piece) for piece in pieces[2:8]], tail


def body(features, weight, out_bias, upstream, adj_tiles, tile_rows, tile_cols, tile_count):
    tiles, rows, cols = adj_tiles[0, 0], tile_rows[0, 0], tile_cols[0, 0]
    meta = jnp.stack([tile_count[0, 0], lax.axis_index("row"), lax.axis_index("col")])
    channels = features.shape[1]

    part, shard = [jax.ShapeDtypeStruct(shape, BF16) for shape in ((7, SHARD, channels), (SHARD, channels))]
    terms = tile_sums(
        forward_kernel, [part, part, shard, shard], (16, SHARD, channels), 9, meta, rows, cols, tiles,
        gather_rows(features),
    )
    terms = scatter_cols(*terms)
    out_features, grad_pre, tail, message = middle(meta, *terms, weight, out_bias[None, :], upstream)

    pieces, tail = gather_cols(grad_pre, tail, message)
    part = jax.ShapeDtypeStruct((4 * SHARD, channels), BF16)
    pieces = tile_sums(
        backward_kernel, [part] * 4, (8, 2, SHARD, channels), 17, meta, rows, cols, tiles, pieces
    )
    terms = scatter_rows(pieces, tail)
    [tail] = small_call(last_tail_kernel, [jax.ShapeDtypeStruct((TAIL, channels), F32)], *terms)
    swapped = swap(tail)
    [grad_features] = small_call(last_kernel, [jax.ShapeDtypeStruct(features.shape, BF16)], *terms, weight)
    lower = (lax.axis_index("col") & 1) == 0
    first, second = jnp.where(lower, tail, swapped), jnp.where(lower, swapped[:HALF], tail[:HALF])
    return (out_features, grad_features, jnp.concatenate([first[:HALF], second]), first[HALF])


def solution(mesh):
    return jax.shard_map(
        body,
        mesh=mesh,
        in_specs=(
            P(("col", "row"), None),
            P(),
            P(),
            P(("row", "col"), None),
            P("row", "col", None, None, None),
            P("row", "col", None),
            P("row", "col", None),
            P("row", "col"),
        ),
        out_specs=(P(("row", "col"), None), P(("col", "row"), None), P(), P()),
        check_vma=False,
    )
```

```python
import jax
import jax.numpy as jnp
from jax import lax
from jax.experimental import pallas as pl
from jax.experimental.pallas import tpu as pltpu
from jax.sharding import PartitionSpec as P

TILE = 128
UNROLL = 8
SHARD = 512
LOCAL = SHARD // TILE
HALF = 128
TAIL = HALF + 16
BF16, F32 = jnp.bfloat16, jnp.float32

SMEM = pl.BlockSpec(memory_space=pltpu.SMEM)
VMEM = pl.BlockSpec(memory_space=pltpu.VMEM)
ANY = pl.BlockSpec(memory_space=pl.ANY)


def ring(value, second, step):
    pairs = []
    for row in range(16):
        for col in range(16):
            x, y = row // 4, row % 4
            if col % 2 == second:
                x = (x + step) % 4
            else:
                y = (y + step) % 4
            pairs.append((row * 16 + col, (x * 4 + y) * 16 + col))
    return lax.ppermute(value, ("row", "col"), pairs)


def along_z(value):
    return lax.ppermute(value, "col", [(i, (i + (-2 if i % 2 else 2)) % 16) for i in range(16)])


def along_z_across(value, own):
    pairs = []
    for i in range(16):
        core = i % 2 if own else 1 - i % 2
        pairs.append((i, ((i + (-2 if core else 2)) % 16) ^ 1))
    return lax.ppermute(value, "col", pairs)


def swap(value, mask=1):
    return lax.ppermute(value, "col", [(i, i ^ mask) for i in range(16)])


def total(*values):
    result = values[0].astype(F32)
    for value in values[1:]:
        result = result + value.astype(F32)
    return result


def row_place(block, meta_ref, sign):
    row, core = meta_ref[1], meta_ref[2] & 1
    owner, within = block >> 2, block & 3
    x, y = (sign * ((owner >> 2) - (row >> 2))) & 3, (sign * (owner - row)) & 3
    return jnp.where(core == 0, y * 4 + x, x * 4 + y), within


def col_steps(block, meta_ref, sign):
    col = meta_ref[2]
    owner, within = block >> 2, block & 3
    way = sign * (1 - 2 * (col & 1))
    return (way * ((owner >> 1) - (col >> 1))) & 7, (owner ^ col) & 1, within


def sum_tiles(dims, meta_ref, source_ref, target_ref, tiles_ref, load, acc_ref, place):
    blocks = acc_ref.shape[0] - 1
    count = meta_ref[0]

    def add_group(group, carry):
        products, targets = [], []
        for member in range(UNROLL):
            slot = group * UNROLL + member
            products.append(
                lax.dot_general(tiles_ref[slot], load(source_ref[slot]), (dims, ((), ())), preferred_element_type=F32)
            )
            targets.append(jnp.where(slot < count, place(target_ref[slot]), blocks))
        for product, target in zip(products, targets):
            acc_ref[target] += product
        return carry

    lax.fori_loop(0, (count + UNROLL - 1) // UNROLL, add_group, 0)


def fill(pairs, sems, acc_ref):
    copies = [pltpu.make_async_copy(source, there, sems.at[index]) for index, (source, there) in enumerate(pairs)]
    for copy in copies:
        copy.start()

    def clear(block, carry):
        acc_ref[block] = jnp.zeros(acc_ref.shape[1:], F32)
        return carry

    lax.fori_loop(0, acc_ref.shape[0], clear, 0)
    for copy in copies:
        copy.wait()


def forward_kernel(meta_ref, rows_ref, cols_ref, tiles_any, *refs):
    pieces, (mine_ref, other_ref, far_ref, far_other_ref, tiles_ref, feats_ref, acc_ref, sems) = refs[:8], refs[8:]
    pairs = [(ref, feats_ref.at[pl.ds(index * 2, 2)]) for index, ref in enumerate(pieces)]
    fill(pairs + [(tiles_any, tiles_ref)], sems, acc_ref)

    def load(block):
        owner, within = row_place(block, meta_ref, -1)
        return feats_ref[owner, pl.ds(pl.multiple_of(within * TILE, TILE), TILE), :]

    def place(block):
        steps, other, within = col_steps(block, meta_ref, 1)
        flip = jnp.where((steps > 4) | ((steps == 0) & (other == 1)), 1, 0)
        near, side = jnp.where(flip == 1, (8 - steps) & 7, steps), other ^ flip
        near = flip * 7 + jnp.maximum(2 * near - 1, 0) + side
        return jnp.where(steps == 4, 14 + other, near) * LOCAL + within

    sum_tiles(((1,), (0,)), meta_ref, cols_ref, rows_ref, tiles_ref, load, acc_ref, place)

    def finish(step, carry):
        at = pl.ds(pl.multiple_of((step & 3) * TILE, TILE), TILE)
        mine_ref[step >> 2, at, :] = acc_ref[step].astype(BF16)
        other_ref[step >> 2, at, :] = acc_ref[7 * LOCAL + step].astype(BF16)
        return carry

    lax.fori_loop(0, 7 * LOCAL, finish, 0)
    for within in range(LOCAL):
        at = pl.ds(within * TILE, TILE)
        far_ref[at, :] = acc_ref[14 * LOCAL + within].astype(BF16)
        far_other_ref[at, :] = acc_ref[15 * LOCAL + within].astype(BF16)


def backward_kernel(meta_ref, rows_ref, cols_ref, tiles_any, *refs):
    pieces, near, outs, (tiles_ref, feats_ref, acc_ref, sems) = refs[:10], refs[10:16], refs[16:20], refs[20:]
    pairs = [(ref, feats_ref.at[index // 2, index % 2]) for index, ref in enumerate(pieces)]
    pairs += [(ref, feats_ref.at[7 - index // 2, 1 - index % 2]) for index, ref in enumerate(near)]
    fill(pairs + [(tiles_any, tiles_ref)], sems, acc_ref)

    def load(block):
        steps, other, within = col_steps(block, meta_ref, -1)
        return feats_ref[steps, other, pl.ds(pl.multiple_of(within * TILE, TILE), TILE), :]

    def place(block):
        owner, within = row_place(block, meta_ref, 1)
        return owner * LOCAL + within

    sum_tiles(((0,), (0,)), meta_ref, rows_ref, cols_ref, tiles_ref, load, acc_ref, place)
    for second in (2, 1, 3, 0):
        out, first_block = outs[second], second * 4 * LOCAL

        def finish(index, carry):
            out[pl.ds(pl.multiple_of(index * TILE, TILE), TILE), :] = acc_ref[first_block + index].astype(BF16)
            return carry

        lax.fori_loop(0, 4 * LOCAL, finish, 0)


def tile_sums(kernel, outs, scratch, copies, meta, rows, cols, tiles, pieces):
    channels = scratch[-1]
    blocks = 16 * LOCAL
    return pl.pallas_call(
        kernel,
        out_shape=outs,
        in_specs=[SMEM] * 3 + [ANY] * (1 + len(pieces)),
        out_specs=[VMEM] * len(outs),
        scratch_shapes=[
            pltpu.VMEM(tiles.shape, BF16),
            pltpu.VMEM(scratch, BF16),
            pltpu.VMEM((blocks + 1, TILE, channels), F32),
            pltpu.SemaphoreType.DMA((copies,)),
        ],
        compiler_params=pltpu.CompilerParams(vmem_limit_bytes=28 * 2**20),
        cost_estimate=pl.CostEstimate(
            flops=2 * tiles.shape[0] * TILE * TILE * channels, bytes_accessed=12 * 2**20, transcendentals=0
        ),
    )(meta, rows, cols, tiles, *pieces)


def small_call(kernel, outs, *args, **more):
    return pl.pallas_call(
        kernel, out_shape=outs, in_specs=[VMEM] * len(args), out_specs=[VMEM] * len(outs),
        compiler_params=pltpu.CompilerParams(vmem_limit_bytes=16 * 2**20), **more,
    )(*args)


def middle_kernel(meta_ref, same_ref, cross_ref, weight_ref, bias_ref, upstream_ref,
                  out_ref, grad_ref, tail_ref, message_ref):
    gathered = total(same_ref[...], cross_ref[...]).astype(BF16)
    preact = jnp.dot(gathered, weight_ref[...], preferred_element_type=F32) + bias_ref[...]
    squashed = jax.nn.sigmoid(preact)
    out_ref[...] = (preact * squashed).astype(BF16)
    slope = squashed * (1.0 + preact * (1.0 - squashed))
    grad = (upstream_ref[...].astype(F32) * slope).astype(BF16)
    grad_ref[...] = grad
    weight_part = lax.dot_general(gathered, grad, (((0,), (0,)), ((), ())), preferred_element_type=F32)
    bias_part = jnp.sum(grad.astype(F32), axis=0, keepdims=True)
    first = lax.broadcasted_iota(jnp.int32, (TAIL - HALF, bias_part.shape[1]), 0) == 0
    bias_part = jnp.where(first, bias_part, 0.0)
    lower = (meta_ref[2] & 1) == 0
    tail_ref[pl.ds(0, HALF), :] = jnp.where(lower, weight_part[:HALF], weight_part[HALF:])
    tail_ref[pl.ds(HALF, TAIL - HALF), :] = bias_part
    message_ref[pl.ds(0, HALF), :] = jnp.where(lower, weight_part[HALF:], weight_part[:HALF]).astype(BF16)
    message_ref[pl.ds(HALF, TAIL - HALF), :] = bias_part.astype(BF16)


def middle(meta, same, cross, weight, bias, upstream):
    channels = weight.shape[0]

    return pl.pallas_call(
        middle_kernel,
        out_shape=[
            jax.ShapeDtypeStruct(upstream.shape, BF16),
            jax.ShapeDtypeStruct(upstream.shape, BF16),
            jax.ShapeDtypeStruct((TAIL, channels), F32),
            jax.ShapeDtypeStruct((TAIL, channels), BF16),
        ],
        in_specs=[SMEM] + [VMEM] * 5,
        out_specs=[VMEM] * 4,
        compiler_params=pltpu.CompilerParams(vmem_limit_bytes=16 * 2**20),
    )(meta, same, cross, weight, bias, upstream)


def four(own, plus, far, minus):
    return total(own, far) + total(plus, minus)


def split_kernel(tail_ref, own_ref, plus_ref, far_ref, minus_ref, *outs):
    for first, out_ref in enumerate(outs):
        at = pl.ds(first * SHARD, SHARD)
        out_ref[pl.ds(0, SHARD), :] = total(*[ref[at, :] for ref in (own_ref, plus_ref, far_ref, minus_ref)]).astype(BF16)
        out_ref[pl.ds(SHARD, TAIL), :] = tail_ref[...]


def last_tail_kernel(own_ref, plus_ref, far_ref, minus_ref, out_ref):
    out_ref[...] = four(*[ref[pl.ds(SHARD, TAIL), :] for ref in (own_ref, plus_ref, far_ref, minus_ref)])


def last_kernel(own_ref, plus_ref, far_ref, minus_ref, weight_ref, out_ref):
    hidden = total(*[ref[pl.ds(0, SHARD), :] for ref in (own_ref, plus_ref, far_ref, minus_ref)]).astype(BF16)
    out_ref[...] = lax.dot_general(
        hidden, weight_ref[...], (((1,), (1,)), ((), ())), preferred_element_type=F32
    ).astype(BF16)


def gather_rows(value):
    one, three, two = ring(value, 0, 1), ring(value, 0, 3), ring(value, 0, 2)
    a = jnp.stack([value, one])
    two, three = lax.optimization_barrier((two, three, a))[:2]
    b = jnp.stack([two, three])
    b3, a1 = ring(b, 1, 3), ring(a, 1, 1)
    b1, a3 = ring(b, 1, 1), ring(a, 1, 3)
    b2, a2 = ring(b3, 1, 3), ring(a1, 1, 1)
    return a, b, a1, b1, a2, b2, a3, b3


def scatter_rows(pieces, tail):
    moved = [ring(pieces[step], 1, step) for step in (1, 2, 3)]
    for mask in (2, 4, 8):
        tail = total(tail, swap(tail, mask)).astype(BF16)
    shard = jax.ShapeDtypeStruct((SHARD + TAIL, tail.shape[1]), BF16)
    pieces = small_call(split_kernel, [shard] * 4, tail, pieces[0], *moved)
    return [pieces[0]] + [ring(pieces[step], 0, step) for step in (1, 2, 3)]


def add_kernel(mine_ref, other_ref, arrived_ref, out_ref):
    out_ref[...] = total(mine_ref[0], other_ref[0], arrived_ref[...]).astype(BF16)


def add(index, mine, other, arrived):
    shard = pl.BlockSpec((1, *arrived.shape), lambda step: (index, 0, 0))
    return pl.pallas_call(
        add_kernel, grid=(1,), out_shape=jax.ShapeDtypeStruct(arrived.shape, BF16), in_specs=[shard, shard, VMEM],
        out_specs=VMEM, compiler_params=pltpu.CompilerParams(vmem_limit_bytes=16 * 2**20),
    )(mine, other, arrived)


def scatter_cols(mine, other, far, far_other):
    same, cross = along_z(far), along_z(far_other)
    other = swap(other)
    for steps in (3, 2, 1):
        same = along_z(add(2 * steps - 1, mine, other, same))
        cross = add(2 * steps, mine, other, cross)
        cross = along_z(cross) if steps > 1 else along_z_across(cross, True)
    return add(0, mine, other, same), cross


def gather_cols(value, tail, message):
    tie = lax.optimization_barrier
    pieces = [value, swap(value)]
    same, cross = value, value
    for hop in range(4):
        same, cross = along_z(same), along_z(cross) if hop else along_z_across(cross, False)
        if hop == 0:
            tail = total(tail, swap(message)).astype(BF16)
        if hop == 2:
            tail = four(tail, *[ring(tail, 1, step) for step in (1, 2, 3)]).astype(BF16)
        if hop in (0, 2):
            cross, tail = tie((cross, tail))
        pieces += [same, cross]
    return pieces + [swap(piece) for piece in pieces[2:8]], tail


def body(features, weight, out_bias, upstream, adj_tiles, tile_rows, tile_cols, tile_count):
    tiles, rows, cols = adj_tiles[0, 0], tile_rows[0, 0], tile_cols[0, 0]
    meta = jnp.stack([tile_count[0, 0], lax.axis_index("row"), lax.axis_index("col")])
    channels = features.shape[1]

    part, shard = [jax.ShapeDtypeStruct(shape, BF16) for shape in ((7, SHARD, channels), (SHARD, channels))]
    terms = tile_sums(
        forward_kernel, [part, part, shard, shard], (16, SHARD, channels), 9, meta, rows, cols, tiles,
        gather_rows(features),
    )
    terms = scatter_cols(*terms)
    out_features, grad_pre, tail, message = middle(meta, *terms, weight, out_bias[None, :], upstream)

    pieces, tail = gather_cols(grad_pre, tail, message)
    part = jax.ShapeDtypeStruct((4 * SHARD, channels), BF16)
    pieces = tile_sums(
        backward_kernel, [part] * 4, (8, 2, SHARD, channels), 17, meta, rows, cols, tiles, pieces
    )
    terms = scatter_rows(pieces, tail)
    [tail] = small_call(last_tail_kernel, [jax.ShapeDtypeStruct((TAIL, channels), F32)], *terms)
    swapped = swap(tail)
    [grad_features] = small_call(last_kernel, [jax.ShapeDtypeStruct(features.shape, BF16)], *terms, weight)
    lower = (lax.axis_index("col") & 1) == 0
    first, second = jnp.where(lower, tail, swapped), jnp.where(lower, swapped[:HALF], tail[:HALF])
    return (out_features, grad_features, jnp.concatenate([first[:HALF], second]), first[HALF])


def solution(mesh):
    return jax.shard_map(
        body,
        mesh=mesh,
        in_specs=(
            P(("col", "row"), None),
            P(),
            P(),
            P(("row", "col"), None),
            P("row", "col", None, None, None),
            P("row", "col", None),
            P("row", "col", None),
            P("row", "col"),
        ),
        out_specs=(P(("row", "col"), None), P(("col", "row"), None), P(), P()),
        check_vma=False,
    )
```

```python
import jax
import jax.numpy as jnp
from jax import lax
from jax.experimental import pallas as pl
from jax.experimental.pallas import tpu as pltpu
from jax.sharding import PartitionSpec as P

TILE = 128
UNROLL = 8
SHARD = 512
LOCAL = SHARD // TILE
HALF = 128
TAIL = HALF + 16
BF16, F32 = jnp.bfloat16, jnp.float32

SMEM = pl.BlockSpec(memory_space=pltpu.SMEM)
VMEM = pl.BlockSpec(memory_space=pltpu.VMEM)
ANY = pl.BlockSpec(memory_space=pl.ANY)


def ring(value, second, step):
    pairs = []
    for row in range(16):
        for col in range(16):
            x, y = row // 4, row % 4
            if col % 2 == second:
                x = (x + step) % 4
            else:
                y = (y + step) % 4
            pairs.append((row * 16 + col, (x * 4 + y) * 16 + col))
    return lax.ppermute(value, ("row", "col"), pairs)


def along_z(value):
    return lax.ppermute(value, "col", [(i, (i + (-2 if i % 2 else 2)) % 16) for i in range(16)])


def along_z_across(value, own):
    pairs = []
    for i in range(16):
        core = i % 2 if own else 1 - i % 2
        pairs.append((i, ((i + (-2 if core else 2)) % 16) ^ 1))
    return lax.ppermute(value, "col", pairs)


def swap(value, mask=1):
    return lax.ppermute(value, "col", [(i, i ^ mask) for i in range(16)])


def total(*values):
    result = values[0].astype(F32)
    for value in values[1:]:
        result = result + value.astype(F32)
    return result


def row_place(block, meta_ref, sign):
    row, core = meta_ref[1], meta_ref[2] & 1
    owner, within = block >> 2, block & 3
    x, y = (sign * ((owner >> 2) - (row >> 2))) & 3, (sign * (owner - row)) & 3
    return jnp.where(core == 0, y * 4 + x, x * 4 + y), within


def col_steps(block, meta_ref, sign):
    col = meta_ref[2]
    owner, within = block >> 2, block & 3
    way = sign * (1 - 2 * (col & 1))
    return (way * ((owner >> 1) - (col >> 1))) & 7, (owner ^ col) & 1, within


def sum_tiles(dims, meta_ref, source_ref, target_ref, tiles_ref, load, acc_ref, place):
    blocks = acc_ref.shape[0] - 1
    count = meta_ref[0]

    def add_group(group, carry):
        products, targets = [], []
        for member in range(UNROLL):
            slot = group * UNROLL + member
            products.append(
                lax.dot_general(tiles_ref[slot], load(source_ref[slot]), (dims, ((), ())), preferred_element_type=F32)
            )
            targets.append(jnp.where(slot < count, place(target_ref[slot]), blocks))
        for product, target in zip(products, targets):
            acc_ref[target] += product
        return carry

    lax.fori_loop(0, (count + UNROLL - 1) // UNROLL, add_group, 0)


def fill(pairs, sems, acc_ref):
    copies = [pltpu.make_async_copy(source, there, sems.at[index]) for index, (source, there) in enumerate(pairs)]
    for copy in copies:
        copy.start()

    def clear(block, carry):
        acc_ref[block] = jnp.zeros(acc_ref.shape[1:], F32)
        return carry

    lax.fori_loop(0, acc_ref.shape[0], clear, 0)
    for copy in copies:
        copy.wait()


def forward_kernel(meta_ref, rows_ref, cols_ref, tiles_any, *refs):
    pieces, (mine_ref, other_ref, far_ref, far_other_ref, tiles_ref, feats_ref, acc_ref, sems) = refs[:8], refs[8:]
    pairs = [(ref, feats_ref.at[pl.ds(index * 2, 2)]) for index, ref in enumerate(pieces)]
    fill(pairs + [(tiles_any, tiles_ref)], sems, acc_ref)

    def load(block):
        owner, within = row_place(block, meta_ref, -1)
        return feats_ref[owner, pl.ds(pl.multiple_of(within * TILE, TILE), TILE), :]

    def place(block):
        steps, other, within = col_steps(block, meta_ref, 1)
        flip = jnp.where((steps > 4) | ((steps == 0) & (other == 1)), 1, 0)
        near, side = jnp.where(flip == 1, (8 - steps) & 7, steps), other ^ flip
        near = flip * 7 + jnp.maximum(2 * near - 1, 0) + side
        return jnp.where(steps == 4, 14 + other, near) * LOCAL + within

    sum_tiles(((1,), (0,)), meta_ref, cols_ref, rows_ref, tiles_ref, load, acc_ref, place)

    def finish(step, carry):
        at = pl.ds(pl.multiple_of((step & 3) * TILE, TILE), TILE)
        mine_ref[step >> 2, at, :] = acc_ref[step].astype(BF16)
        other_ref[step >> 2, at, :] = acc_ref[7 * LOCAL + step].astype(BF16)
        return carry

    lax.fori_loop(0, 7 * LOCAL, finish, 0)
    for within in range(LOCAL):
        at = pl.ds(within * TILE, TILE)
        far_ref[at, :] = acc_ref[14 * LOCAL + within].astype(BF16)
        far_other_ref[at, :] = acc_ref[15 * LOCAL + within].astype(BF16)


def backward_kernel(meta_ref, rows_ref, cols_ref, tiles_any, *refs):
    pieces, near, outs, (tiles_ref, feats_ref, acc_ref, sems) = refs[:10], refs[10:16], refs[16:20], refs[20:]
    pairs = [(ref, feats_ref.at[index // 2, index % 2]) for index, ref in enumerate(pieces)]
    pairs += [(ref, feats_ref.at[7 - index // 2, 1 - index % 2]) for index, ref in enumerate(near)]
    fill(pairs + [(tiles_any, tiles_ref)], sems, acc_ref)

    def load(block):
        steps, other, within = col_steps(block, meta_ref, -1)
        return feats_ref[steps, other, pl.ds(pl.multiple_of(within * TILE, TILE), TILE), :]

    def place(block):
        owner, within = row_place(block, meta_ref, 1)
        return owner * LOCAL + within

    sum_tiles(((0,), (0,)), meta_ref, rows_ref, cols_ref, tiles_ref, load, acc_ref, place)
    for second in (2, 1, 3, 0):
        out, first_block = outs[second], second * 4 * LOCAL

        def finish(index, carry):
            out[pl.ds(pl.multiple_of(index * TILE, TILE), TILE), :] = acc_ref[first_block + index].astype(BF16)
            return carry

        lax.fori_loop(0, 4 * LOCAL, finish, 0)


def tile_sums(kernel, outs, scratch, copies, meta, rows, cols, tiles, pieces):
    channels = scratch[-1]
    blocks = 16 * LOCAL
    return pl.pallas_call(
        kernel,
        out_shape=outs,
        in_specs=[SMEM] * 3 + [ANY] * (1 + len(pieces)),
        out_specs=[VMEM] * len(outs),
        scratch_shapes=[
            pltpu.VMEM(tiles.shape, BF16),
            pltpu.VMEM(scratch, BF16),
            pltpu.VMEM((blocks + 1, TILE, channels), F32),
            pltpu.SemaphoreType.DMA((copies,)),
        ],
        compiler_params=pltpu.CompilerParams(vmem_limit_bytes=28 * 2**20),
        cost_estimate=pl.CostEstimate(
            flops=2 * tiles.shape[0] * TILE * TILE * channels, bytes_accessed=12 * 2**20, transcendentals=0
        ),
    )(meta, rows, cols, tiles, *pieces)


def small_call(kernel, outs, *args, **more):
    return pl.pallas_call(
        kernel, out_shape=outs, in_specs=[VMEM] * len(args), out_specs=[VMEM] * len(outs),
        compiler_params=pltpu.CompilerParams(vmem_limit_bytes=16 * 2**20), **more,
    )(*args)


def middle_kernel(meta_ref, same_ref, cross_ref, weight_ref, bias_ref, upstream_ref,
                  out_ref, grad_ref, tail_ref, message_ref):
    gathered = total(same_ref[...], cross_ref[...]).astype(BF16)
    preact = jnp.dot(gathered, weight_ref[...], preferred_element_type=F32) + bias_ref[...]
    squashed = jax.nn.sigmoid(preact)
    out_ref[...] = (preact * squashed).astype(BF16)
    slope = squashed * (1.0 + preact * (1.0 - squashed))
    grad = (upstream_ref[...].astype(F32) * slope).astype(BF16)
    grad_ref[...] = grad
    weight_part = lax.dot_general(gathered, grad, (((0,), (0,)), ((), ())), preferred_element_type=F32)
    bias_part = jnp.sum(grad.astype(F32), axis=0, keepdims=True)
    first = lax.broadcasted_iota(jnp.int32, (TAIL - HALF, bias_part.shape[1]), 0) == 0
    bias_part = jnp.where(first, bias_part, 0.0)
    lower = (meta_ref[2] & 1) == 0
    tail_ref[pl.ds(0, HALF), :] = jnp.where(lower, weight_part[:HALF], weight_part[HALF:])
    tail_ref[pl.ds(HALF, TAIL - HALF), :] = bias_part
    message_ref[pl.ds(0, HALF), :] = jnp.where(lower, weight_part[HALF:], weight_part[:HALF]).astype(BF16)
    message_ref[pl.ds(HALF, TAIL - HALF), :] = bias_part.astype(BF16)


def middle(meta, same, cross, weight, bias, upstream):
    channels = weight.shape[0]

    return pl.pallas_call(
        middle_kernel,
        out_shape=[
            jax.ShapeDtypeStruct(upstream.shape, BF16),
            jax.ShapeDtypeStruct(upstream.shape, BF16),
            jax.ShapeDtypeStruct((TAIL, channels), F32),
            jax.ShapeDtypeStruct((TAIL, channels), BF16),
        ],
        in_specs=[SMEM] + [VMEM] * 5,
        out_specs=[VMEM] * 4,
        compiler_params=pltpu.CompilerParams(vmem_limit_bytes=16 * 2**20),
    )(meta, same, cross, weight, bias, upstream)


def four(own, plus, far, minus):
    return total(own, far) + total(plus, minus)


def split_kernel(tail_ref, own_ref, plus_ref, far_ref, minus_ref, *outs):
    for first, out_ref in enumerate(outs):
        at = pl.ds(first * SHARD, SHARD)
        out_ref[pl.ds(0, SHARD), :] = total(*[ref[at, :] for ref in (own_ref, plus_ref, far_ref, minus_ref)]).astype(BF16)
        out_ref[pl.ds(SHARD, TAIL), :] = tail_ref[...]


def last_tail_kernel(own_ref, plus_ref, far_ref, minus_ref, out_ref):
    out_ref[...] = four(*[ref[pl.ds(SHARD, TAIL), :] for ref in (own_ref, plus_ref, far_ref, minus_ref)])


def last_kernel(own_ref, plus_ref, far_ref, minus_ref, weight_ref, out_ref):
    hidden = total(*[ref[pl.ds(0, SHARD), :] for ref in (own_ref, plus_ref, far_ref, minus_ref)]).astype(BF16)
    out_ref[...] = lax.dot_general(
        hidden, weight_ref[...], (((1,), (1,)), ((), ())), preferred_element_type=F32
    ).astype(BF16)


def gather_rows(value):
    one, three, two = ring(value, 0, 1), ring(value, 0, 3), ring(value, 0, 2)
    a = jnp.stack([value, one])
    two, three = lax.optimization_barrier((two, three, a))[:2]
    b = jnp.stack([two, three])
    b3, a1 = ring(b, 1, 3), ring(a, 1, 1)
    b1, a3 = ring(b, 1, 1), ring(a, 1, 3)
    b2, a2 = ring(b3, 1, 3), ring(a1, 1, 1)
    return a, b, a1, b1, a2, b2, a3, b3


def scatter_rows(pieces, tail):
    moved = [ring(pieces[step], 1, step) for step in (1, 2, 3)]
    for mask in (2, 4, 8):
        tail = total(tail, swap(tail, mask)).astype(BF16)
    shard = jax.ShapeDtypeStruct((SHARD + TAIL, tail.shape[1]), BF16)
    pieces = small_call(split_kernel, [shard] * 4, tail, pieces[0], *moved)
    return [pieces[0]] + [ring(pieces[step], 0, step) for step in (1, 2, 3)]


def add_kernel(mine_ref, other_ref, arrived_ref, out_ref):
    out_ref[...] = total(mine_ref[0], other_ref[0], arrived_ref[...]).astype(BF16)


def add(index, mine, other, arrived):
    shard = pl.BlockSpec((1, *arrived.shape), lambda step: (index, 0, 0))
    return pl.pallas_call(
        add_kernel, grid=(1,), out_shape=jax.ShapeDtypeStruct(arrived.shape, BF16), in_specs=[shard, shard, VMEM],
        out_specs=VMEM, compiler_params=pltpu.CompilerParams(vmem_limit_bytes=16 * 2**20),
    )(mine, other, arrived)


def scatter_cols(mine, other, far, far_other):
    same, cross = along_z(far), along_z(far_other)
    other = swap(other)
    for steps in (3, 2, 1):
        same = along_z(add(2 * steps - 1, mine, other, same))
        cross = add(2 * steps, mine, other, cross)
        cross = along_z(cross) if steps > 1 else along_z_across(cross, True)
    return add(0, mine, other, same), cross


def gather_cols(value, tail, message):
    tie = lax.optimization_barrier
    pieces = [value, swap(value)]
    same, cross = value, value
    for hop in range(4):
        same, cross = along_z(same), along_z(cross) if hop else along_z_across(cross, False)
        if hop == 1:
            tail = total(tail, swap(message)).astype(BF16)
        if hop == 3:
            tail = four(tail, *[ring(tail, 1, step) for step in (1, 2, 3)]).astype(BF16)
        if hop in (1, 3):
            cross, tail = tie((cross, tail))
        pieces += [same, cross]
    return pieces + [swap(piece) for piece in pieces[2:8]], tail


def body(features, weight, out_bias, upstream, adj_tiles, tile_rows, tile_cols, tile_count):
    tiles, rows, cols = adj_tiles[0, 0], tile_rows[0, 0], tile_cols[0, 0]
    meta = jnp.stack([tile_count[0, 0], lax.axis_index("row"), lax.axis_index("col")])
    channels = features.shape[1]

    part, shard = [jax.ShapeDtypeStruct(shape, BF16) for shape in ((7, SHARD, channels), (SHARD, channels))]
    terms = tile_sums(
        forward_kernel, [part, part, shard, shard], (16, SHARD, channels), 9, meta, rows, cols, tiles,
        gather_rows(features),
    )
    terms = scatter_cols(*terms)
    out_features, grad_pre, tail, message = middle(meta, *terms, weight, out_bias[None, :], upstream)

    pieces, tail = gather_cols(grad_pre, tail, message)
    part = jax.ShapeDtypeStruct((4 * SHARD, channels), BF16)
    pieces = tile_sums(
        backward_kernel, [part] * 4, (8, 2, SHARD, channels), 17, meta, rows, cols, tiles, pieces
    )
    terms = scatter_rows(pieces, tail)
    [tail] = small_call(last_tail_kernel, [jax.ShapeDtypeStruct((TAIL, channels), F32)], *terms)
    swapped = swap(tail)
    [grad_features] = small_call(last_kernel, [jax.ShapeDtypeStruct(features.shape, BF16)], *terms, weight)
    lower = (lax.axis_index("col") & 1) == 0
    mine = (jnp.arange(2) == 0) == lower
    grad_weight = jnp.where(mine[:, None, None], tail[None, :HALF], swapped[None, :HALF]).reshape(weight.shape)
    return (out_features, grad_features, grad_weight, jnp.where(lower, tail[HALF], swapped[HALF]))


def solution(mesh):
    return jax.shard_map(
        body,
        mesh=mesh,
        in_specs=(
            P(("col", "row"), None),
            P(),
            P(),
            P(("row", "col"), None),
            P("row", "col", None, None, None),
            P("row", "col", None),
            P("row", "col", None),
            P("row", "col"),
        ),
        out_specs=(P(("row", "col"), None), P(("col", "row"), None), P(), P()),
        check_vma=False,
    )
```

```python
import jax
import jax.numpy as jnp
from jax import lax
from jax.experimental import pallas as pl
from jax.experimental.pallas import tpu as pltpu
from jax.sharding import PartitionSpec as P

TILE = 128
UNROLL = 16
SHARD = 512
LOCAL = SHARD // TILE
HALF = 128
TAIL = HALF + 16
BF16, F32 = jnp.bfloat16, jnp.float32

SMEM = pl.BlockSpec(memory_space=pltpu.SMEM)
VMEM = pl.BlockSpec(memory_space=pltpu.VMEM)
ANY = pl.BlockSpec(memory_space=pl.ANY)


def ring(value, second, step):
    pairs = []
    for row in range(16):
        for col in range(16):
            x, y = row // 4, row % 4
            if col % 2 == second:
                x = (x + step) % 4
            else:
                y = (y + step) % 4
            pairs.append((row * 16 + col, (x * 4 + y) * 16 + col))
    return lax.ppermute(value, ("row", "col"), pairs)


def along_z(value):
    return lax.ppermute(value, "col", [(i, (i + (-2 if i % 2 else 2)) % 16) for i in range(16)])


def along_z_across(value, own):
    pairs = []
    for i in range(16):
        core = i % 2 if own else 1 - i % 2
        pairs.append((i, ((i + (-2 if core else 2)) % 16) ^ 1))
    return lax.ppermute(value, "col", pairs)


def swap(value, mask=1):
    return lax.ppermute(value, "col", [(i, i ^ mask) for i in range(16)])


def total(*values):
    result = values[0].astype(F32)
    for value in values[1:]:
        result = result + value.astype(F32)
    return result


def row_place(block, meta_ref, sign):
    row, core = meta_ref[1], meta_ref[2] & 1
    owner, within = block >> 2, block & 3
    x, y = (sign * ((owner >> 2) - (row >> 2))) & 3, (sign * (owner - row)) & 3
    return jnp.where(core == 0, y * 4 + x, x * 4 + y), within


def col_steps(block, meta_ref, sign):
    col = meta_ref[2]
    owner, within = block >> 2, block & 3
    way = sign * (1 - 2 * (col & 1))
    return (way * ((owner >> 1) - (col >> 1))) & 7, (owner ^ col) & 1, within


def sum_tiles(dims, meta_ref, source_ref, target_ref, tiles_ref, load, acc_ref, place):
    blocks = acc_ref.shape[0] - 1
    count = meta_ref[0]

    def add_group(group, carry):
        products, targets = [], []
        for member in range(UNROLL):
            slot = group * UNROLL + member
            products.append(
                lax.dot_general(tiles_ref[slot], load(source_ref[slot]), (dims, ((), ())), preferred_element_type=F32)
            )
            targets.append(jnp.where(slot < count, place(target_ref[slot]), blocks))
        for product, target in zip(products, targets):
            acc_ref[target] += product
        return carry

    lax.fori_loop(0, (count + UNROLL - 1) // UNROLL, add_group, 0)


def fill(pairs, sems, acc_ref):
    copies = [pltpu.make_async_copy(source, there, sems.at[index]) for index, (source, there) in enumerate(pairs)]
    for copy in copies:
        copy.start()

    def clear(block, carry):
        acc_ref[block] = jnp.zeros(acc_ref.shape[1:], F32)
        return carry

    lax.fori_loop(0, acc_ref.shape[0], clear, 0)
    for copy in copies:
        copy.wait()


def forward_kernel(meta_ref, rows_ref, cols_ref, tiles_any, *refs):
    pieces, (mine_ref, other_ref, far_ref, far_other_ref, tiles_ref, feats_ref, acc_ref, sems) = refs[:8], refs[8:]
    pairs = [(ref, feats_ref.at[pl.ds(index * 2, 2)]) for index, ref in enumerate(pieces)]
    fill(pairs + [(tiles_any, tiles_ref)], sems, acc_ref)

    def load(block):
        owner, within = row_place(block, meta_ref, -1)
        return feats_ref[owner, pl.ds(pl.multiple_of(within * TILE, TILE), TILE), :]

    def place(block):
        steps, other, within = col_steps(block, meta_ref, 1)
        flip = jnp.where((steps > 4) | ((steps == 0) & (other == 1)), 1, 0)
        near, side = jnp.where(flip == 1, (8 - steps) & 7, steps), other ^ flip
        near = flip * 7 + jnp.maximum(2 * near - 1, 0) + side
        return jnp.where(steps == 4, 14 + other, near) * LOCAL + within

    sum_tiles(((1,), (0,)), meta_ref, cols_ref, rows_ref, tiles_ref, load, acc_ref, place)

    def finish(step, carry):
        at = pl.ds(pl.multiple_of((step & 3) * TILE, TILE), TILE)
        mine_ref[step >> 2, at, :] = acc_ref[step].astype(BF16)
        other_ref[step >> 2, at, :] = acc_ref[7 * LOCAL + step].astype(BF16)
        return carry

    lax.fori_loop(0, 7 * LOCAL, finish, 0)
    for within in range(LOCAL):
        at = pl.ds(within * TILE, TILE)
        far_ref[at, :] = acc_ref[14 * LOCAL + within].astype(BF16)
        far_other_ref[at, :] = acc_ref[15 * LOCAL + within].astype(BF16)


def backward_kernel(meta_ref, rows_ref, cols_ref, tiles_any, *refs):
    pieces, near, outs, (tiles_ref, feats_ref, acc_ref, sems) = refs[:10], refs[10:16], refs[16:20], refs[20:]
    pairs = [(ref, feats_ref.at[index // 2, index % 2]) for index, ref in enumerate(pieces)]
    pairs += [(ref, feats_ref.at[7 - index // 2, 1 - index % 2]) for index, ref in enumerate(near)]
    fill(pairs + [(tiles_any, tiles_ref)], sems, acc_ref)

    def load(block):
        steps, other, within = col_steps(block, meta_ref, -1)
        return feats_ref[steps, other, pl.ds(pl.multiple_of(within * TILE, TILE), TILE), :]

    def place(block):
        owner, within = row_place(block, meta_ref, 1)
        return owner * LOCAL + within

    sum_tiles(((0,), (0,)), meta_ref, rows_ref, cols_ref, tiles_ref, load, acc_ref, place)
    for second in (2, 1, 3, 0):
        out, first_block = outs[second], second * 4 * LOCAL

        def finish(index, carry):
            out[pl.ds(pl.multiple_of(index * TILE, TILE), TILE), :] = acc_ref[first_block + index].astype(BF16)
            return carry

        lax.fori_loop(0, 4 * LOCAL, finish, 0)


def tile_sums(kernel, outs, scratch, copies, meta, rows, cols, tiles, pieces):
    channels = scratch[-1]
    blocks = 16 * LOCAL
    return pl.pallas_call(
        kernel,
        out_shape=outs,
        in_specs=[SMEM] * 3 + [ANY] * (1 + len(pieces)),
        out_specs=[VMEM] * len(outs),
        scratch_shapes=[
            pltpu.VMEM(tiles.shape, BF16),
            pltpu.VMEM(scratch, BF16),
            pltpu.VMEM((blocks + 1, TILE, channels), F32),
            pltpu.SemaphoreType.DMA((copies,)),
        ],
        compiler_params=pltpu.CompilerParams(vmem_limit_bytes=28 * 2**20),
        cost_estimate=pl.CostEstimate(
            flops=2 * tiles.shape[0] * TILE * TILE * channels, bytes_accessed=12 * 2**20, transcendentals=0
        ),
    )(meta, rows, cols, tiles, *pieces)


def small_call(kernel, outs, *args, **more):
    return pl.pallas_call(
        kernel, out_shape=outs, in_specs=[VMEM] * len(args), out_specs=[VMEM] * len(outs),
        compiler_params=pltpu.CompilerParams(vmem_limit_bytes=16 * 2**20), **more,
    )(*args)


def middle_kernel(meta_ref, same_ref, cross_ref, weight_ref, bias_ref, upstream_ref,
                  out_ref, grad_ref, tail_ref, message_ref):
    gathered = total(same_ref[...], cross_ref[...]).astype(BF16)
    preact = jnp.dot(gathered, weight_ref[...], preferred_element_type=F32) + bias_ref[...]
    squashed = jax.nn.sigmoid(preact)
    out_ref[...] = (preact * squashed).astype(BF16)
    slope = squashed * (1.0 + preact * (1.0 - squashed))
    grad = (upstream_ref[...].astype(F32) * slope).astype(BF16)
    grad_ref[...] = grad
    weight_part = lax.dot_general(gathered, grad, (((0,), (0,)), ((), ())), preferred_element_type=F32)
    bias_part = jnp.sum(grad.astype(F32), axis=0, keepdims=True)
    first = lax.broadcasted_iota(jnp.int32, (TAIL - HALF, bias_part.shape[1]), 0) == 0
    bias_part = jnp.where(first, bias_part, 0.0)
    lower = (meta_ref[2] & 1) == 0
    tail_ref[pl.ds(0, HALF), :] = jnp.where(lower, weight_part[:HALF], weight_part[HALF:])
    tail_ref[pl.ds(HALF, TAIL - HALF), :] = bias_part
    message_ref[pl.ds(0, HALF), :] = jnp.where(lower, weight_part[HALF:], weight_part[:HALF]).astype(BF16)
    message_ref[pl.ds(HALF, TAIL - HALF), :] = bias_part.astype(BF16)


def middle(meta, same, cross, weight, bias, upstream):
    channels = weight.shape[0]

    return pl.pallas_call(
        middle_kernel,
        out_shape=[
            jax.ShapeDtypeStruct(upstream.shape, BF16),
            jax.ShapeDtypeStruct(upstream.shape, BF16),
            jax.ShapeDtypeStruct((TAIL, channels), F32),
            jax.ShapeDtypeStruct((TAIL, channels), BF16),
        ],
        in_specs=[SMEM] + [VMEM] * 5,
        out_specs=[VMEM] * 4,
        compiler_params=pltpu.CompilerParams(vmem_limit_bytes=16 * 2**20),
    )(meta, same, cross, weight, bias, upstream)


def four(own, plus, far, minus):
    return total(own, far) + total(plus, minus)


def split_kernel(tail_ref, own_ref, plus_ref, far_ref, minus_ref, *outs):
    for first, out_ref in enumerate(outs):
        at = pl.ds(first * SHARD, SHARD)
        out_ref[pl.ds(0, SHARD), :] = total(*[ref[at, :] for ref in (own_ref, plus_ref, far_ref, minus_ref)]).astype(BF16)
        out_ref[pl.ds(SHARD, TAIL), :] = tail_ref[...]


def last_tail_kernel(own_ref, plus_ref, far_ref, minus_ref, out_ref):
    out_ref[...] = four(*[ref[pl.ds(SHARD, TAIL), :] for ref in (own_ref, plus_ref, far_ref, minus_ref)])


def last_kernel(own_ref, plus_ref, far_ref, minus_ref, weight_ref, out_ref):
    hidden = total(*[ref[pl.ds(0, SHARD), :] for ref in (own_ref, plus_ref, far_ref, minus_ref)]).astype(BF16)
    out_ref[...] = lax.dot_general(
        hidden, weight_ref[...], (((1,), (1,)), ((), ())), preferred_element_type=F32
    ).astype(BF16)


def meta_kernel(count_ref, place_ref, tiles_ref, meta_ref):
    meta_ref[0] = count_ref[0]
    meta_ref[1] = place_ref[0]
    meta_ref[2] = place_ref[1]


def gather_rows(value, meta):
    one, three, two = ring(value, 0, 1), ring(value, 0, 3), ring(value, 0, 2)
    one = lax.optimization_barrier((one, meta))[0]
    a = jnp.stack([value, one])
    two, three = lax.optimization_barrier((two, three, a))[:2]
    b = jnp.stack([two, three])
    b3, a1 = ring(b, 1, 3), ring(a, 1, 1)
    b1, a3 = ring(b, 1, 1), ring(a, 1, 3)
    b2, a2 = ring(b3, 1, 3), ring(a1, 1, 1)
    return a, b, a1, b1, a2, b2, a3, b3


def scatter_rows(pieces, tail):
    moved = [ring(pieces[step], 1, step) for step in (1, 2, 3)]
    for mask in (2, 4, 8):
        tail = total(tail, swap(tail, mask)).astype(BF16)
    shard = jax.ShapeDtypeStruct((SHARD + TAIL, tail.shape[1]), BF16)
    pieces = small_call(split_kernel, [shard] * 4, tail, pieces[0], *moved)
    return [pieces[0]] + [ring(pieces[step], 0, step) for step in (1, 2, 3)]


def add_kernel(mine_ref, other_ref, arrived_ref, out_ref):
    out_ref[...] = total(mine_ref[0], other_ref[0], arrived_ref[...]).astype(BF16)


def add(index, mine, other, arrived):
    shard = pl.BlockSpec((1, *arrived.shape), lambda step: (index, 0, 0))
    return pl.pallas_call(
        add_kernel, grid=(1,), out_shape=jax.ShapeDtypeStruct(arrived.shape, BF16), in_specs=[shard, shard, VMEM],
        out_specs=VMEM, compiler_params=pltpu.CompilerParams(vmem_limit_bytes=16 * 2**20),
    )(mine, other, arrived)


def scatter_cols(mine, other, far, far_other):
    same, cross = along_z(far), along_z(far_other)
    other = swap(other)
    for steps in (3, 2, 1):
        same = along_z(add(2 * steps - 1, mine, other, same))
        cross = add(2 * steps, mine, other, cross)
        cross = along_z(cross) if steps > 1 else along_z_across(cross, True)
    return add(0, mine, other, same), cross


def gather_cols(value, tail, message):
    tie = lax.optimization_barrier
    pieces = [value, swap(value)]
    same, cross = value, value
    for hop in range(4):
        same, cross = along_z(same), along_z(cross) if hop else along_z_across(cross, False)
        if hop == 1:
            tail = total(tail, swap(message)).astype(BF16)
        if hop == 3:
            tail = four(tail, *[ring(tail, 1, step) for step in (1, 2, 3)]).astype(BF16)
        if hop in (1, 3):
            cross, tail = tie((cross, tail))
        pieces += [same, cross]
    return pieces + [swap(piece) for piece in pieces[2:8]], tail


def body(features, weight, out_bias, upstream, adj_tiles, tile_rows, tile_cols, tile_count):
    tiles, rows, cols = adj_tiles[0, 0], tile_rows[0, 0], tile_cols[0, 0]
    place = jnp.stack([lax.axis_index("row"), lax.axis_index("col")])
    meta = pl.pallas_call(
        meta_kernel, out_shape=jax.ShapeDtypeStruct((3,), jnp.int32), in_specs=[SMEM, SMEM, ANY], out_specs=SMEM,
        compiler_params=pltpu.CompilerParams(vmem_limit_bytes=8 * 2**20),
    )(tile_count[0], place, tiles)
    channels = features.shape[1]

    part, shard = [jax.ShapeDtypeStruct(shape, BF16) for shape in ((7, SHARD, channels), (SHARD, channels))]
    terms = tile_sums(
        forward_kernel, [part, part, shard, shard], (16, SHARD, channels), 9, meta, rows, cols, tiles,
        gather_rows(features, meta),
    )
    terms = scatter_cols(*terms)
    out_features, grad_pre, tail, message = middle(meta, *terms, weight, out_bias[None, :], upstream)

    pieces, tail = gather_cols(grad_pre, tail, message)
    part = jax.ShapeDtypeStruct((4 * SHARD, channels), BF16)
    pieces = tile_sums(
        backward_kernel, [part] * 4, (8, 2, SHARD, channels), 17, meta, rows, cols, tiles, pieces
    )
    terms = scatter_rows(pieces, tail)
    [tail] = small_call(last_tail_kernel, [jax.ShapeDtypeStruct((TAIL, channels), F32)], *terms)
    swapped = swap(tail)
    [grad_features] = small_call(last_kernel, [jax.ShapeDtypeStruct(features.shape, BF16)], *terms, weight)
    lower = (lax.axis_index("col") & 1) == 0
    mine = (jnp.arange(2) == 0) == lower
    grad_weight = jnp.where(mine[:, None, None], tail[None, :HALF], swapped[None, :HALF]).reshape(weight.shape)
    return (out_features, grad_features, grad_weight, jnp.where(lower, tail[HALF], swapped[HALF]))


def solution(mesh):
    return jax.shard_map(
        body,
        mesh=mesh,
        in_specs=(
            P(("col", "row"), None),
            P(),
            P(),
            P(("row", "col"), None),
            P("row", "col", None, None, None),
            P("row", "col", None),
            P("row", "col", None),
            P("row", "col"),
        ),
        out_specs=(P(("row", "col"), None), P(("col", "row"), None), P(), P()),
        check_vma=False,
    )
```

```python
import jax
import jax.numpy as jnp
from jax import lax
from jax.experimental import pallas as pl
from jax.experimental.pallas import tpu as pltpu
from jax.sharding import PartitionSpec as P

TILE = 128
UNROLL = 24
SHARD = 512
LOCAL = SHARD // TILE
HALF = 128
TAIL = HALF + 16
BF16, F32 = jnp.bfloat16, jnp.float32

SMEM = pl.BlockSpec(memory_space=pltpu.SMEM)
VMEM = pl.BlockSpec(memory_space=pltpu.VMEM)
ANY = pl.BlockSpec(memory_space=pl.ANY)


def ring(value, second, step):
    pairs = []
    for row in range(16):
        for col in range(16):
            x, y = row // 4, row % 4
            if col % 2 == second:
                x = (x + step) % 4
            else:
                y = (y + step) % 4
            pairs.append((row * 16 + col, (x * 4 + y) * 16 + col))
    return lax.ppermute(value, ("row", "col"), pairs)


def along_z(value):
    return lax.ppermute(value, "col", [(i, (i + (-2 if i % 2 else 2)) % 16) for i in range(16)])


def along_z_across(value, own):
    pairs = []
    for i in range(16):
        core = i % 2 if own else 1 - i % 2
        pairs.append((i, ((i + (-2 if core else 2)) % 16) ^ 1))
    return lax.ppermute(value, "col", pairs)


def swap(value, mask=1):
    return lax.ppermute(value, "col", [(i, i ^ mask) for i in range(16)])


def total(*values):
    result = values[0].astype(F32)
    for value in values[1:]:
        result = result + value.astype(F32)
    return result


def row_place(block, meta_ref, sign):
    row, core = meta_ref[1], meta_ref[2] & 1
    owner, within = block >> 2, block & 3
    x, y = (sign * ((owner >> 2) - (row >> 2))) & 3, (sign * (owner - row)) & 3
    return jnp.where(core == 0, y * 4 + x, x * 4 + y), within


def col_steps(block, meta_ref, sign):
    col = meta_ref[2]
    owner, within = block >> 2, block & 3
    way = sign * (1 - 2 * (col & 1))
    return (way * ((owner >> 1) - (col >> 1))) & 7, (owner ^ col) & 1, within


def sum_tiles(dims, meta_ref, source_ref, target_ref, tiles_ref, load, acc_ref, place):
    blocks = acc_ref.shape[0] - 1
    count = meta_ref[0]

    def add_group(group, carry):
        products, targets = [], []
        for member in range(UNROLL):
            slot = group * UNROLL + member
            products.append(
                lax.dot_general(tiles_ref[slot], load(source_ref[slot]), (dims, ((), ())), preferred_element_type=F32)
            )
            targets.append(jnp.where(slot < count, place(target_ref[slot]), blocks))
        for product, target in zip(products, targets):
            acc_ref[target] += product
        return carry

    lax.fori_loop(0, (count + UNROLL - 1) // UNROLL, add_group, 0)


def fill(pairs, sems, acc_ref):
    copies = [pltpu.make_async_copy(source, there, sems.at[index]) for index, (source, there) in enumerate(pairs)]
    for copy in copies:
        copy.start()

    def clear(block, carry):
        acc_ref[block] = jnp.zeros(acc_ref.shape[1:], F32)
        return carry

    lax.fori_loop(0, acc_ref.shape[0], clear, 0)
    for copy in copies:
        copy.wait()


def forward_kernel(meta_ref, rows_ref, cols_ref, tiles_any, *refs):
    pieces, (mine_ref, other_ref, far_ref, far_other_ref, tiles_ref, feats_ref, acc_ref, sems) = refs[:8], refs[8:]
    pairs = [(ref, feats_ref.at[pl.ds(index * 2, 2)]) for index, ref in enumerate(pieces)]
    fill(pairs + [(tiles_any, tiles_ref)], sems, acc_ref)

    def load(block):
        owner, within = row_place(block, meta_ref, -1)
        return feats_ref[owner, pl.ds(pl.multiple_of(within * TILE, TILE), TILE), :]

    def place(block):
        steps, other, within = col_steps(block, meta_ref, 1)
        flip = jnp.where((steps > 4) | ((steps == 0) & (other == 1)), 1, 0)
        near, side = jnp.where(flip == 1, (8 - steps) & 7, steps), other ^ flip
        near = flip * 7 + jnp.maximum(2 * near - 1, 0) + side
        return jnp.where(steps == 4, 14 + other, near) * LOCAL + within

    sum_tiles(((1,), (0,)), meta_ref, cols_ref, rows_ref, tiles_ref, load, acc_ref, place)

    def finish(step, carry):
        at = pl.ds(pl.multiple_of((step & 3) * TILE, TILE), TILE)
        mine_ref[step >> 2, at, :] = acc_ref[step].astype(BF16)
        other_ref[step >> 2, at, :] = acc_ref[7 * LOCAL + step].astype(BF16)
        return carry

    lax.fori_loop(0, 7 * LOCAL, finish, 0)
    for within in range(LOCAL):
        at = pl.ds(within * TILE, TILE)
        far_ref[at, :] = acc_ref[14 * LOCAL + within].astype(BF16)
        far_other_ref[at, :] = acc_ref[15 * LOCAL + within].astype(BF16)


def backward_kernel(meta_ref, rows_ref, cols_ref, tiles_any, *refs):
    pieces, near, outs, (tiles_ref, feats_ref, acc_ref, sems) = refs[:10], refs[10:16], refs[16:20], refs[20:]
    pairs = [(ref, feats_ref.at[index // 2, index % 2]) for index, ref in enumerate(pieces)]
    pairs += [(ref, feats_ref.at[7 - index // 2, 1 - index % 2]) for index, ref in enumerate(near)]
    fill(pairs + [(tiles_any, tiles_ref)], sems, acc_ref)

    def load(block):
        steps, other, within = col_steps(block, meta_ref, -1)
        return feats_ref[steps, other, pl.ds(pl.multiple_of(within * TILE, TILE), TILE), :]

    def place(block):
        owner, within = row_place(block, meta_ref, 1)
        return owner * LOCAL + within

    sum_tiles(((0,), (0,)), meta_ref, rows_ref, cols_ref, tiles_ref, load, acc_ref, place)
    for second in (2, 1, 3, 0):
        out, first_block = outs[second], second * 4 * LOCAL

        def finish(index, carry):
            out[pl.ds(pl.multiple_of(index * TILE, TILE), TILE), :] = acc_ref[first_block + index].astype(BF16)
            return carry

        lax.fori_loop(0, 4 * LOCAL, finish, 0)


def tile_sums(kernel, outs, scratch, copies, meta, rows, cols, tiles, pieces):
    channels = scratch[-1]
    blocks = 16 * LOCAL
    return pl.pallas_call(
        kernel,
        out_shape=outs,
        in_specs=[SMEM] * 3 + [ANY] * (1 + len(pieces)),
        out_specs=[VMEM] * len(outs),
        scratch_shapes=[
            pltpu.VMEM(tiles.shape, BF16),
            pltpu.VMEM(scratch, BF16),
            pltpu.VMEM((blocks + 1, TILE, channels), F32),
            pltpu.SemaphoreType.DMA((copies,)),
        ],
        compiler_params=pltpu.CompilerParams(vmem_limit_bytes=28 * 2**20),
        cost_estimate=pl.CostEstimate(
            flops=2 * tiles.shape[0] * TILE * TILE * channels, bytes_accessed=12 * 2**20, transcendentals=0
        ),
    )(meta, rows, cols, tiles, *pieces)


def small_call(kernel, outs, *args, **more):
    return pl.pallas_call(
        kernel, out_shape=outs, in_specs=[VMEM] * len(args), out_specs=[VMEM] * len(outs),
        compiler_params=pltpu.CompilerParams(vmem_limit_bytes=16 * 2**20), **more,
    )(*args)


def middle_kernel(same_ref, cross_ref, weight_ref, bias_ref, upstream_ref, out_ref, grad_ref, gathered_ref):
    gathered = total(same_ref[...], cross_ref[...]).astype(BF16)
    gathered_ref[...] = gathered
    preact = jnp.dot(gathered, weight_ref[...], preferred_element_type=F32) + bias_ref[...]
    squashed = jax.nn.sigmoid(preact)
    out_ref[...] = (preact * squashed).astype(BF16)
    slope = squashed * (1.0 + preact * (1.0 - squashed))
    grad_ref[...] = (upstream_ref[...].astype(F32) * slope).astype(BF16)


def parts_kernel(meta_ref, gathered_ref, grad_ref, tail_ref, message_ref):
    grad = grad_ref[...]
    weight_part = lax.dot_general(gathered_ref[...], grad, (((0,), (0,)), ((), ())), preferred_element_type=F32)
    bias_part = jnp.sum(grad.astype(F32), axis=0, keepdims=True)
    first = lax.broadcasted_iota(jnp.int32, (TAIL - HALF, bias_part.shape[1]), 0) == 0
    bias_part = jnp.where(first, bias_part, 0.0)
    lower = (meta_ref[2] & 1) == 0
    tail_ref[pl.ds(0, HALF), :] = jnp.where(lower, weight_part[:HALF], weight_part[HALF:])
    tail_ref[pl.ds(HALF, TAIL - HALF), :] = bias_part
    message_ref[pl.ds(0, HALF), :] = jnp.where(lower, weight_part[HALF:], weight_part[:HALF]).astype(BF16)
    message_ref[pl.ds(HALF, TAIL - HALF), :] = bias_part.astype(BF16)


def parts(meta, gathered, grad):
    channels = grad.shape[1]
    return pl.pallas_call(
        parts_kernel,
        out_shape=[jax.ShapeDtypeStruct((TAIL, channels), F32), jax.ShapeDtypeStruct((TAIL, channels), BF16)],
        in_specs=[SMEM, VMEM, VMEM], out_specs=[VMEM] * 2,
        compiler_params=pltpu.CompilerParams(vmem_limit_bytes=16 * 2**20),
    )(meta, gathered, grad)


def four(own, plus, far, minus):
    return total(own, far) + total(plus, minus)


def split_kernel(tail_ref, own_ref, plus_ref, far_ref, minus_ref, *outs):
    for first, out_ref in enumerate(outs):
        at = pl.ds(first * SHARD, SHARD)
        out_ref[pl.ds(0, SHARD), :] = total(*[ref[at, :] for ref in (own_ref, plus_ref, far_ref, minus_ref)]).astype(BF16)
        out_ref[pl.ds(SHARD, TAIL), :] = tail_ref[...]


def last_tail_kernel(own_ref, plus_ref, far_ref, minus_ref, out_ref):
    out_ref[...] = four(*[ref[pl.ds(SHARD, TAIL), :] for ref in (own_ref, plus_ref, far_ref, minus_ref)])


def last_kernel(own_ref, plus_ref, far_ref, minus_ref, weight_ref, out_ref):
    hidden = total(*[ref[pl.ds(0, SHARD), :] for ref in (own_ref, plus_ref, far_ref, minus_ref)]).astype(BF16)
    out_ref[...] = lax.dot_general(
        hidden, weight_ref[...], (((1,), (1,)), ((), ())), preferred_element_type=F32
    ).astype(BF16)


def meta_kernel(count_ref, place_ref, tiles_ref, meta_ref):
    meta_ref[0] = count_ref[0]
    meta_ref[1] = place_ref[0]
    meta_ref[2] = place_ref[1]


def gather_rows(value, meta):
    one, three, two = ring(value, 0, 1), ring(value, 0, 3), ring(value, 0, 2)
    one = lax.optimization_barrier((one, meta))[0]
    a = jnp.stack([value, one])
    two, three = lax.optimization_barrier((two, three, a))[:2]
    b = jnp.stack([two, three])
    b3, a1 = ring(b, 1, 3), ring(a, 1, 1)
    b1, a3 = ring(b, 1, 1), ring(a, 1, 3)
    b2, a2 = ring(b3, 1, 3), ring(a1, 1, 1)
    return a, b, a1, b1, a2, b2, a3, b3


def scatter_rows(pieces, tail):
    moved = [ring(pieces[step], 1, step) for step in (1, 2, 3)]
    for mask in (2, 4, 8):
        tail = total(tail, swap(tail, mask)).astype(BF16)
    shard = jax.ShapeDtypeStruct((SHARD + TAIL, tail.shape[1]), BF16)
    pieces = small_call(split_kernel, [shard] * 4, tail, pieces[0], *moved)
    return [pieces[0]] + [ring(pieces[step], 0, step) for step in (1, 2, 3)]


def add_kernel(mine_ref, other_ref, arrived_ref, out_ref):
    out_ref[...] = total(mine_ref[0], other_ref[0], arrived_ref[...]).astype(BF16)


def add(index, mine, other, arrived):
    shard = pl.BlockSpec((1, *arrived.shape), lambda step: (index, 0, 0))
    return pl.pallas_call(
        add_kernel, grid=(1,), out_shape=jax.ShapeDtypeStruct(arrived.shape, BF16), in_specs=[shard, shard, VMEM],
        out_specs=VMEM, compiler_params=pltpu.CompilerParams(vmem_limit_bytes=16 * 2**20),
    )(mine, other, arrived)


def scatter_cols(mine, other, far, far_other):
    same, cross = along_z(far), along_z(far_other)
    other = swap(other)
    for steps in (3, 2, 1):
        same = along_z(add(2 * steps - 1, mine, other, same))
        cross = add(2 * steps, mine, other, cross)
        cross = along_z(cross) if steps > 1 else along_z_across(cross, True)
    return add(0, mine, other, same), cross


def gather_cols(value, tail, message):
    tie = lax.optimization_barrier
    pieces = [value, swap(value)]
    same, cross = value, value
    for hop in range(4):
        same, cross = along_z(same), along_z(cross) if hop else along_z_across(cross, False)
        if hop == 1:
            tail = total(tail, swap(message)).astype(BF16)
        if hop == 3:
            tail = four(tail, *[ring(tail, 1, step) for step in (1, 2, 3)]).astype(BF16)
        if hop in (1, 3):
            cross, tail = tie((cross, tail))
        pieces += [same, cross]
    return pieces + [swap(piece) for piece in pieces[2:8]], tail


def body(features, weight, out_bias, upstream, adj_tiles, tile_rows, tile_cols, tile_count):
    tiles, rows, cols = adj_tiles[0, 0], tile_rows[0, 0], tile_cols[0, 0]
    place = jnp.stack([lax.axis_index("row"), lax.axis_index("col")])
    meta = pl.pallas_call(
        meta_kernel, out_shape=jax.ShapeDtypeStruct((3,), jnp.int32), in_specs=[SMEM, SMEM, ANY], out_specs=SMEM,
        compiler_params=pltpu.CompilerParams(vmem_limit_bytes=8 * 2**20),
    )(tile_count[0], place, tiles)
    channels = features.shape[1]

    part, shard = [jax.ShapeDtypeStruct(shape, BF16) for shape in ((7, SHARD, channels), (SHARD, channels))]
    terms = tile_sums(
        forward_kernel, [part, part, shard, shard], (16, SHARD, channels), 9, meta, rows, cols, tiles,
        gather_rows(features, meta),
    )
    terms = scatter_cols(*terms)
    out_features, grad_pre, gathered = small_call(
        middle_kernel, [jax.ShapeDtypeStruct(upstream.shape, BF16)] * 3, *terms, weight, out_bias[None, :], upstream
    )
    tail, message = parts(meta, gathered, grad_pre)

    pieces, tail = gather_cols(grad_pre, tail, message)
    part = jax.ShapeDtypeStruct((4 * SHARD, channels), BF16)
    pieces = tile_sums(
        backward_kernel, [part] * 4, (8, 2, SHARD, channels), 17, meta, rows, cols, tiles, pieces
    )
    terms = scatter_rows(pieces, tail)
    [tail] = small_call(last_tail_kernel, [jax.ShapeDtypeStruct((TAIL, channels), F32)], *terms)
    swapped = swap(tail)
    [grad_features] = small_call(last_kernel, [jax.ShapeDtypeStruct(features.shape, BF16)], *terms, weight)
    lower = (lax.axis_index("col") & 1) == 0
    mine = (jnp.arange(2) == 0) == lower
    grad_weight = jnp.where(mine[:, None, None], tail[None, :HALF], swapped[None, :HALF]).reshape(weight.shape)
    return (out_features, grad_features, grad_weight, jnp.where(lower, tail[HALF], swapped[HALF]))


def solution(mesh):
    return jax.shard_map(
        body,
        mesh=mesh,
        in_specs=(
            P(("col", "row"), None),
            P(),
            P(),
            P(("row", "col"), None),
            P("row", "col", None, None, None),
            P("row", "col", None),
            P("row", "col", None),
            P("row", "col"),
        ),
        out_specs=(P(("row", "col"), None), P(("col", "row"), None), P(), P()),
        check_vma=False,
    )
```
